32 devices in a mesh: groups: 2 (over x), ctx: 16 (over z, y, core).
Axes of the slice: x: 2, y: 2, z: 4, core: 2. Of those that a mesh axis runs over, the one named last changes fastest.
Arguments:
- queries: bfloat16 [32768, 1024], P(('groups', 'ctx')), parts along dimension 0, may hold values from -8 to 8
- key_rows: bfloat16 [32768, 1024], P(('groups', 'ctx')), parts along dimension 0, may hold values from -8 to 8
- value_rows: bfloat16 [32768, 1024], P(('groups', 'ctx')), parts along dimension 0, may hold values from -6 to 6
- grad_out: bfloat16 [32768, 1024], P(('groups', 'ctx')), parts along dimension 0, may hold values from -6 to 6
- tile_keys: int32 [256, 8], P(('groups', 'ctx')), parts along dimension 0, may hold values from 0 to 127, as said below
Outputs:
- grad_queries: bfloat16 [32768, 1024], P(('groups', 'ctx')), parts along dimension 0
- grad_keys: bfloat16 [32768, 1024], P(('groups', 'ctx')), parts along dimension 0
- grad_values: bfloat16 [32768, 1024], P(('groups', 'ctx')), parts along dimension 0
The draws below stay inside these ranges and needn't reach their ends.
There are 2 independent parts, one for each index of `groups`. The reference program is written for one: setup_inputs(seed, part) draws one part's arguments, and reference() takes and returns one part's arrays. A program takes and returns all parts, laid end to end along the dimension named above; each array names one. Nothing has to cross between parts.
Inputs may be any that keep to these rules, and one draw needn't show every extreme that they name: `tile_keys`: block j lies on index j // 8 of ctx. A row names 8 blocks on 8 different indices of ctx, none on the index that holds the row's own query block; all query blocks on one index that name some block of another index name the same block of it.
All inputs are finite; a program needn't handle non-finite values.
Results may differ from the reference program's by a relative error of at most 0.012.
Values may be sent and summed in bfloat16 or wider, within the bound.
No kernel may reach another device: no remote copies, remote signals or barrier semaphores. Data moves between devices by JAX's collectives and lax.ppermute only.
A program may use at most 256 MiB of HBM per device.

```python
import jax
import jax.numpy as jnp
from jax import lax

HEADS = 16
HD = 64
TILE = 128
KSEL = 8
TOK_DEV = 1024
D = 1024
SEQ = 16384
N_CTX = 16


def draw_pair(key):
    folded = jax.random.fold_in(key, 5)
    key_query, key_keys = jax.random.split(folded, 2)
    row_total = TOK_DEV * N_CTX
    width_all = HEADS * HD
    query_draw = jnp.clip(jax.random.normal(key_query, (row_total, width_all), jnp.float32), -6.0, 6.0)
    key_draw = jnp.clip(jax.random.normal(key_keys, (row_total, width_all), jnp.float32), -6.0, 6.0)
    return (query_draw, key_draw)


def draw_queries(key, part):
    return draw_pair(key)[0].astype(jnp.bfloat16)


def draw_key_rows(key, part):
    return draw_pair(key)[1].astype(jnp.bfloat16)


def draw_tile_keys(key, part):
    folded = jax.random.fold_in(key, 11)
    key_hub, key_coin, key_local, key_score = jax.random.split(folded, 4)
    blocks_dev = TOK_DEV // TILE
    all_blocks = N_CTX * blocks_dev
    hub_local = jax.random.randint(key_hub, (N_CTX,), 0, blocks_dev)
    hub_local = hub_local.at[0].set(0).at[N_CTX - 1].set(blocks_dev - 1)
    use_hub = jax.random.randint(key_coin, (N_CTX, N_CTX), 0, 4) < 3
    use_hub = use_hub.at[0, N_CTX - 1].set(True).at[1, 0].set(True)
    random_local = jax.random.randint(key_local, (N_CTX, N_CTX), 0, blocks_dev)
    local_pick = jnp.where(use_hub, hub_local[None, :], random_local)
    peer_range = jnp.arange(N_CTX, dtype=jnp.int32)
    block_pick = peer_range[None, :] * blocks_dev + local_pick
    device_of = jnp.arange(all_blocks, dtype=jnp.int32) // blocks_dev
    raw_score = jax.random.randint(key_score, (all_blocks, N_CTX), 0, 1 << 20)
    score_table = raw_score * N_CTX + peer_range[None, :]
    score_table = jnp.where(peer_range[None, :] == device_of[:, None], -1, score_table)
    top_score = (1 << 20) * N_CTX + N_CTX
    score_table = score_table.at[0, N_CTX - 1].set(top_score).at[blocks_dev, 0].set(top_score)
    chosen_values, chosen_peers = lax.top_k(score_table, KSEL)
    tile_ids = jnp.take_along_axis(block_pick[device_of], chosen_peers.astype(jnp.int32), axis=1)
    return tile_ids.astype(jnp.int32)


def block_levels(stream_key, shape, cuts, low, top_value):
    def one(dim, parts):
        draws = jax.random.uniform(jax.random.fold_in(jax.random.fold_in(stream_key, 6), dim), (parts,), jnp.float32, low / len(cuts), top_value / len(cuts))
        return jnp.repeat(jnp.exp(draws), shape[dim] // parts).reshape((-1,) + (1,) * (len(shape) - dim - 1))

    level = one(*cuts[0])
    for cut in cuts[1:]:
        level = level * one(*cut)
    return level


def gaussian(stream_key, extent, scale, limit, cuts=(), kind=jnp.bfloat16):
    loudness = block_levels(stream_key, extent, cuts, -0.22, 0.18) if cuts else 1.0
    values = jax.random.normal(stream_key, extent, jnp.float32) * scale * loudness
    return jnp.minimum(jnp.maximum(values, -limit), limit).astype(kind)


def setup_inputs(seed: int = 0, part: int = 0) -> dict:
    arg_keys = jax.random.split(jax.random.key(seed), 6)
    part_splits = jax.random.split(jax.random.fold_in(arg_keys[5], part), 6)
    return {
        "queries": draw_queries(jax.random.fold_in(jax.random.fold_in(arg_keys[5], part), 71), part),
        "key_rows": draw_key_rows(jax.random.fold_in(jax.random.fold_in(arg_keys[5], part), 71), part),
        "value_rows": gaussian(part_splits[2], (SEQ, D), 1.0, 6.0, ((0, 16),)),
        "grad_out": gaussian(part_splits[3], (SEQ, D), 1.0, 6.0, ((0, 16),)),
        "tile_keys": draw_tile_keys(jax.random.fold_in(jax.random.fold_in(arg_keys[5], part), 71), part),
    }


def block_backward(query_rows, grad_rows, key_set, value_set):
    row_count = query_rows.shape[0]
    set_count = key_set.shape[0]
    factor = HD ** -0.5
    query_heads = query_rows.reshape(row_count, HEADS, HD).astype(jnp.float32)
    grad_heads = grad_rows.reshape(row_count, HEADS, HD).astype(jnp.float32)
    key_heads = key_set.reshape(set_count, HEADS, HD).astype(jnp.float32)
    value_heads = value_set.reshape(set_count, HEADS, HD).astype(jnp.float32)
    scores = jnp.einsum("qhd,khd->hqk", query_heads, key_heads) * factor
    row_max = jnp.max(scores, axis=2, keepdims=True)
    raised = jnp.exp(scores - row_max)
    weights = raised / jnp.sum(raised, axis=2, keepdims=True)
    weights_low = weights.astype(jnp.bfloat16).astype(jnp.float32)
    attended = jnp.einsum("hqk,khd->qhd", weights_low, value_heads)
    delta_row = jnp.sum(grad_heads * attended, axis=2)
    grad_weights = jnp.einsum("qhd,khd->hqk", grad_heads, value_heads)
    grad_scores = (weights * (grad_weights - delta_row.T[:, :, None])).astype(jnp.bfloat16).astype(jnp.float32)
    grad_query = jnp.einsum("hqk,khd->qhd", grad_scores, key_heads) * factor
    grad_key = jnp.einsum("hqk,qhd->khd", grad_scores, query_heads) * factor
    grad_value = jnp.einsum("hqk,qhd->khd", weights_low, grad_heads)
    return (grad_query.reshape(row_count, D), grad_key.reshape(set_count, D), grad_value.reshape(set_count, D))


def reference(queries, key_rows, value_rows, grad_out, tile_keys):
    blocks_dev = TOK_DEV // TILE
    all_blocks = N_CTX * blocks_dev
    key_blocks = key_rows.reshape(all_blocks, TILE, D)
    value_blocks = value_rows.reshape(all_blocks, TILE, D)
    query_groups = queries.reshape(N_CTX, blocks_dev, TILE, D)
    grad_groups = grad_out.reshape(N_CTX, blocks_dev, TILE, D)
    key_table = tile_keys.reshape(N_CTX, blocks_dev, KSEL)
    peer_range = jnp.arange(N_CTX, dtype=jnp.int32)

    def one_group(totals, entries):
        total_keys, total_values = totals
        group_index, query_part, grad_part, table_part = entries

        def one_block(summed, items):
            summed_keys, summed_values = summed
            offset, query_rows, grad_rows, chosen = items
            own_block = (group_index * blocks_dev + offset).astype(jnp.int32)
            picked = jnp.concatenate([own_block[None], chosen.astype(jnp.int32)])
            key_set = key_blocks[picked].reshape(-1, D)
            value_set = value_blocks[picked].reshape(-1, D)
            grad_query, grad_key, grad_value = block_backward(query_rows, grad_rows, key_set, value_set)
            grad_key = grad_key.reshape(1 + KSEL, TILE, D)
            grad_value = grad_value.reshape(1 + KSEL, TILE, D)
            owners = (chosen // blocks_dev).astype(jnp.int32)
            summed_keys = summed_keys.at[owners].add(grad_key[1:])
            summed_values = summed_values.at[owners].add(grad_value[1:])
            return (summed_keys, summed_values), (grad_query, grad_key[0], grad_value[0])

        empty = jnp.zeros((N_CTX, TILE, D), jnp.float32)
        offsets = jnp.arange(blocks_dev, dtype=jnp.int32)
        (summed_keys, summed_values), (grad_query, own_keys, own_values) = lax.scan(
            one_block, (empty, empty), (offsets, query_part, grad_part, table_part))
        matches = (table_part // blocks_dev)[:, :, None] == peer_range[None, None, :]
        wanted = jnp.max(jnp.where(matches, table_part[:, :, None], -1), axis=(0, 1))
        in_use = (wanted >= 0)[:, None, None]
        target = jnp.maximum(wanted, 0).astype(jnp.int32)
        rounded_keys = lax.optimization_barrier(summed_keys.astype(jnp.bfloat16)).astype(jnp.float32)
        rounded_values = lax.optimization_barrier(summed_values.astype(jnp.bfloat16)).astype(jnp.float32)
        total_keys = total_keys.at[target].add(jnp.where(in_use, rounded_keys, 0.0))
        total_values = total_values.at[target].add(jnp.where(in_use, rounded_values, 0.0))
        own_blocks = (group_index * blocks_dev + offsets).astype(jnp.int32)
        total_keys = total_keys.at[own_blocks].add(own_keys)
        total_values = total_values.at[own_blocks].add(own_values)
        return (total_keys, total_values), grad_query

    start = jnp.zeros((all_blocks, TILE, D), jnp.float32)
    (total_keys, total_values), grad_query = lax.scan(
        one_group, (start, start), (jnp.arange(N_CTX, dtype=jnp.int32), query_groups, grad_groups, key_table))
    return (grad_query.reshape(-1, D).astype(jnp.bfloat16),
            total_keys.reshape(-1, D).astype(jnp.bfloat16),
            total_values.reshape(-1, D).astype(jnp.bfloat16))
```

```python
import functools

import jax
import jax.numpy as jnp
from jax import lax
from jax.experimental import pallas as pl
from jax.experimental.pallas import tpu as pltpu
from jax.sharding import PartitionSpec as P

HD = 64
TILE = 128
PAIR = 2 * HD
LOG2E = 1.4426950408889634
CHUNKS = 2
VMEM_LIMIT = 48 * 1024 * 1024


def dot_nt(a, b):
    return lax.dot_general(a, b, (((1,), (1,)), ((), ())), preferred_element_type=jnp.float32)


def dot_nn(a, b):
    return lax.dot_general(a, b, (((1,), (0,)), ((), ())), preferred_element_type=jnp.float32)


def gather_kernel(peers, chunk_width, chunk, ids_ref, k_ref, v_ref, out_ref, sems):
    cols = pl.ds(chunk * chunk_width, chunk_width)

    def copies(p):
        rows = pl.ds(pl.multiple_of(ids_ref[p] * TILE, TILE), TILE)
        return (
            pltpu.make_async_copy(k_ref.at[rows, cols], out_ref.at[p, pl.ds(0, TILE)], sems.at[0, p]),
            pltpu.make_async_copy(v_ref.at[rows, cols], out_ref.at[p, pl.ds(TILE, TILE)], sems.at[1, p]),
        )

    for p in range(peers):
        for copy in copies(p):
            copy.start()
    for p in range(peers):
        for copy in copies(p):
            copy.wait()


def gather_blocks(ids, key_rows, value_rows, chunk, chunk_width):
    peers = ids.shape[0]
    return pl.pallas_call(
        functools.partial(gather_kernel, peers, chunk_width, chunk),
        grid_spec=pltpu.PrefetchScalarGridSpec(
            num_scalar_prefetch=1,
            grid=(),
            in_specs=[pl.BlockSpec(memory_space=pl.ANY)] * 2,
            out_specs=pl.BlockSpec(memory_space=pl.ANY),
            scratch_shapes=[pltpu.SemaphoreType.DMA((2, peers))],
        ),
        out_shape=jax.ShapeDtypeStruct((peers, 2 * TILE, chunk_width), jnp.bfloat16),
        name="gather_blocks",
    )(ids, key_rows, value_rows)


def attend_kernel(peers, blocks, picks, aliased, slots_ref, q_ref, g_ref, k_ref, v_ref, recv_ref, *rest):
    if aliased:
        rest = rest[1:]
    dq_ref, own_ref, out_ref, s_scr, w_scr, p_scr, kt_scr, acc_scr = rest
    lane = lax.broadcasted_iota(jnp.int32, (TILE, PAIR), 1)
    first = lane < HD

    def prepare(p, carry):
        kt_scr[p] = recv_ref[p, :TILE, :].T
        acc_scr[p] = jnp.zeros((2 * TILE, PAIR), jnp.float32)
        return carry

    lax.fori_loop(0, peers, prepare, 0)

    def split(x):
        zero = jnp.zeros_like(x)
        return jnp.concatenate([jnp.where(first, x, zero), jnp.where(first, zero, x)], axis=0)

    def one_block(b, carry):
        rows = pl.ds(pl.multiple_of(b * TILE, TILE), TILE)
        q2f = split(q_ref[rows, :].astype(jnp.float32) * (HD**-0.5))
        g2f = split(g_ref[rows, :].astype(jnp.float32))
        q2 = q2f.astype(jnp.bfloat16)
        g2 = g2f.astype(jnp.bfloat16)
        slots = [slots_ref[b * picks + j] for j in range(picks)]

        def fold(x, op):
            x = x.reshape(TILE // 8, 8, 2 * TILE)
            return op(x, axis=0)

        top = None
        for j in range(picks + 1):
            if j < picks:
                kb, vb = recv_ref[slots[j], :TILE, :], recv_ref[slots[j], TILE:, :]
            else:
                kb, vb = k_ref[rows, :], v_ref[rows, :]
            s = dot_nt(kb, q2)
            s_scr[j] = s
            w_scr[j] = dot_nt(vb, g2)
            part = fold(s, jnp.max)
            top = part if top is None else jnp.maximum(top, part)
        top = jnp.max(top, axis=0, keepdims=True)
        total = jnp.zeros((8, 2 * TILE), jnp.float32)
        inner = jnp.zeros((8, 2 * TILE), jnp.float32)
        for j in range(picks + 1):
            p = jnp.exp2((s_scr[j] - top) * LOG2E)
            s_scr[j] = p
            p_scr[j] = p.astype(jnp.bfloat16)
            total += fold(p, jnp.sum)
            inner += fold(p * w_scr[j], jnp.sum)
        recip = 1.0 / jnp.sum(total, axis=0, keepdims=True)
        delta = jnp.sum(inner, axis=0, keepdims=True) * recip
        column = jnp.broadcast_to(recip, (PAIR, 2 * TILE)).T
        rq = (q2f * column).astype(jnp.bfloat16)
        rg = (g2f * column).astype(jnp.bfloat16)
        dqt = jnp.zeros((PAIR, 2 * TILE), jnp.float32)
        for j in range(picks + 1):
            ds = (s_scr[j] * (w_scr[j] - delta)).astype(jnp.bfloat16)
            dk = dot_nn(ds, rq)
            dv = dot_nn(p_scr[j], rg)
            if j < picks:
                acc_scr[slots[j], :TILE, :] += dk
                acc_scr[slots[j], TILE:, :] += dv
                kt = kt_scr[slots[j]]
            else:
                own_ref[0, rows, :] = dk
                own_ref[1, rows, :] = dv
                kt = k_ref[rows, :].T
            dqt += dot_nn(kt, ds)
        dqt = dqt * (recip * (HD**-0.5))
        dqt = jnp.concatenate([dqt[:HD, :TILE], dqt[HD:, TILE:]], axis=0)
        dq_ref[rows, :] = dqt.T.astype(jnp.bfloat16)
        return carry

    lax.fori_loop(0, blocks, one_block, 0)

    def finish(p, carry):
        out_ref[p] = acc_scr[p].astype(jnp.bfloat16)
        return carry

    lax.fori_loop(0, peers, finish, 0)


def attend(slots, queries, grad_out, key_rows, value_rows, received, previous, chunk):
    peers, _, chunk_width = received.shape
    rows, width = queries.shape
    blocks = rows // TILE
    picks = slots.shape[0] // blocks
    pairs = chunk_width // PAIR
    base = chunk * pairs
    rows_spec = pl.BlockSpec((rows, PAIR), lambda i, s: (0, base + i))
    pack_spec = pl.BlockSpec((peers, 2 * TILE, PAIR), lambda i, s: (0, 0, i))
    in_specs = [rows_spec] * 4 + [pack_spec]
    operands = [slots, queries, grad_out, key_rows, value_rows, received]
    aliases = {}
    if previous is not None:
        in_specs.append(pl.BlockSpec(memory_space=pl.ANY))
        operands.append(previous)
        aliases = {6: 0}
    keys = TILE * (picks + 1)
    flops = 5 * 2 * 2 * TILE * PAIR * keys * blocks * pairs
    return pl.pallas_call(
        functools.partial(attend_kernel, peers, blocks, picks, previous is not None),
        grid_spec=pltpu.PrefetchScalarGridSpec(
            num_scalar_prefetch=1,
            grid=(pairs,),
            in_specs=in_specs,
            out_specs=[
                rows_spec,
                pl.BlockSpec((2, rows, PAIR), lambda i, s: (0, 0, i)),
                pack_spec,
            ],
            scratch_shapes=[
                pltpu.VMEM((picks + 1, TILE, 2 * TILE), jnp.float32),
                pltpu.VMEM((picks + 1, TILE, 2 * TILE), jnp.float32),
                pltpu.VMEM((picks + 1, TILE, 2 * TILE), jnp.bfloat16),
                pltpu.VMEM((peers, PAIR, TILE), jnp.bfloat16),
                pltpu.VMEM((peers, 2 * TILE, PAIR), jnp.float32),
            ],
        ),
        out_shape=[
            jax.ShapeDtypeStruct((rows, width), jnp.bfloat16),
            jax.ShapeDtypeStruct((2, rows, chunk_width), jnp.float32),
            jax.ShapeDtypeStruct(received.shape, jnp.bfloat16),
        ],
        input_output_aliases=aliases,
        cost_estimate=pl.CostEstimate(
            flops=flops,
            bytes_accessed=24 * 1024 * 1024,
            transcendentals=blocks * pairs * keys * 2 * TILE,
        ),
        compiler_params=pltpu.CompilerParams(vmem_limit_bytes=VMEM_LIMIT),
        name="attend",
    )(*operands)


def combine_kernel(peers, blocks, aliased, ids_ref, own_ref, back_ref, *rest):
    if aliased:
        rest = rest[2:]
    gk_ref, gv_ref, acc = rest
    for b in range(blocks):
        acc[b, :TILE, :] = own_ref[0, b * TILE : (b + 1) * TILE, :]
        acc[b, TILE:, :] = own_ref[1, b * TILE : (b + 1) * TILE, :]

    def add(p, carry):
        target = ids_ref[p]

        @pl.when(target >= 0)
        def _():
            acc[jnp.maximum(target, 0)] += back_ref[p].astype(jnp.float32)

        return carry

    lax.fori_loop(0, peers, add, 0)
    for b in range(blocks):
        gk_ref[b * TILE : (b + 1) * TILE, :] = acc[b, :TILE, :].astype(jnp.bfloat16)
        gv_ref[b * TILE : (b + 1) * TILE, :] = acc[b, TILE:, :].astype(jnp.bfloat16)


def combine(requested, own, returned, previous, chunk, width):
    peers, _, chunk_width = returned.shape
    rows = own.shape[1]
    blocks = rows // TILE
    step = 2 * PAIR
    base = chunk * (chunk_width // step)
    in_specs = [
        pl.BlockSpec((2, rows, step), lambda i, s: (0, 0, i)),
        pl.BlockSpec((peers, 2 * TILE, step), lambda i, s: (0, 0, i)),
    ]
    operands = [requested, own, returned]
    aliases = {}
    if previous is not None:
        in_specs += [pl.BlockSpec(memory_space=pl.ANY)] * 2
        operands += list(previous)
        aliases = {3: 0, 4: 1}
    out_spec = pl.BlockSpec((rows, step), lambda i, s: (0, base + i))
    return pl.pallas_call(
        functools.partial(combine_kernel, peers, blocks, previous is not None),
        grid_spec=pltpu.PrefetchScalarGridSpec(
            num_scalar_prefetch=1,
            grid=(chunk_width // step,),
            in_specs=in_specs,
            out_specs=[out_spec, out_spec],
            scratch_shapes=[pltpu.VMEM((blocks, 2 * TILE, step), jnp.float32)],
        ),
        out_shape=[jax.ShapeDtypeStruct((rows, width), jnp.bfloat16)] * 2,
        input_output_aliases=aliases,
        cost_estimate=pl.CostEstimate(flops=0, bytes_accessed=12 * 1024 * 1024, transcendentals=0),
        compiler_params=pltpu.CompilerParams(vmem_limit_bytes=VMEM_LIMIT),
        name="combine",
    )(*operands)


def exchange(x):
    return lax.all_to_all(x, "ctx", split_axis=0, concat_axis=0, tiled=True)


def on_device(queries, key_rows, value_rows, grad_out, tile_keys):
    rows, width = queries.shape
    blocks = rows // TILE
    peers = lax.axis_size("ctx")
    peer_range = jnp.arange(peers, dtype=jnp.int32)
    owners = tile_keys // blocks
    local_ids = tile_keys % blocks
    matches = owners[:, :, None] == peer_range[None, None, :]
    wanted = jnp.max(jnp.where(matches, local_ids[:, :, None], -1), axis=(0, 1))
    requested = exchange(wanted)
    serve_ids = jnp.maximum(requested, 0)
    slots = owners.reshape(-1)
    chunk_width = width // CHUNKS

    received = [
        exchange(gather_blocks(serve_ids, key_rows, value_rows, c, chunk_width)) for c in range(CHUNKS)
    ]
    grad_queries = None
    owns, backs = [], []
    for c in range(CHUNKS):
        grad_queries, own, out = attend(
            slots, queries, grad_out, key_rows, value_rows, received[c], grad_queries, c
        )
        owns.append(own)
        backs.append(exchange(out))
    result = None
    for c in range(CHUNKS):
        result = combine(requested, owns[c], backs[c], result, c, width)
    return grad_queries, result[0], result[1]


def solution(mesh):
    spec = P(("groups", "ctx"), None)
    return jax.shard_map(
        on_device, mesh=mesh, in_specs=(spec,) * 5, out_specs=(spec,) * 3, check_vma=False
    )
```

```python
import functools

import jax
import jax.numpy as jnp
from jax import lax
from jax.experimental import pallas as pl
from jax.experimental.pallas import tpu as pltpu
from jax.sharding import PartitionSpec as P

HD = 64
TILE = 128
PAIR = 2 * HD
LOG2E = 1.4426950408889634
CHUNKS = 2
VMEM_LIMIT = 48 * 1024 * 1024


def dot_nt(a, b):
    return lax.dot_general(a, b, (((1,), (1,)), ((), ())), preferred_element_type=jnp.float32)


def dot_nn(a, b):
    return lax.dot_general(a, b, (((1,), (0,)), ((), ())), preferred_element_type=jnp.float32)


def gather_kernel(ids_ref, k_ref, v_ref, out_ref):
    rows = pl.ds(pl.multiple_of(ids_ref[pl.program_id(0)] * TILE, TILE), TILE)
    out_ref[0, :TILE, :] = k_ref[rows, :]
    out_ref[0, TILE:, :] = v_ref[rows, :]


def gather_blocks(ids, key_rows, value_rows, chunk, chunk_width):
    peers = ids.shape[0]
    rows_spec = pl.BlockSpec((key_rows.shape[0], chunk_width), lambda p, s: (0, chunk))
    return pl.pallas_call(
        gather_kernel,
        grid_spec=pltpu.PrefetchScalarGridSpec(
            num_scalar_prefetch=1,
            grid=(peers,),
            in_specs=[rows_spec, rows_spec],
            out_specs=pl.BlockSpec((1, 2 * TILE, chunk_width), lambda p, s: (p, 0, 0)),
        ),
        out_shape=jax.ShapeDtypeStruct((peers, 2 * TILE, chunk_width), jnp.bfloat16),
        compiler_params=pltpu.CompilerParams(vmem_limit_bytes=VMEM_LIMIT),
        name="gather_blocks",
    )(ids, key_rows, value_rows)


def attend_kernel(peers, blocks, picks, aliased, slots_ref, q_ref, g_ref, k_ref, v_ref, recv_ref, *rest):
    if aliased:
        rest = rest[1:]
    dq_ref, own_ref, out_ref, s_scr, w_scr, p_scr, kt_scr, acc_scr = rest
    lane = lax.broadcasted_iota(jnp.int32, (TILE, PAIR), 1)
    first = lane < HD

    def prepare(p, carry):
        kt_scr[p] = recv_ref[p, :TILE, :].T
        acc_scr[p] = jnp.zeros((2 * TILE, PAIR), jnp.float32)
        return carry

    lax.fori_loop(0, peers, prepare, 0)

    def split(x):
        zero = jnp.zeros_like(x)
        return jnp.concatenate([jnp.where(first, x, zero), jnp.where(first, zero, x)], axis=0)

    def one_block(b, carry):
        rows = pl.ds(pl.multiple_of(b * TILE, TILE), TILE)
        q2f = split(q_ref[rows, :].astype(jnp.float32) * (HD**-0.5))
        g2f = split(g_ref[rows, :].astype(jnp.float32))
        q2 = q2f.astype(jnp.bfloat16)
        g2 = g2f.astype(jnp.bfloat16)
        slots = [slots_ref[b * picks + j] for j in range(picks)]

        def fold(x, op):
            x = x.reshape(TILE // 8, 8, 2 * TILE)
            return op(x, axis=0)

        top = None
        for j in range(picks + 1):
            if j < picks:
                kb, vb = recv_ref[slots[j], :TILE, :], recv_ref[slots[j], TILE:, :]
            else:
                kb, vb = k_ref[rows, :], v_ref[rows, :]
            s = dot_nt(kb, q2)
            s_scr[j] = s
            w_scr[j] = dot_nt(vb, g2)
            part = fold(s, jnp.max)
            top = part if top is None else jnp.maximum(top, part)
        top = jnp.max(top, axis=0, keepdims=True)
        total = jnp.zeros((8, 2 * TILE), jnp.float32)
        inner = jnp.zeros((8, 2 * TILE), jnp.float32)
        for j in range(picks + 1):
            p = jnp.exp2((s_scr[j] - top) * LOG2E)
            s_scr[j] = p
            p_scr[j] = p.astype(jnp.bfloat16)
            total += fold(p, jnp.sum)
            inner += fold(p * w_scr[j], jnp.sum)
        recip = 1.0 / jnp.sum(total, axis=0, keepdims=True)
        delta = jnp.sum(inner, axis=0, keepdims=True) * recip
        column = jnp.broadcast_to(recip, (PAIR, 2 * TILE)).T
        rq = (q2f * column).astype(jnp.bfloat16)
        rg = (g2f * column).astype(jnp.bfloat16)
        dqt = jnp.zeros((PAIR, 2 * TILE), jnp.float32)
        for j in range(picks + 1):
            ds = (s_scr[j] * (w_scr[j] - delta)).astype(jnp.bfloat16)
            dk = dot_nn(ds, rq)
            dv = dot_nn(p_scr[j], rg)
            if j < picks:
                acc_scr[slots[j], :TILE, :] += dk
                acc_scr[slots[j], TILE:, :] += dv
                kt = kt_scr[slots[j]]
            else:
                own_ref[0, rows, :] = dk
                own_ref[1, rows, :] = dv
                kt = k_ref[rows, :].T
            dqt += dot_nn(kt, ds)
        dqt = dqt * (recip * (HD**-0.5))
        dqt = jnp.concatenate([dqt[:HD, :TILE], dqt[HD:, TILE:]], axis=0)
        dq_ref[rows, :] = dqt.T.astype(jnp.bfloat16)
        return carry

    lax.fori_loop(0, blocks, one_block, 0)

    def finish(p, carry):
        out_ref[p] = acc_scr[p].astype(jnp.bfloat16)
        return carry

    lax.fori_loop(0, peers, finish, 0)


def attend(slots, queries, grad_out, key_rows, value_rows, received, previous, chunk):
    peers, _, chunk_width = received.shape
    rows, width = queries.shape
    blocks = rows // TILE
    picks = slots.shape[0] // blocks
    pairs = chunk_width // PAIR
    base = chunk * pairs
    rows_spec = pl.BlockSpec((rows, PAIR), lambda i, s: (0, base + i))
    pack_spec = pl.BlockSpec((peers, 2 * TILE, PAIR), lambda i, s: (0, 0, i))
    in_specs = [rows_spec] * 4 + [pack_spec]
    operands = [slots, queries, grad_out, key_rows, value_rows, received]
    aliases = {}
    if previous is not None:
        in_specs.append(pl.BlockSpec(memory_space=pl.ANY))
        operands.append(previous)
        aliases = {6: 0}
    keys = TILE * (picks + 1)
    flops = 5 * 2 * 2 * TILE * PAIR * keys * blocks * pairs
    return pl.pallas_call(
        functools.partial(attend_kernel, peers, blocks, picks, previous is not None),
        grid_spec=pltpu.PrefetchScalarGridSpec(
            num_scalar_prefetch=1,
            grid=(pairs,),
            in_specs=in_specs,
            out_specs=[
                rows_spec,
                pl.BlockSpec((2, rows, PAIR), lambda i, s: (0, 0, i)),
                pack_spec,
            ],
            scratch_shapes=[
                pltpu.VMEM((picks + 1, TILE, 2 * TILE), jnp.float32),
                pltpu.VMEM((picks + 1, TILE, 2 * TILE), jnp.float32),
                pltpu.VMEM((picks + 1, TILE, 2 * TILE), jnp.bfloat16),
                pltpu.VMEM((peers, PAIR, TILE), jnp.bfloat16),
                pltpu.VMEM((peers, 2 * TILE, PAIR), jnp.float32),
            ],
        ),
        out_shape=[
            jax.ShapeDtypeStruct((rows, width), jnp.bfloat16),
            jax.ShapeDtypeStruct((2, rows, chunk_width), jnp.float32),
            jax.ShapeDtypeStruct(received.shape, jnp.bfloat16),
        ],
        input_output_aliases=aliases,
        cost_estimate=pl.CostEstimate(
            flops=flops,
            bytes_accessed=24 * 1024 * 1024,
            transcendentals=blocks * pairs * keys * 2 * TILE,
        ),
        compiler_params=pltpu.CompilerParams(vmem_limit_bytes=VMEM_LIMIT),
        name="attend",
    )(*operands)


def combine_kernel(peers, blocks, aliased, ids_ref, own_ref, back_ref, *rest):
    if aliased:
        rest = rest[2:]
    gk_ref, gv_ref, acc = rest
    for b in range(blocks):
        acc[b, :TILE, :] = own_ref[0, b * TILE : (b + 1) * TILE, :]
        acc[b, TILE:, :] = own_ref[1, b * TILE : (b + 1) * TILE, :]

    def add(p, carry):
        target = ids_ref[p]

        @pl.when(target >= 0)
        def _():
            acc[jnp.maximum(target, 0)] += back_ref[p].astype(jnp.float32)

        return carry

    lax.fori_loop(0, peers, add, 0)
    for b in range(blocks):
        gk_ref[b * TILE : (b + 1) * TILE, :] = acc[b, :TILE, :].astype(jnp.bfloat16)
        gv_ref[b * TILE : (b + 1) * TILE, :] = acc[b, TILE:, :].astype(jnp.bfloat16)


def combine(requested, own, returned, previous, chunk, width):
    peers, _, chunk_width = returned.shape
    rows = own.shape[1]
    blocks = rows // TILE
    step = 2 * PAIR
    base = chunk * (chunk_width // step)
    in_specs = [
        pl.BlockSpec((2, rows, step), lambda i, s: (0, 0, i)),
        pl.BlockSpec((peers, 2 * TILE, step), lambda i, s: (0, 0, i)),
    ]
    operands = [requested, own, returned]
    aliases = {}
    if previous is not None:
        in_specs += [pl.BlockSpec(memory_space=pl.ANY)] * 2
        operands += list(previous)
        aliases = {3: 0, 4: 1}
    out_spec = pl.BlockSpec((rows, step), lambda i, s: (0, base + i))
    return pl.pallas_call(
        functools.partial(combine_kernel, peers, blocks, previous is not None),
        grid_spec=pltpu.PrefetchScalarGridSpec(
            num_scalar_prefetch=1,
            grid=(chunk_width // step,),
            in_specs=in_specs,
            out_specs=[out_spec, out_spec],
            scratch_shapes=[pltpu.VMEM((blocks, 2 * TILE, step), jnp.float32)],
        ),
        out_shape=[jax.ShapeDtypeStruct((rows, width), jnp.bfloat16)] * 2,
        input_output_aliases=aliases,
        cost_estimate=pl.CostEstimate(flops=0, bytes_accessed=12 * 1024 * 1024, transcendentals=0),
        compiler_params=pltpu.CompilerParams(vmem_limit_bytes=VMEM_LIMIT),
        name="combine",
    )(*operands)


def exchange(x):
    return lax.all_to_all(x, "ctx", split_axis=0, concat_axis=0, tiled=True)


def on_device(queries, key_rows, value_rows, grad_out, tile_keys):
    rows, width = queries.shape
    blocks = rows // TILE
    peers = lax.axis_size("ctx")
    peer_range = jnp.arange(peers, dtype=jnp.int32)
    owners = tile_keys // blocks
    local_ids = tile_keys % blocks
    matches = owners[:, :, None] == peer_range[None, None, :]
    wanted = jnp.max(jnp.where(matches, local_ids[:, :, None], -1), axis=(0, 1))
    requested = exchange(wanted)
    serve_ids = jnp.maximum(requested, 0)
    slots = owners.reshape(-1)
    chunk_width = width // CHUNKS

    received = [
        exchange(gather_blocks(serve_ids, key_rows, value_rows, c, chunk_width)) for c in range(CHUNKS)
    ]
    grad_queries = None
    owns, backs = [], []
    for c in range(CHUNKS):
        grad_queries, own, out = attend(
            slots, queries, grad_out, key_rows, value_rows, received[c], grad_queries, c
        )
        owns.append(own)
        backs.append(exchange(out))
    result = None
    for c in range(CHUNKS):
        result = combine(requested, owns[c], backs[c], result, c, width)
    return grad_queries, result[0], result[1]


def solution(mesh):
    spec = P(("groups", "ctx"), None)
    return jax.shard_map(
        on_device, mesh=mesh, in_specs=(spec,) * 5, out_specs=(spec,) * 3, check_vma=False
    )
```

```python
import functools

import jax
import jax.numpy as jnp
from jax import lax
from jax.experimental import pallas as pl
from jax.experimental.pallas import tpu as pltpu
from jax.sharding import PartitionSpec as P

HD = 64
TILE = 128
PAIR = 2 * HD
LOG2E = 1.4426950408889634
CHUNKS = 2
VMEM_LIMIT = 60 * 1024 * 1024


def dot_nt(a, b):
    return lax.dot_general(a, b, (((1,), (1,)), ((), ())), preferred_element_type=jnp.float32)


def dot_nn(a, b):
    return lax.dot_general(a, b, (((1,), (0,)), ((), ())), preferred_element_type=jnp.float32)


def gather_kernel(peers, ids_ref, k_ref, v_ref, out_ref, sems):
    def copies(p):
        rows = pl.ds(pl.multiple_of(jnp.maximum(ids_ref[p], 0) * TILE, TILE), TILE)
        return (
            pltpu.make_async_copy(k_ref.at[rows], out_ref.at[p, pl.ds(0, TILE)], sems.at[0, p]),
            pltpu.make_async_copy(v_ref.at[rows], out_ref.at[p, pl.ds(TILE, TILE)], sems.at[1, p]),
        )

    for p in range(peers):
        for copy in copies(p):
            copy.start()
    for p in range(peers):
        for copy in copies(p):
            copy.wait()


def gather_blocks(ids, key_rows, value_rows, chunk, chunk_width):
    peers = ids.shape[0]
    rows_spec = pl.BlockSpec((key_rows.shape[0], chunk_width), lambda i, s: (0, chunk))
    return pl.pallas_call(
        functools.partial(gather_kernel, peers),
        grid_spec=pltpu.PrefetchScalarGridSpec(
            num_scalar_prefetch=1,
            grid=(1,),
            in_specs=[rows_spec, rows_spec],
            out_specs=pl.BlockSpec(memory_space=pl.ANY),
            scratch_shapes=[pltpu.SemaphoreType.DMA((2, peers))],
        ),
        out_shape=jax.ShapeDtypeStruct((peers, 2 * TILE, chunk_width), jnp.bfloat16),
        compiler_params=pltpu.CompilerParams(vmem_limit_bytes=VMEM_LIMIT),
        name="gather_blocks",
    )(ids, key_rows, value_rows)


def attend_kernel(peers, blocks, picks, aliased, slots_ref, q_ref, g_ref, k_ref, v_ref, recv_ref, *rest):
    if aliased:
        rest = rest[1:]
    dq_ref, own_ref, out_ref, s_scr, w_scr, p_scr, kt_scr, acc_scr = rest
    lane = lax.broadcasted_iota(jnp.int32, (TILE, PAIR), 1)
    first = lane < HD

    def prepare(p, carry):
        kt_scr[p] = recv_ref[p, :TILE, :].T
        acc_scr[p] = jnp.zeros((2 * TILE, PAIR), jnp.float32)
        return carry

    lax.fori_loop(0, peers, prepare, 0)

    def split(x):
        zero = jnp.zeros_like(x)
        return jnp.concatenate([jnp.where(first, x, zero), jnp.where(first, zero, x)], axis=0)

    def one_block(b, carry):
        rows = pl.ds(pl.multiple_of(b * TILE, TILE), TILE)
        q2f = split(q_ref[rows, :].astype(jnp.float32) * (HD**-0.5))
        g2f = split(g_ref[rows, :].astype(jnp.float32))
        q2 = q2f.astype(jnp.bfloat16)
        g2 = g2f.astype(jnp.bfloat16)
        slots = [slots_ref[b * picks + j] for j in range(picks)]

        def fold(x, op):
            x = x.reshape(TILE // 8, 8, 2 * TILE)
            return op(x, axis=0)

        top = None
        for j in range(picks + 1):
            if j < picks:
                kb, vb = recv_ref[slots[j], :TILE, :], recv_ref[slots[j], TILE:, :]
            else:
                kb, vb = k_ref[rows, :], v_ref[rows, :]
            s = dot_nt(kb, q2)
            s_scr[j] = s
            w_scr[j] = dot_nt(vb, g2)
            part = fold(s, jnp.max)
            top = part if top is None else jnp.maximum(top, part)
        top = jnp.max(top, axis=0, keepdims=True)
        total = jnp.zeros((8, 2 * TILE), jnp.float32)
        inner = jnp.zeros((8, 2 * TILE), jnp.float32)
        for j in range(picks + 1):
            p = jnp.exp2((s_scr[j] - top) * LOG2E)
            s_scr[j] = p
            p_scr[j] = p.astype(jnp.bfloat16)
            total += fold(p, jnp.sum)
            inner += fold(p * w_scr[j], jnp.sum)
        recip = 1.0 / jnp.sum(total, axis=0, keepdims=True)
        delta = jnp.sum(inner, axis=0, keepdims=True) * recip
        column = jnp.broadcast_to(recip, (PAIR, 2 * TILE)).T
        rq = (q2f * column).astype(jnp.bfloat16)
        rg = (g2f * column).astype(jnp.bfloat16)
        dqt = jnp.zeros((PAIR, 2 * TILE), jnp.float32)
        for j in range(picks + 1):
            ds = (s_scr[j] * (w_scr[j] - delta)).astype(jnp.bfloat16)
            dk = dot_nn(ds, rq)
            dv = dot_nn(p_scr[j], rg)
            if j < picks:
                acc_scr[slots[j], :TILE, :] += dk
                acc_scr[slots[j], TILE:, :] += dv
                kt = kt_scr[slots[j]]
            else:
                own_ref[0, rows, :] = dk
                own_ref[1, rows, :] = dv
                kt = k_ref[rows, :].T
            dqt += dot_nn(kt, ds)
        dqt = dqt * (recip * (HD**-0.5))
        dqt = jnp.concatenate([dqt[:HD, :TILE], dqt[HD:, TILE:]], axis=0)
        dq_ref[rows, :] = dqt.T.astype(jnp.bfloat16)
        return carry

    lax.fori_loop(0, blocks, one_block, 0)

    def finish(p, carry):
        out_ref[p] = acc_scr[p].astype(jnp.bfloat16)
        return carry

    lax.fori_loop(0, peers, finish, 0)


def attend(slots, queries, grad_out, key_rows, value_rows, received, previous, chunk):
    peers, _, chunk_width = received.shape
    rows, width = queries.shape
    blocks = rows // TILE
    picks = slots.shape[0] // blocks
    pairs = chunk_width // PAIR
    base = chunk * pairs
    rows_spec = pl.BlockSpec((rows, PAIR), lambda i, s: (0, base + i))
    pack_spec = pl.BlockSpec((peers, 2 * TILE, PAIR), lambda i, s: (0, 0, i))
    in_specs = [rows_spec] * 4 + [pack_spec]
    operands = [slots, queries, grad_out, key_rows, value_rows, received]
    aliases = {}
    if previous is not None:
        in_specs.append(pl.BlockSpec(memory_space=pl.ANY))
        operands.append(previous)
        aliases = {6: 0}
    keys = TILE * (picks + 1)
    flops = 5 * 2 * 2 * TILE * PAIR * keys * blocks * pairs
    return pl.pallas_call(
        functools.partial(attend_kernel, peers, blocks, picks, previous is not None),
        grid_spec=pltpu.PrefetchScalarGridSpec(
            num_scalar_prefetch=1,
            grid=(pairs,),
            in_specs=in_specs,
            out_specs=[
                rows_spec,
                pl.BlockSpec((2, rows, PAIR), lambda i, s: (0, 0, i)),
                pack_spec,
            ],
            scratch_shapes=[
                pltpu.VMEM((picks + 1, TILE, 2 * TILE), jnp.float32),
                pltpu.VMEM((picks + 1, TILE, 2 * TILE), jnp.float32),
                pltpu.VMEM((picks + 1, TILE, 2 * TILE), jnp.bfloat16),
                pltpu.VMEM((peers, PAIR, TILE), jnp.bfloat16),
                pltpu.VMEM((peers, 2 * TILE, PAIR), jnp.float32),
            ],
        ),
        out_shape=[
            jax.ShapeDtypeStruct((rows, width), jnp.bfloat16),
            jax.ShapeDtypeStruct((2, rows, chunk_width), jnp.float32),
            jax.ShapeDtypeStruct(received.shape, jnp.bfloat16),
        ],
        input_output_aliases=aliases,
        cost_estimate=pl.CostEstimate(
            flops=flops,
            bytes_accessed=24 * 1024 * 1024,
            transcendentals=blocks * pairs * keys * 2 * TILE,
        ),
        compiler_params=pltpu.CompilerParams(vmem_limit_bytes=VMEM_LIMIT),
        name="attend",
    )(*operands)


def combine_kernel(peers, blocks, aliased, ids_ref, own_ref, back_ref, *rest):
    if aliased:
        rest = rest[2:]
    gk_ref, gv_ref, acc = rest
    for b in range(blocks):
        acc[b, :TILE, :] = own_ref[0, b * TILE : (b + 1) * TILE, :]
        acc[b, TILE:, :] = own_ref[1, b * TILE : (b + 1) * TILE, :]

    def add(p, carry):
        target = ids_ref[p]

        @pl.when(target >= 0)
        def _():
            acc[jnp.maximum(target, 0)] += back_ref[p].astype(jnp.float32)

        return carry

    lax.fori_loop(0, peers, add, 0)
    for b in range(blocks):
        gk_ref[b * TILE : (b + 1) * TILE, :] = acc[b, :TILE, :].astype(jnp.bfloat16)
        gv_ref[b * TILE : (b + 1) * TILE, :] = acc[b, TILE:, :].astype(jnp.bfloat16)


def combine(requested, own, returned, previous, chunk, width):
    peers, _, chunk_width = returned.shape
    rows = own.shape[1]
    blocks = rows // TILE
    step = PAIR
    base = chunk * (chunk_width // step)
    in_specs = [
        pl.BlockSpec((2, rows, step), lambda i, s: (0, 0, i)),
        pl.BlockSpec((peers, 2 * TILE, step), lambda i, s: (0, 0, i)),
    ]
    operands = [requested, own, returned]
    aliases = {}
    if previous is not None:
        in_specs += [pl.BlockSpec(memory_space=pl.ANY)] * 2
        operands += list(previous)
        aliases = {3: 0, 4: 1}
    out_spec = pl.BlockSpec((rows, step), lambda i, s: (0, base + i))
    return pl.pallas_call(
        functools.partial(combine_kernel, peers, blocks, previous is not None),
        grid_spec=pltpu.PrefetchScalarGridSpec(
            num_scalar_prefetch=1,
            grid=(chunk_width // step,),
            in_specs=in_specs,
            out_specs=[out_spec, out_spec],
            scratch_shapes=[pltpu.VMEM((blocks, 2 * TILE, step), jnp.float32)],
        ),
        out_shape=[jax.ShapeDtypeStruct((rows, width), jnp.bfloat16)] * 2,
        input_output_aliases=aliases,
        cost_estimate=pl.CostEstimate(flops=0, bytes_accessed=12 * 1024 * 1024, transcendentals=0),
        compiler_params=pltpu.CompilerParams(vmem_limit_bytes=VMEM_LIMIT),
        name="combine",
    )(*operands)


def exchange(x):
    return lax.all_to_all(x, "ctx", split_axis=0, concat_axis=0, tiled=True)


def on_device(queries, key_rows, value_rows, grad_out, tile_keys):
    rows, width = queries.shape
    blocks = rows // TILE
    peers = lax.axis_size("ctx")
    peer_range = jnp.arange(peers, dtype=jnp.int32)
    owners = tile_keys // blocks
    local_ids = tile_keys % blocks
    matches = owners[:, :, None] == peer_range[None, None, :]
    wanted = jnp.max(jnp.where(matches, local_ids[:, :, None], -1), axis=(0, 1))
    requested = exchange(wanted)
    slots = owners.reshape(-1)
    chunk_width = width // CHUNKS

    received = [
        exchange(gather_blocks(requested, key_rows, value_rows, c, chunk_width)) for c in range(CHUNKS)
    ]
    grad_queries = None
    owns, backs = [], []
    for c in range(CHUNKS):
        grad_queries, own, out = attend(
            slots, queries, grad_out, key_rows, value_rows, received[c], grad_queries, c
        )
        owns.append(own)
        backs.append(exchange(out))
    result = None
    for c in range(CHUNKS):
        result = combine(requested, owns[c], backs[c], result, c, width)
    return grad_queries, result[0], result[1]


def solution(mesh):
    spec = P(("groups", "ctx"), None)
    return jax.shard_map(
        on_device, mesh=mesh, in_specs=(spec,) * 5, out_specs=(spec,) * 3, check_vma=False
    )
```

```python
import functools

import jax
import jax.numpy as jnp
from jax import lax
from jax.experimental import pallas as pl
from jax.experimental.pallas import tpu as pltpu
from jax.sharding import PartitionSpec as P

HD = 64
TILE = 128
PAIR = 2 * HD
LOG2E = 1.4426950408889634
CHUNKS = 2
VMEM_LIMIT = 60 * 1024 * 1024


def dot_nt(a, b):
    return lax.dot_general(a, b, (((1,), (1,)), ((), ())), preferred_element_type=jnp.float32)


def dot_nn(a, b):
    return lax.dot_general(a, b, (((1,), (0,)), ((), ())), preferred_element_type=jnp.float32)


def gather_kernel(peers, ids_ref, k_ref, v_ref, out_ref, sems):
    def copies(p):
        rows = pl.ds(pl.multiple_of(jnp.maximum(ids_ref[p], 0) * TILE, TILE), TILE)
        return (
            pltpu.make_async_copy(k_ref.at[rows], out_ref.at[p, pl.ds(0, TILE)], sems.at[0, p]),
            pltpu.make_async_copy(v_ref.at[rows], out_ref.at[p, pl.ds(TILE, TILE)], sems.at[1, p]),
        )

    for p in range(peers):
        for copy in copies(p):
            copy.start()
    for p in range(peers):
        for copy in copies(p):
            copy.wait()


def gather_blocks(ids, key_rows, value_rows, chunk, chunk_width):
    peers = ids.shape[0]
    rows_spec = pl.BlockSpec((key_rows.shape[0], chunk_width), lambda i, s: (0, chunk))
    return pl.pallas_call(
        functools.partial(gather_kernel, peers),
        grid_spec=pltpu.PrefetchScalarGridSpec(
            num_scalar_prefetch=1,
            grid=(1,),
            in_specs=[rows_spec, rows_spec],
            out_specs=pl.BlockSpec(memory_space=pl.ANY),
            scratch_shapes=[pltpu.SemaphoreType.DMA((2, peers))],
        ),
        out_shape=jax.ShapeDtypeStruct((peers, 2 * TILE, chunk_width), jnp.bfloat16),
        compiler_params=pltpu.CompilerParams(vmem_limit_bytes=VMEM_LIMIT),
        name="gather_blocks",
    )(ids, key_rows, value_rows)


def attend_kernel(peers, blocks, picks, aliased, slots_ref, q_ref, g_ref, k_ref, v_ref, recv_ref, *rest):
    if aliased:
        rest = rest[1:]
    dq_ref, own_ref, out_ref, s_scr, w_scr, p_scr, kt_scr, acc_scr = rest
    lane = lax.broadcasted_iota(jnp.int32, (TILE, PAIR), 1)
    first = lane < HD

    def prepare(p, carry):
        kt_scr[p] = recv_ref[p, :TILE, :].T
        acc_scr[p] = jnp.zeros((2 * TILE, PAIR), jnp.float32)
        return carry

    lax.fori_loop(0, peers, prepare, 0)

    def split(x):
        zero = jnp.zeros_like(x)
        return jnp.concatenate([jnp.where(first, x, zero), jnp.where(first, zero, x)], axis=0)

    def one_block(b, carry):
        rows = pl.ds(pl.multiple_of(b * TILE, TILE), TILE)
        q2f = split(q_ref[rows, :].astype(jnp.float32) * (HD**-0.5))
        g2f = split(g_ref[rows, :].astype(jnp.float32))
        q2 = q2f.astype(jnp.bfloat16)
        g2 = g2f.astype(jnp.bfloat16)
        slots = [slots_ref[b * picks + j] for j in range(picks)]

        def fold(x, op):
            x = x.reshape(TILE // 8, 8, 2 * TILE)
            return op(x, axis=0)

        top = None
        for j in range(picks + 1):
            if j < picks:
                kb, vb = recv_ref[slots[j], :TILE, :], recv_ref[slots[j], TILE:, :]
            else:
                kb, vb = k_ref[rows, :], v_ref[rows, :]
            s = dot_nt(kb, q2)
            s_scr[j] = s
            w_scr[j] = dot_nt(vb, g2)
            part = fold(s, jnp.max)
            top = part if top is None else jnp.maximum(top, part)
        top = jnp.max(top, axis=0, keepdims=True)
        total = jnp.zeros((8, 2 * TILE), jnp.float32)
        inner = jnp.zeros((8, 2 * TILE), jnp.float32)
        for j in range(picks + 1):
            p = jnp.exp2((s_scr[j] - top) * LOG2E)
            s_scr[j] = p
            p_scr[j] = p.astype(jnp.bfloat16)
            total += fold(p, jnp.sum)
            inner += fold(p * w_scr[j], jnp.sum)
        recip = 1.0 / jnp.sum(total, axis=0, keepdims=True)
        delta = jnp.sum(inner, axis=0, keepdims=True) * recip
        column = jnp.broadcast_to(recip, (PAIR, 2 * TILE)).T
        rq = (q2f * column).astype(jnp.bfloat16)
        rg = (g2f * column).astype(jnp.bfloat16)
        dqt = jnp.zeros((PAIR, 2 * TILE), jnp.float32)
        for j in range(picks + 1):
            ds = (s_scr[j] * (w_scr[j] - delta)).astype(jnp.bfloat16)
            dk = dot_nn(ds, rq)
            dv = dot_nn(p_scr[j], rg)
            if j < picks:
                acc_scr[slots[j], :TILE, :] += dk
                acc_scr[slots[j], TILE:, :] += dv
                kt = kt_scr[slots[j]]
            else:
                own_ref[0, rows, :] = dk
                own_ref[1, rows, :] = dv
                kt = k_ref[rows, :].T
            dqt += dot_nn(kt, ds)
        dqt = dqt * (recip * (HD**-0.5))
        dqt = jnp.concatenate([dqt[:HD, :TILE], dqt[HD:, TILE:]], axis=0)
        dq_ref[rows, :] = dqt.T.astype(jnp.bfloat16)
        return carry

    lax.fori_loop(0, blocks, one_block, 0)

    def finish(p, carry):
        out_ref[p] = acc_scr[p].astype(jnp.bfloat16)
        return carry

    lax.fori_loop(0, peers, finish, 0)


def attend(slots, queries, grad_out, key_rows, value_rows, received, previous, chunk):
    peers, _, chunk_width = received.shape
    rows, width = queries.shape
    blocks = rows // TILE
    picks = slots.shape[0] // blocks
    pairs = chunk_width // PAIR
    base = chunk * pairs
    rows_spec = pl.BlockSpec((rows, PAIR), lambda i, s: (0, base + i))
    pack_spec = pl.BlockSpec((peers, 2 * TILE, PAIR), lambda i, s: (0, 0, i))
    in_specs = [rows_spec] * 4 + [pack_spec]
    operands = [slots, queries, grad_out, key_rows, value_rows, received]
    aliases = {}
    if previous is not None:
        in_specs.append(pl.BlockSpec(memory_space=pl.ANY))
        operands.append(previous)
        aliases = {6: 0}
    keys = TILE * (picks + 1)
    flops = 5 * 2 * 2 * TILE * PAIR * keys * blocks * pairs
    return pl.pallas_call(
        functools.partial(attend_kernel, peers, blocks, picks, previous is not None),
        grid_spec=pltpu.PrefetchScalarGridSpec(
            num_scalar_prefetch=1,
            grid=(pairs,),
            in_specs=in_specs,
            out_specs=[
                rows_spec,
                pl.BlockSpec((2, rows, PAIR), lambda i, s: (0, 0, i)),
                pack_spec,
            ],
            scratch_shapes=[
                pltpu.VMEM((picks + 1, TILE, 2 * TILE), jnp.float32),
                pltpu.VMEM((picks + 1, TILE, 2 * TILE), jnp.float32),
                pltpu.VMEM((picks + 1, TILE, 2 * TILE), jnp.bfloat16),
                pltpu.VMEM((peers, PAIR, TILE), jnp.bfloat16),
                pltpu.VMEM((peers, 2 * TILE, PAIR), jnp.float32),
            ],
        ),
        out_shape=[
            jax.ShapeDtypeStruct((rows, width), jnp.bfloat16),
            jax.ShapeDtypeStruct((2, rows, chunk_width), jnp.float32),
            jax.ShapeDtypeStruct(received.shape, jnp.bfloat16),
        ],
        input_output_aliases=aliases,
        cost_estimate=pl.CostEstimate(
            flops=flops,
            bytes_accessed=24 * 1024 * 1024,
            transcendentals=blocks * pairs * keys * 2 * TILE,
        ),
        compiler_params=pltpu.CompilerParams(vmem_limit_bytes=VMEM_LIMIT),
        name="attend",
    )(*operands)


def combine_kernel(peers, blocks, aliased, ids_ref, own_ref, back_ref, *rest):
    if aliased:
        rest = rest[2:]
    gk_ref, gv_ref, acc = rest
    for b in range(blocks):
        acc[b, :TILE, :] = own_ref[0, b * TILE : (b + 1) * TILE, :]
        acc[b, TILE:, :] = own_ref[1, b * TILE : (b + 1) * TILE, :]

    def add(p, carry):
        target = ids_ref[p]

        @pl.when(target >= 0)
        def _():
            acc[jnp.maximum(target, 0)] += back_ref[p].astype(jnp.float32)

        return carry

    lax.fori_loop(0, peers, add, 0)
    for b in range(blocks):
        gk_ref[b * TILE : (b + 1) * TILE, :] = acc[b, :TILE, :].astype(jnp.bfloat16)
        gv_ref[b * TILE : (b + 1) * TILE, :] = acc[b, TILE:, :].astype(jnp.bfloat16)


def combine(requested, own, returned, previous, chunk, width):
    peers, _, chunk_width = returned.shape
    rows = own.shape[1]
    blocks = rows // TILE
    step = PAIR
    base = chunk * (chunk_width // step)
    in_specs = [
        pl.BlockSpec((2, rows, step), lambda i, s: (0, 0, i)),
        pl.BlockSpec((peers, 2 * TILE, step), lambda i, s: (0, 0, i)),
    ]
    operands = [requested, own, returned]
    aliases = {}
    if previous is not None:
        in_specs += [pl.BlockSpec(memory_space=pl.ANY)] * 2
        operands += list(previous)
        aliases = {3: 0, 4: 1}
    out_spec = pl.BlockSpec((rows, step), lambda i, s: (0, base + i))
    return pl.pallas_call(
        functools.partial(combine_kernel, peers, blocks, previous is not None),
        grid_spec=pltpu.PrefetchScalarGridSpec(
            num_scalar_prefetch=1,
            grid=(chunk_width // step,),
            in_specs=in_specs,
            out_specs=[out_spec, out_spec],
            scratch_shapes=[pltpu.VMEM((blocks, 2 * TILE, step), jnp.float32)],
        ),
        out_shape=[jax.ShapeDtypeStruct((rows, width), jnp.bfloat16)] * 2,
        input_output_aliases=aliases,
        cost_estimate=pl.CostEstimate(flops=0, bytes_accessed=12 * 1024 * 1024, transcendentals=0),
        compiler_params=pltpu.CompilerParams(vmem_limit_bytes=VMEM_LIMIT),
        name="combine",
    )(*operands)


def exchange(x):
    return lax.all_to_all(x, "ctx", split_axis=0, concat_axis=0, tiled=True)


def merge_lanes(a, b):
    low = jnp.concatenate([a[:, :HD], b[:, :HD]], axis=1)
    high = jnp.concatenate([a[:, HD:], b[:, HD:]], axis=1)
    return low, high


def pack_kernel(a_ref, b_ref, out_ref):
    out_ref[0], out_ref[1] = merge_lanes(a_ref[...], b_ref[...])


def pack_heads(a, b, start, count):
    rows, width = a.shape
    tokens = count * TILE
    first = start // count
    spec = pl.BlockSpec((tokens, PAIR), lambda i: (first, i))
    return pl.pallas_call(
        pack_kernel,
        grid=(width // PAIR,),
        in_specs=[spec, spec],
        out_specs=pl.BlockSpec((2, tokens, PAIR), lambda i: (i, 0, 0)),
        out_shape=jax.ShapeDtypeStruct((width // HD, tokens, PAIR), jnp.bfloat16),
        cost_estimate=pl.CostEstimate(
            flops=0, bytes_accessed=8 * tokens * width, transcendentals=0
        ),
        compiler_params=pltpu.CompilerParams(vmem_limit_bytes=VMEM_LIMIT),
        name="pack_heads",
    )(a, b)


def turn_kernel(kv_ref, out_ref):
    for j in range(kv_ref.shape[0] // TILE):
        out_ref[j] = kv_ref[j * TILE : (j + 1) * TILE, :].T[:HD, :]


def turn_keys(kv):
    total = kv.shape[0] // TILE
    step = 8
    return pl.pallas_call(
        turn_kernel,
        grid=(total // step,),
        in_specs=[pl.BlockSpec((step * TILE, PAIR), lambda i: (i, 0))],
        out_specs=pl.BlockSpec((step, HD, TILE), lambda i: (i, 0, 0)),
        out_shape=jax.ShapeDtypeStruct((total, HD, TILE), jnp.bfloat16),
        compiler_params=pltpu.CompilerParams(vmem_limit_bytes=VMEM_LIMIT),
        name="turn_keys",
    )(kv)


def head_kernel(dims, *refs):
    blocks, picks, start, count, last = dims
    if last:
        table_ref, qg_ref, kv_ref, kt_ref, before_ref, out_ref, acc_ref, before_scr, sem = refs[:9]
        scratch = refs[9:]
    else:
        table_ref, qg_ref, kv_ref, kt_ref, out_ref, acc_ref = refs[:6]
        scratch = refs[6:]
    source = pl.program_id(0)
    sources = pl.num_programs(0)
    width = TILE * (picks + 1)
    lane = lax.broadcasted_iota(jnp.int32, (TILE, PAIR), 1)
    low = lane < HD

    @pl.when(source == 0)
    def _():
        acc_ref[...] = jnp.zeros_like(acc_ref)
        if last:
            pltpu.make_async_copy(before_ref, before_scr, sem).start()

    def fold(x, op):
        return op(x.reshape(-1, 8, x.shape[-1]), axis=0)

    def spans(block):
        named = [table_ref[block * picks + j] for j in range(picks)] + [block]
        return named, [pl.ds(pl.multiple_of(n * TILE, TILE), TILE) for n in named]

    def one_block(local, raw_scr, pair_scr):
        block = source * blocks + start + local
        named, rows = spans(block)
        qg = qg_ref[0, pl.ds(pl.multiple_of(local * TILE, TILE), TILE), :].astype(jnp.float32)
        zero = jnp.zeros_like(qg)
        both = jnp.concatenate(
            [jnp.where(low, qg * (HD**-0.5), zero), jnp.where(low, zero, qg)], axis=0
        )
        keys = jnp.concatenate([kv_ref[r, :] for r in rows], axis=0)
        raw = dot_nt(keys, both.astype(jnp.bfloat16))
        raw_scr[...] = raw
        top = jnp.max(fold(raw[:, :TILE], jnp.max), axis=0, keepdims=True)
        total = jnp.zeros((8, TILE), jnp.float32)
        inner = jnp.zeros((8, TILE), jnp.float32)
        for j in range(picks + 1):
            part = slice(j * TILE, (j + 1) * TILE)
            p = jnp.exp2((raw_scr[part, :TILE] - top) * LOG2E)
            raw_scr[part, :TILE] = p
            pair_scr[part, TILE:] = p.astype(jnp.bfloat16)
            total += fold(p, jnp.sum)
            inner += fold(p * raw_scr[part, TILE:], jnp.sum)
        recip = 1.0 / jnp.sum(total, axis=0, keepdims=True)
        delta = jnp.sum(inner, axis=0, keepdims=True) * recip
        for j in range(picks + 1):
            part = slice(j * TILE, (j + 1) * TILE)
            ds = raw_scr[part, :TILE] * (raw_scr[part, TILE:] - delta)
            pair_scr[part, :TILE] = ds.astype(jnp.bfloat16)
        column = jnp.broadcast_to(recip, (TILE, TILE)).T
        scaled = jnp.concatenate([both[:TILE] * column, both[TILE:] * column], axis=0)
        grads = dot_nn(pair_scr[...], scaled.astype(jnp.bfloat16))
        for j in range(picks + 1):
            acc_ref[rows[j], :] += grads[j * TILE : (j + 1) * TILE, :]
        turned = jnp.concatenate([kt_ref[n] for n in named], axis=1)
        dqt = dot_nn(turned, pair_scr[:, :TILE])
        return dqt * (recip * (HD**-0.5))

    offset = blocks * TILE if last else 0

    def two_blocks(m, carry):
        first = one_block(2 * m, scratch[0], scratch[1])
        second = one_block(2 * m + 1, scratch[2], scratch[3])
        both = jnp.concatenate([first, second], axis=0).T.astype(jnp.bfloat16)
        if last:
            out_ref[source, pl.ds(pl.multiple_of(offset + m * TILE, TILE), TILE), :] = both
        else:
            out_ref[0, pl.ds(pl.multiple_of(m * TILE, TILE), TILE), :] = both
        return carry

    lax.fori_loop(0, count // 2, two_blocks, 0)

    if last:

        @pl.when(source == sources - 1)
        def _():
            pltpu.make_async_copy(before_ref, before_scr, sem).wait()

            def finish(s, carry):
                rows = pl.ds(pl.multiple_of(s * blocks * TILE, TILE), blocks * TILE)
                out_ref[s, : blocks * TILE, :] = (acc_ref[rows, :] + before_scr[rows, :]).astype(
                    jnp.bfloat16
                )
                return carry

            lax.fori_loop(0, sources, finish, 0)


def attend_head(table, qg, kv, turned, before, blocks, start):
    peers, tokens, _ = qg.shape
    total = kv.shape[0]
    count = tokens // TILE
    picks = table.shape[0] // (total // TILE)
    last = before is not None
    keys = TILE * (picks + 1)
    in_specs = [
        pl.BlockSpec((1, tokens, PAIR), lambda i, t: (i, 0, 0)),
        pl.BlockSpec((total, PAIR), lambda i, t: (0, 0)),
        pl.BlockSpec(turned.shape, lambda i, t: (0, 0, 0)),
    ]
    operands = [table, qg, kv, turned]
    acc_shape = (total, PAIR)
    scratch = [
        pltpu.VMEM((keys, 2 * TILE), jnp.float32),
        pltpu.VMEM((keys, 2 * TILE), jnp.bfloat16),
        pltpu.VMEM((keys, 2 * TILE), jnp.float32),
        pltpu.VMEM((keys, 2 * TILE), jnp.bfloat16),
    ]
    if last:
        in_specs.append(pl.BlockSpec(memory_space=pl.ANY))
        operands.append(before)
        packed = (peers, (blocks + count // 2) * TILE, PAIR)
        out_specs = pl.BlockSpec(packed, lambda i, t: (0, 0, 0))
        out_shape = jax.ShapeDtypeStruct(packed, jnp.bfloat16)
        scratch = [
            pltpu.VMEM(acc_shape, jnp.float32),
            pltpu.VMEM(acc_shape, jnp.float32),
            pltpu.SemaphoreType.DMA,
        ] + scratch
    else:
        out_specs = [
            pl.BlockSpec((1, tokens // 2, PAIR), lambda i, t: (i, 0, 0)),
            pl.BlockSpec(acc_shape, lambda i, t: (0, 0)),
        ]
        out_shape = [
            jax.ShapeDtypeStruct((peers, tokens // 2, PAIR), jnp.bfloat16),
            jax.ShapeDtypeStruct(acc_shape, jnp.float32),
        ]
    return pl.pallas_call(
        functools.partial(head_kernel, (blocks, picks, start, count, last)),
        grid_spec=pltpu.PrefetchScalarGridSpec(
            num_scalar_prefetch=1,
            grid=(peers,),
            in_specs=in_specs,
            out_specs=out_specs,
            scratch_shapes=scratch,
        ),
        out_shape=out_shape,
        cost_estimate=pl.CostEstimate(
            flops=5 * 2 * 2 * TILE * PAIR * keys * peers * count // 2,
            bytes_accessed=24 * 1024 * 1024,
            transcendentals=peers * count * keys * TILE,
        ),
        compiler_params=pltpu.CompilerParams(vmem_limit_bytes=VMEM_LIMIT),
        name="attend_head",
    )(*operands)


def unpack_kernel(blocks, start, count, last, in_ref, *refs):
    refs = refs[-3:] if last else refs[-1:]
    gq_ref = refs[0]
    offset = 0
    if last:
        offset = blocks * TILE
        refs[1][...], refs[2][...] = merge_lanes(in_ref[0, :offset, :], in_ref[1, :offset, :])
    for m in range(count // 2):
        rows = slice(offset + m * TILE, offset + (m + 1) * TILE)
        even, odd = merge_lanes(in_ref[0, rows, :], in_ref[1, rows, :])
        gq_ref[2 * m * TILE : (2 * m + 1) * TILE, :] = even
        gq_ref[(2 * m + 1) * TILE : (2 * m + 2) * TILE, :] = odd


def unpack_heads(back, previous, blocks, start, count):
    heads, tokens, _ = back.shape
    width = heads * HD
    last = previous is not None
    rows = blocks * TILE
    first = start // count
    in_specs = [pl.BlockSpec((2, tokens, PAIR), lambda i: (i, 0, 0))]
    operands = [back]
    out_specs = [pl.BlockSpec((count * TILE, PAIR), lambda i: (first, i))]
    out_shape = [jax.ShapeDtypeStruct((rows, width), jnp.bfloat16)]
    aliases = {}
    if last:
        in_specs.append(pl.BlockSpec(memory_space=pl.ANY))
        operands.append(previous)
        aliases = {1: 0}
        out_specs += [pl.BlockSpec((rows, PAIR), lambda i: (0, i))] * 2
        out_shape += [out_shape[0]] * 2
    return pl.pallas_call(
        functools.partial(unpack_kernel, blocks, start, count, last),
        grid=(heads // 2,),
        in_specs=in_specs,
        out_specs=out_specs,
        out_shape=out_shape,
        input_output_aliases=aliases,
        cost_estimate=pl.CostEstimate(
            flops=0, bytes_accessed=4 * heads * tokens * PAIR, transcendentals=0
        ),
        compiler_params=pltpu.CompilerParams(vmem_limit_bytes=VMEM_LIMIT),
        name="unpack_heads",
    )(*operands)


def by_heads(queries, key_rows, value_rows, grad_out, tile_keys):
    rows, _ = queries.shape
    blocks = rows // TILE
    half = blocks // 2
    table = lax.all_gather(tile_keys, "ctx", tiled=True).reshape(-1)
    kv = exchange(pack_heads(key_rows, value_rows, 0, blocks))
    qg = [exchange(pack_heads(queries, grad_out, c * half, half)) for c in range(2)]
    kv = kv.reshape(-1, PAIR)
    turned = turn_keys(kv)
    dq, before = attend_head(table, qg[0], kv, turned, None, blocks, 0)
    back = exchange(dq)
    packed = attend_head(table, qg[1], kv, turned, before, blocks, half)
    final = exchange(packed)
    grad_queries = unpack_heads(back, None, blocks, 0, half)[0]
    return unpack_heads(final, grad_queries, blocks, half, half)


def by_blocks(queries, key_rows, value_rows, grad_out, tile_keys):
    rows, width = queries.shape
    blocks = rows // TILE
    peers = lax.axis_size("ctx")
    peer_range = jnp.arange(peers, dtype=jnp.int32)
    owners = tile_keys // blocks
    local_ids = tile_keys % blocks
    matches = owners[:, :, None] == peer_range[None, None, :]
    wanted = jnp.max(jnp.where(matches, local_ids[:, :, None], -1), axis=(0, 1))
    requested = exchange(wanted)
    slots = owners.reshape(-1)
    chunk_width = width // CHUNKS

    received = [
        exchange(gather_blocks(requested, key_rows, value_rows, c, chunk_width)) for c in range(CHUNKS)
    ]
    grad_queries = None
    owns, backs = [], []
    for c in range(CHUNKS):
        grad_queries, own, out = attend(
            slots, queries, grad_out, key_rows, value_rows, received[c], grad_queries, c
        )
        owns.append(own)
        backs.append(exchange(out))
    result = None
    for c in range(CHUNKS):
        result = combine(requested, owns[c], backs[c], result, c, width)
    return grad_queries, result[0], result[1]


def on_device(queries, key_rows, value_rows, grad_out, tile_keys):
    split_evenly = lax.axis_size("ctx") * HD == queries.shape[1]
    plan = by_heads if split_evenly and queries.shape[0] % (4 * TILE) == 0 else by_blocks
    return tuple(plan(queries, key_rows, value_rows, grad_out, tile_keys))


def solution(mesh):
    spec = P(("groups", "ctx"), None)
    return jax.shard_map(
        on_device, mesh=mesh, in_specs=(spec,) * 5, out_specs=(spec,) * 3, check_vma=False
    )
```

```python
import functools

import jax
import jax.numpy as jnp
from jax import lax
from jax.experimental import pallas as pl
from jax.experimental.pallas import tpu as pltpu
from jax.sharding import PartitionSpec as P

HD = 64
TILE = 128
PAIR = 2 * HD
LOG2E = 1.4426950408889634
CHUNKS = 2
DEPTH = 4
VMEM_LIMIT = 60 * 1024 * 1024


def dot_nt(a, b):
    return lax.dot_general(a, b, (((1,), (1,)), ((), ())), preferred_element_type=jnp.float32)


def dot_nn(a, b):
    return lax.dot_general(a, b, (((1,), (0,)), ((), ())), preferred_element_type=jnp.float32)


def gather_kernel(peers, ids_ref, k_ref, v_ref, out_ref, sems):
    def copies(p):
        rows = pl.ds(pl.multiple_of(jnp.maximum(ids_ref[p], 0) * TILE, TILE), TILE)
        return (
            pltpu.make_async_copy(k_ref.at[rows], out_ref.at[p, pl.ds(0, TILE)], sems.at[0, p]),
            pltpu.make_async_copy(v_ref.at[rows], out_ref.at[p, pl.ds(TILE, TILE)], sems.at[1, p]),
        )

    for p in range(peers):
        for copy in copies(p):
            copy.start()
    for p in range(peers):
        for copy in copies(p):
            copy.wait()


def gather_blocks(ids, key_rows, value_rows, chunk, chunk_width):
    peers = ids.shape[0]
    rows_spec = pl.BlockSpec((key_rows.shape[0], chunk_width), lambda i, s: (0, chunk))
    return pl.pallas_call(
        functools.partial(gather_kernel, peers),
        grid_spec=pltpu.PrefetchScalarGridSpec(
            num_scalar_prefetch=1,
            grid=(1,),
            in_specs=[rows_spec, rows_spec],
            out_specs=pl.BlockSpec(memory_space=pl.ANY),
            scratch_shapes=[pltpu.SemaphoreType.DMA((2, peers))],
        ),
        out_shape=jax.ShapeDtypeStruct((peers, 2 * TILE, chunk_width), jnp.bfloat16),
        compiler_params=pltpu.CompilerParams(vmem_limit_bytes=VMEM_LIMIT),
        name="gather_blocks",
    )(ids, key_rows, value_rows)


def attend_kernel(peers, blocks, picks, aliased, slots_ref, q_ref, g_ref, k_ref, v_ref, recv_ref, *rest):
    if aliased:
        rest = rest[1:]
    dq_ref, own_ref, out_ref, s_scr, w_scr, p_scr, kt_scr, acc_scr = rest
    lane = lax.broadcasted_iota(jnp.int32, (TILE, PAIR), 1)
    first = lane < HD

    def prepare(p, carry):
        kt_scr[p] = recv_ref[p, :TILE, :].T
        acc_scr[p] = jnp.zeros((2 * TILE, PAIR), jnp.float32)
        return carry

    lax.fori_loop(0, peers, prepare, 0)

    def split(x):
        zero = jnp.zeros_like(x)
        return jnp.concatenate([jnp.where(first, x, zero), jnp.where(first, zero, x)], axis=0)

    def one_block(b, carry):
        rows = pl.ds(pl.multiple_of(b * TILE, TILE), TILE)
        q2f = split(q_ref[rows, :].astype(jnp.float32) * (HD**-0.5))
        g2f = split(g_ref[rows, :].astype(jnp.float32))
        q2 = q2f.astype(jnp.bfloat16)
        g2 = g2f.astype(jnp.bfloat16)
        slots = [slots_ref[b * picks + j] for j in range(picks)]

        def fold(x, op):
            x = x.reshape(TILE // 8, 8, 2 * TILE)
            return op(x, axis=0)

        top = None
        for j in range(picks + 1):
            if j < picks:
                kb, vb = recv_ref[slots[j], :TILE, :], recv_ref[slots[j], TILE:, :]
            else:
                kb, vb = k_ref[rows, :], v_ref[rows, :]
            s = dot_nt(kb, q2)
            s_scr[j] = s
            w_scr[j] = dot_nt(vb, g2)
            part = fold(s, jnp.max)
            top = part if top is None else jnp.maximum(top, part)
        top = jnp.max(top, axis=0, keepdims=True)
        total = jnp.zeros((8, 2 * TILE), jnp.float32)
        inner = jnp.zeros((8, 2 * TILE), jnp.float32)
        for j in range(picks + 1):
            p = jnp.exp2((s_scr[j] - top) * LOG2E)
            s_scr[j] = p
            p_scr[j] = p.astype(jnp.bfloat16)
            total += fold(p, jnp.sum)
            inner += fold(p * w_scr[j], jnp.sum)
        recip = 1.0 / jnp.sum(total, axis=0, keepdims=True)
        delta = jnp.sum(inner, axis=0, keepdims=True) * recip
        column = jnp.broadcast_to(recip, (PAIR, 2 * TILE)).T
        rq = (q2f * column).astype(jnp.bfloat16)
        rg = (g2f * column).astype(jnp.bfloat16)
        dqt = jnp.zeros((PAIR, 2 * TILE), jnp.float32)
        for j in range(picks + 1):
            ds = (s_scr[j] * (w_scr[j] - delta)).astype(jnp.bfloat16)
            dk = dot_nn(ds, rq)
            dv = dot_nn(p_scr[j], rg)
            if j < picks:
                acc_scr[slots[j], :TILE, :] += dk
                acc_scr[slots[j], TILE:, :] += dv
                kt = kt_scr[slots[j]]
            else:
                own_ref[0, rows, :] = dk
                own_ref[1, rows, :] = dv
                kt = k_ref[rows, :].T
            dqt += dot_nn(kt, ds)
        dqt = dqt * (recip * (HD**-0.5))
        dqt = jnp.concatenate([dqt[:HD, :TILE], dqt[HD:, TILE:]], axis=0)
        dq_ref[rows, :] = dqt.T.astype(jnp.bfloat16)
        return carry

    lax.fori_loop(0, blocks, one_block, 0)

    def finish(p, carry):
        out_ref[p] = acc_scr[p].astype(jnp.bfloat16)
        return carry

    lax.fori_loop(0, peers, finish, 0)


def attend(slots, queries, grad_out, key_rows, value_rows, received, previous, chunk):
    peers, _, chunk_width = received.shape
    rows, width = queries.shape
    blocks = rows // TILE
    picks = slots.shape[0] // blocks
    pairs = chunk_width // PAIR
    base = chunk * pairs
    rows_spec = pl.BlockSpec((rows, PAIR), lambda i, s: (0, base + i))
    pack_spec = pl.BlockSpec((peers, 2 * TILE, PAIR), lambda i, s: (0, 0, i))
    in_specs = [rows_spec] * 4 + [pack_spec]
    operands = [slots, queries, grad_out, key_rows, value_rows, received]
    aliases = {}
    if previous is not None:
        in_specs.append(pl.BlockSpec(memory_space=pl.ANY))
        operands.append(previous)
        aliases = {6: 0}
    keys = TILE * (picks + 1)
    flops = 5 * 2 * 2 * TILE * PAIR * keys * blocks * pairs
    return pl.pallas_call(
        functools.partial(attend_kernel, peers, blocks, picks, previous is not None),
        grid_spec=pltpu.PrefetchScalarGridSpec(
            num_scalar_prefetch=1,
            grid=(pairs,),
            in_specs=in_specs,
            out_specs=[
                rows_spec,
                pl.BlockSpec((2, rows, PAIR), lambda i, s: (0, 0, i)),
                pack_spec,
            ],
            scratch_shapes=[
                pltpu.VMEM((picks + 1, TILE, 2 * TILE), jnp.float32),
                pltpu.VMEM((picks + 1, TILE, 2 * TILE), jnp.float32),
                pltpu.VMEM((picks + 1, TILE, 2 * TILE), jnp.bfloat16),
                pltpu.VMEM((peers, PAIR, TILE), jnp.bfloat16),
                pltpu.VMEM((peers, 2 * TILE, PAIR), jnp.float32),
            ],
        ),
        out_shape=[
            jax.ShapeDtypeStruct((rows, width), jnp.bfloat16),
            jax.ShapeDtypeStruct((2, rows, chunk_width), jnp.float32),
            jax.ShapeDtypeStruct(received.shape, jnp.bfloat16),
        ],
        input_output_aliases=aliases,
        cost_estimate=pl.CostEstimate(
            flops=flops,
            bytes_accessed=24 * 1024 * 1024,
            transcendentals=blocks * pairs * keys * 2 * TILE,
        ),
        compiler_params=pltpu.CompilerParams(vmem_limit_bytes=VMEM_LIMIT),
        name="attend",
    )(*operands)


def combine_kernel(peers, blocks, aliased, ids_ref, own_ref, back_ref, *rest):
    if aliased:
        rest = rest[2:]
    gk_ref, gv_ref, acc = rest
    for b in range(blocks):
        acc[b, :TILE, :] = own_ref[0, b * TILE : (b + 1) * TILE, :]
        acc[b, TILE:, :] = own_ref[1, b * TILE : (b + 1) * TILE, :]

    def add(p, carry):
        target = ids_ref[p]

        @pl.when(target >= 0)
        def _():
            acc[jnp.maximum(target, 0)] += back_ref[p].astype(jnp.float32)

        return carry

    lax.fori_loop(0, peers, add, 0)
    for b in range(blocks):
        gk_ref[b * TILE : (b + 1) * TILE, :] = acc[b, :TILE, :].astype(jnp.bfloat16)
        gv_ref[b * TILE : (b + 1) * TILE, :] = acc[b, TILE:, :].astype(jnp.bfloat16)


def combine(requested, own, returned, previous, chunk, width):
    peers, _, chunk_width = returned.shape
    rows = own.shape[1]
    blocks = rows // TILE
    step = PAIR
    base = chunk * (chunk_width // step)
    in_specs = [
        pl.BlockSpec((2, rows, step), lambda i, s: (0, 0, i)),
        pl.BlockSpec((peers, 2 * TILE, step), lambda i, s: (0, 0, i)),
    ]
    operands = [requested, own, returned]
    aliases = {}
    if previous is not None:
        in_specs += [pl.BlockSpec(memory_space=pl.ANY)] * 2
        operands += list(previous)
        aliases = {3: 0, 4: 1}
    out_spec = pl.BlockSpec((rows, step), lambda i, s: (0, base + i))
    return pl.pallas_call(
        functools.partial(combine_kernel, peers, blocks, previous is not None),
        grid_spec=pltpu.PrefetchScalarGridSpec(
            num_scalar_prefetch=1,
            grid=(chunk_width // step,),
            in_specs=in_specs,
            out_specs=[out_spec, out_spec],
            scratch_shapes=[pltpu.VMEM((blocks, 2 * TILE, step), jnp.float32)],
        ),
        out_shape=[jax.ShapeDtypeStruct((rows, width), jnp.bfloat16)] * 2,
        input_output_aliases=aliases,
        cost_estimate=pl.CostEstimate(flops=0, bytes_accessed=12 * 1024 * 1024, transcendentals=0),
        compiler_params=pltpu.CompilerParams(vmem_limit_bytes=VMEM_LIMIT),
        name="combine",
    )(*operands)


def exchange(x):
    return lax.all_to_all(x, "ctx", split_axis=0, concat_axis=0, tiled=True)


def merge_lanes(a, b):
    low = jnp.concatenate([a[:, :HD], b[:, :HD]], axis=1)
    high = jnp.concatenate([a[:, HD:], b[:, HD:]], axis=1)
    return low, high


def pack_kernel(tokens, a_ref, b_ref, *refs):
    out_ref = refs[-1]
    low, high = merge_lanes(a_ref[...], b_ref[...])
    out_ref[0, :tokens, :] = low
    out_ref[1, :tokens, :] = high
    if len(refs) > 1:
        out_ref[0, tokens:, :] = refs[0][...]
        out_ref[1, tokens:, :] = refs[0][...]


def pack_heads(a, b, start, count, extra=None):
    _, width = a.shape
    tokens = count * TILE
    first = start // count
    spec = pl.BlockSpec((tokens, PAIR), lambda i: (first, i))
    in_specs, operands = [spec, spec], [a, b]
    length = tokens
    if extra is not None:
        length += extra.shape[0]
        in_specs.append(pl.BlockSpec(extra.shape, lambda i: (0, 0)))
        operands.append(extra)
    return pl.pallas_call(
        functools.partial(pack_kernel, tokens),
        grid=(width // PAIR,),
        in_specs=in_specs,
        out_specs=pl.BlockSpec((2, length, PAIR), lambda i: (i, 0, 0)),
        out_shape=jax.ShapeDtypeStruct((width // HD, length, PAIR), jnp.bfloat16),
        cost_estimate=pl.CostEstimate(
            flops=0, bytes_accessed=8 * tokens * width, transcendentals=0
        ),
        compiler_params=pltpu.CompilerParams(vmem_limit_bytes=VMEM_LIMIT),
        name="pack_heads",
    )(*operands)


def turn_kernel(kv_ref, out_ref):
    for j in range(kv_ref.shape[0] // TILE):
        out_ref[j] = kv_ref[j * TILE : (j + 1) * TILE, :].T[:HD, :]


def turn_keys(kv):
    total = kv.shape[0] // TILE
    step = 8
    return pl.pallas_call(
        turn_kernel,
        grid=(total // step,),
        in_specs=[pl.BlockSpec((step * TILE, PAIR), lambda i: (i, 0))],
        out_specs=pl.BlockSpec((step, HD, TILE), lambda i: (i, 0, 0)),
        out_shape=jax.ShapeDtypeStruct((total, HD, TILE), jnp.bfloat16),
        compiler_params=pltpu.CompilerParams(vmem_limit_bytes=VMEM_LIMIT),
        name="turn_keys",
    )(kv)


def head_kernel(dims, *refs):
    blocks, picks, start, count, last = dims
    if last:
        table_ref, qg_ref, kv_ref, kt_ref, before_ref, out_ref, acc_ref, sem = refs[:8]
        buffers = refs[8:]
    else:
        table_ref, qg_ref, kv_ref, kt_ref, out_ref, acc_ref = refs[:6]
        buffers = refs[6:]
    raws, pairs = buffers[:DEPTH], buffers[DEPTH:]
    sources = out_ref.shape[0]
    lane = lax.broadcasted_iota(jnp.int32, (TILE, PAIR), 1)
    low = lane < HD
    parts = [slice(j * TILE, (j + 1) * TILE) for j in range(picks + 1)]
    final = sources * count - 1

    def fold(x, op):
        return op(x.reshape(-1, 8, x.shape[-1]), axis=0)

    def load_block(index):
        index = jnp.minimum(index, final)
        source, local = index // count, index % count
        block = source * blocks + start + local
        named = [table_ref[block * picks + j] for j in range(picks)] + [block]
        rows = [pl.ds(pl.multiple_of(n * TILE, TILE), TILE) for n in named]
        local_rows = pl.ds(pl.multiple_of(local * TILE, TILE), TILE)
        qg = qg_ref[source, local_rows, :].astype(jnp.float32)
        zero = jnp.zeros_like(qg)
        both = jnp.concatenate(
            [jnp.where(low, qg * (HD**-0.5), zero), jnp.where(low, zero, qg)], axis=0
        )
        return named, rows, both

    def stage_raw(state, slot):
        _, rows, both = state
        low_both = both.astype(jnp.bfloat16)
        top = None
        for j in range(picks + 1):
            raw = dot_nt(kv_ref[rows[j], :], low_both)
            raws[slot][parts[j]] = raw
            part = fold(raw[:, :TILE], jnp.max)
            top = part if top is None else jnp.maximum(top, part)
            yield
        yield jnp.max(top, axis=0, keepdims=True)

    def stage_exp(top, slot):
        raw_scr, pair_scr = raws[slot], pairs[slot]
        total = jnp.zeros((8, TILE), jnp.float32)
        inner = jnp.zeros((8, TILE), jnp.float32)
        for j in range(picks + 1):
            p = jnp.exp2((raw_scr[parts[j], :TILE] - top) * LOG2E)
            raw_scr[parts[j], :TILE] = p
            pair_scr[parts[j], TILE:] = p.astype(jnp.bfloat16)
            total += fold(p, jnp.sum)
            inner += fold(p * raw_scr[parts[j], TILE:], jnp.sum)
            yield
        recip = 1.0 / jnp.sum(total, axis=0, keepdims=True)
        delta = jnp.sum(inner, axis=0, keepdims=True) * recip
        yield recip, delta

    def stage_grad(state, recip, delta, slot):
        named, rows, both = state
        raw_scr, pair_scr = raws[slot], pairs[slot]
        column = jnp.broadcast_to(recip, (TILE, TILE)).T
        scaled = jnp.concatenate([both[:TILE] * column, both[TILE:] * column], axis=0)
        scaled = scaled.astype(jnp.bfloat16)
        for j in range(picks + 1):
            ds = raw_scr[parts[j], :TILE] * (raw_scr[parts[j], TILE:] - delta)
            pair_scr[parts[j], :TILE] = ds.astype(jnp.bfloat16)
            acc_ref[rows[j], :] += dot_nn(pair_scr[parts[j]], scaled)
            yield
        turned = jnp.concatenate([kt_ref[n] for n in named], axis=1)
        dqt = dot_nn(turned, pair_scr[:, :TILE])
        yield dqt * (recip * (HD**-0.5))

    def together(*stages):
        results = [None] * len(stages)
        live = list(range(len(stages)))
        while live:
            for n in list(live):
                try:
                    value = next(stages[n])
                    if value is not None:
                        results[n] = value
                except StopIteration:
                    live.remove(n)
        return results

    if last:
        fill = pltpu.make_async_copy(before_ref, acc_ref, sem)
        fill.start()
    else:

        def clear(n, carry):
            rows = pl.ds(pl.multiple_of(n * 8 * TILE, TILE), 8 * TILE)
            acc_ref[rows, :] = jnp.zeros((8 * TILE, PAIR), jnp.float32)
            return carry

        lax.fori_loop(0, acc_ref.shape[0] // (8 * TILE), clear, 0)

    (top0,) = together(stage_raw(load_block(0), 0))
    top1, stats0 = together(stage_raw(load_block(1), 1), stage_exp(top0, 0))
    if last:
        fill.wait()
    offset = blocks * TILE if last else 0

    def round_of_blocks(m, carry):
        top, recip, delta = carry
        base = m * DEPTH
        held = None
        for n in range(DEPTH):
            index = base + n
            top, (next_recip, next_delta), dqt = together(
                stage_raw(load_block(index + 2), (n + 2) % DEPTH),
                stage_exp(top, (n + 1) % DEPTH),
                stage_grad(load_block(index), recip, delta, n),
            )
            recip, delta = next_recip, next_delta
            if n % 2 == 0:
                held = dqt
            else:
                both = jnp.concatenate([held, dqt], axis=0).T.astype(jnp.bfloat16)
                source, local = index // count, index % count
                rows = pl.ds(pl.multiple_of(offset + local // 2 * TILE, TILE), TILE)
                out_ref[source, rows, :] = both
        return top, recip, delta

    lax.fori_loop(0, sources * count // DEPTH, round_of_blocks, (top1, *stats0))

    if last:

        def finish(s, carry):
            rows = pl.ds(pl.multiple_of(s * blocks * TILE, TILE), blocks * TILE)
            out_ref[s, : blocks * TILE, :] = acc_ref[rows, :].astype(jnp.bfloat16)
            return carry

        lax.fori_loop(0, sources, finish, 0)


def attend_head(table, qg, kv, turned, before, blocks, start, count):
    peers = qg.shape[0]
    total = kv.shape[0]
    picks = table.shape[0] // (total // TILE)
    last = before is not None
    keys = TILE * (picks + 1)

    def whole(shape):
        return pl.BlockSpec(shape, lambda i, t: (0,) * len(shape))

    in_specs = [whole((peers, count * TILE, PAIR)), whole(kv.shape), whole(turned.shape)]
    operands = [table, qg, kv, turned]
    acc_shape = (total, PAIR)
    buffers = [pltpu.VMEM((keys, 2 * TILE), jnp.float32)] * DEPTH
    buffers += [pltpu.VMEM((keys, 2 * TILE), jnp.bfloat16)] * DEPTH
    if last:
        in_specs.append(pl.BlockSpec(memory_space=pl.ANY))
        operands.append(before)
        packed = (peers, (blocks + count // 2) * TILE, PAIR)
        out_specs = whole(packed)
        out_shape = jax.ShapeDtypeStruct(packed, jnp.bfloat16)
        buffers = [pltpu.VMEM(acc_shape, jnp.float32), pltpu.SemaphoreType.DMA] + buffers
    else:
        dq_shape = (peers, count // 2 * TILE, PAIR)
        out_specs = [whole(dq_shape), whole(acc_shape)]
        out_shape = [
            jax.ShapeDtypeStruct(dq_shape, jnp.bfloat16),
            jax.ShapeDtypeStruct(acc_shape, jnp.float32),
        ]
    return pl.pallas_call(
        functools.partial(head_kernel, (blocks, picks, start, count, last)),
        grid_spec=pltpu.PrefetchScalarGridSpec(
            num_scalar_prefetch=1,
            grid=(1,),
            in_specs=in_specs,
            out_specs=out_specs,
            scratch_shapes=buffers,
        ),
        out_shape=out_shape,
        cost_estimate=pl.CostEstimate(
            flops=5 * 2 * TILE * PAIR * keys * peers * count,
            bytes_accessed=24 * 1024 * 1024,
            transcendentals=peers * count * keys * TILE,
        ),
        compiler_params=pltpu.CompilerParams(vmem_limit_bytes=VMEM_LIMIT),
        name="attend_head",
    )(*operands)


def unpack_kernel(blocks, start, count, last, in_ref, *refs):
    refs = refs[-3:] if last else refs[-1:]
    gq_ref = refs[0]
    offset = 0
    if last:
        offset = blocks * TILE
        refs[1][...], refs[2][...] = merge_lanes(in_ref[0, :offset, :], in_ref[1, :offset, :])
    for m in range(count // 2):
        rows = slice(offset + m * TILE, offset + (m + 1) * TILE)
        even, odd = merge_lanes(in_ref[0, rows, :], in_ref[1, rows, :])
        gq_ref[2 * m * TILE : (2 * m + 1) * TILE, :] = even
        gq_ref[(2 * m + 1) * TILE : (2 * m + 2) * TILE, :] = odd


def unpack_heads(back, previous, blocks, start, count):
    heads, tokens, _ = back.shape
    width = heads * HD
    last = previous is not None
    rows = blocks * TILE
    first = start // count
    in_specs = [pl.BlockSpec((2, tokens, PAIR), lambda i: (i, 0, 0))]
    operands = [back]
    out_specs = [pl.BlockSpec((count * TILE, PAIR), lambda i: (first, i))]
    out_shape = [jax.ShapeDtypeStruct((rows, width), jnp.bfloat16)]
    aliases = {}
    if last:
        in_specs.append(pl.BlockSpec(memory_space=pl.ANY))
        operands.append(previous)
        aliases = {1: 0}
        out_specs += [pl.BlockSpec((rows, PAIR), lambda i: (0, i))] * 2
        out_shape += [out_shape[0]] * 2
    return pl.pallas_call(
        functools.partial(unpack_kernel, blocks, start, count, last),
        grid=(heads // 2,),
        in_specs=in_specs,
        out_specs=out_specs,
        out_shape=out_shape,
        input_output_aliases=aliases,
        cost_estimate=pl.CostEstimate(
            flops=0, bytes_accessed=4 * heads * tokens * PAIR, transcendentals=0
        ),
        compiler_params=pltpu.CompilerParams(vmem_limit_bytes=VMEM_LIMIT),
        name="unpack_heads",
    )(*operands)


def by_heads(queries, key_rows, value_rows, grad_out, tile_keys):
    rows, _ = queries.shape
    blocks, picks = tile_keys.shape
    half = blocks // 2
    tokens = half * TILE
    extra = jnp.pad(tile_keys.astype(jnp.bfloat16), ((0, 16 - blocks), (0, PAIR - picks)))
    kv = pack_heads(key_rows, value_rows, 0, blocks)
    qg0 = pack_heads(queries, grad_out, 0, half, extra)
    qg1 = pack_heads(queries, grad_out, half, half)
    kv = exchange(kv)
    kv, qg0 = lax.optimization_barrier((kv, qg0))
    qg0 = exchange(qg0)
    kv = kv.reshape(-1, PAIR)
    turned = turn_keys(kv)
    qg0, qg1, turned = lax.optimization_barrier((qg0, qg1, turned))
    qg1 = exchange(qg1)
    table = qg0[:, tokens : tokens + blocks, :picks].astype(jnp.int32).reshape(-1)
    dq, before = attend_head(table, qg0, kv, turned, None, blocks, 0, half)
    back = exchange(dq)
    packed = attend_head(table, qg1, kv, turned, before, blocks, half, half)
    final = exchange(packed)
    grad_queries = unpack_heads(back, None, blocks, 0, half)[0]
    return unpack_heads(final, grad_queries, blocks, half, half)


def by_blocks(queries, key_rows, value_rows, grad_out, tile_keys):
    rows, width = queries.shape
    blocks = rows // TILE
    peers = lax.axis_size("ctx")
    peer_range = jnp.arange(peers, dtype=jnp.int32)
    owners = tile_keys // blocks
    local_ids = tile_keys % blocks
    matches = owners[:, :, None] == peer_range[None, None, :]
    wanted = jnp.max(jnp.where(matches, local_ids[:, :, None], -1), axis=(0, 1))
    requested = exchange(wanted)
    slots = owners.reshape(-1)
    chunk_width = width // CHUNKS

    received = [
        exchange(gather_blocks(requested, key_rows, value_rows, c, chunk_width)) for c in range(CHUNKS)
    ]
    grad_queries = None
    owns, backs = [], []
    for c in range(CHUNKS):
        grad_queries, own, out = attend(
            slots, queries, grad_out, key_rows, value_rows, received[c], grad_queries, c
        )
        owns.append(own)
        backs.append(exchange(out))
    result = None
    for c in range(CHUNKS):
        result = combine(requested, owns[c], backs[c], result, c, width)
    return grad_queries, result[0], result[1]


def on_device(queries, key_rows, value_rows, grad_out, tile_keys):
    peers = lax.axis_size("ctx")
    blocks = tile_keys.shape[0]
    one_head_each = peers * HD == queries.shape[1]
    fits = one_head_each and blocks % 4 == 0 and blocks <= 16 and peers * blocks <= 256
    plan = by_heads if fits else by_blocks
    return tuple(plan(queries, key_rows, value_rows, grad_out, tile_keys))


def solution(mesh):
    spec = P(("groups", "ctx"), None)
    return jax.shard_map(
        on_device, mesh=mesh, in_specs=(spec,) * 5, out_specs=(spec,) * 3, check_vma=False
    )
```

```python
import functools

import jax
import jax.numpy as jnp
from jax import lax
from jax.experimental import pallas as pl
from jax.experimental.pallas import tpu as pltpu
from jax.sharding import PartitionSpec as P

HD = 64
TILE = 128
PAIR = 2 * HD
LOG2E = 1.4426950408889634
CHUNKS = 2
DEPTH = 4
PHASES = 2
VMEM_LIMIT = 60 * 1024 * 1024


def dot_nt(a, b):
    return lax.dot_general(a, b, (((1,), (1,)), ((), ())), preferred_element_type=jnp.float32)


def dot_nn(a, b):
    return lax.dot_general(a, b, (((1,), (0,)), ((), ())), preferred_element_type=jnp.float32)


def gather_kernel(peers, ids_ref, k_ref, v_ref, out_ref, sems):
    def copies(p):
        rows = pl.ds(pl.multiple_of(jnp.maximum(ids_ref[p], 0) * TILE, TILE), TILE)
        return (
            pltpu.make_async_copy(k_ref.at[rows], out_ref.at[p, pl.ds(0, TILE)], sems.at[0, p]),
            pltpu.make_async_copy(v_ref.at[rows], out_ref.at[p, pl.ds(TILE, TILE)], sems.at[1, p]),
        )

    for p in range(peers):
        for copy in copies(p):
            copy.start()
    for p in range(peers):
        for copy in copies(p):
            copy.wait()


def gather_blocks(ids, key_rows, value_rows, chunk, chunk_width):
    peers = ids.shape[0]
    rows_spec = pl.BlockSpec((key_rows.shape[0], chunk_width), lambda i, s: (0, chunk))
    return pl.pallas_call(
        functools.partial(gather_kernel, peers),
        grid_spec=pltpu.PrefetchScalarGridSpec(
            num_scalar_prefetch=1,
            grid=(1,),
            in_specs=[rows_spec, rows_spec],
            out_specs=pl.BlockSpec(memory_space=pl.ANY),
            scratch_shapes=[pltpu.SemaphoreType.DMA((2, peers))],
        ),
        out_shape=jax.ShapeDtypeStruct((peers, 2 * TILE, chunk_width), jnp.bfloat16),
        compiler_params=pltpu.CompilerParams(vmem_limit_bytes=VMEM_LIMIT),
        name="gather_blocks",
    )(ids, key_rows, value_rows)


def attend_kernel(peers, blocks, picks, aliased, slots_ref, q_ref, g_ref, k_ref, v_ref, recv_ref, *rest):
    if aliased:
        rest = rest[1:]
    dq_ref, own_ref, out_ref, s_scr, w_scr, p_scr, kt_scr, acc_scr = rest
    lane = lax.broadcasted_iota(jnp.int32, (TILE, PAIR), 1)
    first = lane < HD

    def prepare(p, carry):
        kt_scr[p] = recv_ref[p, :TILE, :].T
        acc_scr[p] = jnp.zeros((2 * TILE, PAIR), jnp.float32)
        return carry

    lax.fori_loop(0, peers, prepare, 0)

    def split(x):
        zero = jnp.zeros_like(x)
        return jnp.concatenate([jnp.where(first, x, zero), jnp.where(first, zero, x)], axis=0)

    def one_block(b, carry):
        rows = pl.ds(pl.multiple_of(b * TILE, TILE), TILE)
        q2f = split(q_ref[rows, :].astype(jnp.float32) * (HD**-0.5))
        g2f = split(g_ref[rows, :].astype(jnp.float32))
        q2 = q2f.astype(jnp.bfloat16)
        g2 = g2f.astype(jnp.bfloat16)
        slots = [slots_ref[b * picks + j] for j in range(picks)]

        def fold(x, op):
            x = x.reshape(TILE // 8, 8, 2 * TILE)
            return op(x, axis=0)

        top = None
        for j in range(picks + 1):
            if j < picks:
                kb, vb = recv_ref[slots[j], :TILE, :], recv_ref[slots[j], TILE:, :]
            else:
                kb, vb = k_ref[rows, :], v_ref[rows, :]
            s = dot_nt(kb, q2)
            s_scr[j] = s
            w_scr[j] = dot_nt(vb, g2)
            part = fold(s, jnp.max)
            top = part if top is None else jnp.maximum(top, part)
        top = jnp.max(top, axis=0, keepdims=True)
        total = jnp.zeros((8, 2 * TILE), jnp.float32)
        inner = jnp.zeros((8, 2 * TILE), jnp.float32)
        for j in range(picks + 1):
            p = jnp.exp2((s_scr[j] - top) * LOG2E)
            s_scr[j] = p
            p_scr[j] = p.astype(jnp.bfloat16)
            total += fold(p, jnp.sum)
            inner += fold(p * w_scr[j], jnp.sum)
        recip = 1.0 / jnp.sum(total, axis=0, keepdims=True)
        delta = jnp.sum(inner, axis=0, keepdims=True) * recip
        column = jnp.broadcast_to(recip, (PAIR, 2 * TILE)).T
        rq = (q2f * column).astype(jnp.bfloat16)
        rg = (g2f * column).astype(jnp.bfloat16)
        dqt = jnp.zeros((PAIR, 2 * TILE), jnp.float32)
        for j in range(picks + 1):
            ds = (s_scr[j] * (w_scr[j] - delta)).astype(jnp.bfloat16)
            dk = dot_nn(ds, rq)
            dv = dot_nn(p_scr[j], rg)
            if j < picks:
                acc_scr[slots[j], :TILE, :] += dk
                acc_scr[slots[j], TILE:, :] += dv
                kt = kt_scr[slots[j]]
            else:
                own_ref[0, rows, :] = dk
                own_ref[1, rows, :] = dv
                kt = k_ref[rows, :].T
            dqt += dot_nn(kt, ds)
        dqt = dqt * (recip * (HD**-0.5))
        dqt = jnp.concatenate([dqt[:HD, :TILE], dqt[HD:, TILE:]], axis=0)
        dq_ref[rows, :] = dqt.T.astype(jnp.bfloat16)
        return carry

    lax.fori_loop(0, blocks, one_block, 0)

    def finish(p, carry):
        out_ref[p] = acc_scr[p].astype(jnp.bfloat16)
        return carry

    lax.fori_loop(0, peers, finish, 0)


def attend(slots, queries, grad_out, key_rows, value_rows, received, previous, chunk):
    peers, _, chunk_width = received.shape
    rows, width = queries.shape
    blocks = rows // TILE
    picks = slots.shape[0] // blocks
    pairs = chunk_width // PAIR
    base = chunk * pairs
    rows_spec = pl.BlockSpec((rows, PAIR), lambda i, s: (0, base + i))
    pack_spec = pl.BlockSpec((peers, 2 * TILE, PAIR), lambda i, s: (0, 0, i))
    in_specs = [rows_spec] * 4 + [pack_spec]
    operands = [slots, queries, grad_out, key_rows, value_rows, received]
    aliases = {}
    if previous is not None:
        in_specs.append(pl.BlockSpec(memory_space=pl.ANY))
        operands.append(previous)
        aliases = {6: 0}
    keys = TILE * (picks + 1)
    flops = 5 * 2 * 2 * TILE * PAIR * keys * blocks * pairs
    return pl.pallas_call(
        functools.partial(attend_kernel, peers, blocks, picks, previous is not None),
        grid_spec=pltpu.PrefetchScalarGridSpec(
            num_scalar_prefetch=1,
            grid=(pairs,),
            in_specs=in_specs,
            out_specs=[
                rows_spec,
                pl.BlockSpec((2, rows, PAIR), lambda i, s: (0, 0, i)),
                pack_spec,
            ],
            scratch_shapes=[
                pltpu.VMEM((picks + 1, TILE, 2 * TILE), jnp.float32),
                pltpu.VMEM((picks + 1, TILE, 2 * TILE), jnp.float32),
                pltpu.VMEM((picks + 1, TILE, 2 * TILE), jnp.bfloat16),
                pltpu.VMEM((peers, PAIR, TILE), jnp.bfloat16),
                pltpu.VMEM((peers, 2 * TILE, PAIR), jnp.float32),
            ],
        ),
        out_shape=[
            jax.ShapeDtypeStruct((rows, width), jnp.bfloat16),
            jax.ShapeDtypeStruct((2, rows, chunk_width), jnp.float32),
            jax.ShapeDtypeStruct(received.shape, jnp.bfloat16),
        ],
        input_output_aliases=aliases,
        cost_estimate=pl.CostEstimate(
            flops=flops,
            bytes_accessed=24 * 1024 * 1024,
            transcendentals=blocks * pairs * keys * 2 * TILE,
        ),
        compiler_params=pltpu.CompilerParams(vmem_limit_bytes=VMEM_LIMIT),
        name="attend",
    )(*operands)


def combine_kernel(peers, blocks, aliased, ids_ref, own_ref, back_ref, *rest):
    if aliased:
        rest = rest[2:]
    gk_ref, gv_ref, acc = rest
    for b in range(blocks):
        acc[b, :TILE, :] = own_ref[0, b * TILE : (b + 1) * TILE, :]
        acc[b, TILE:, :] = own_ref[1, b * TILE : (b + 1) * TILE, :]

    def add(p, carry):
        target = ids_ref[p]

        @pl.when(target >= 0)
        def _():
            acc[jnp.maximum(target, 0)] += back_ref[p].astype(jnp.float32)

        return carry

    lax.fori_loop(0, peers, add, 0)
    for b in range(blocks):
        gk_ref[b * TILE : (b + 1) * TILE, :] = acc[b, :TILE, :].astype(jnp.bfloat16)
        gv_ref[b * TILE : (b + 1) * TILE, :] = acc[b, TILE:, :].astype(jnp.bfloat16)


def combine(requested, own, returned, previous, chunk, width):
    peers, _, chunk_width = returned.shape
    rows = own.shape[1]
    blocks = rows // TILE
    step = PAIR
    base = chunk * (chunk_width // step)
    in_specs = [
        pl.BlockSpec((2, rows, step), lambda i, s: (0, 0, i)),
        pl.BlockSpec((peers, 2 * TILE, step), lambda i, s: (0, 0, i)),
    ]
    operands = [requested, own, returned]
    aliases = {}
    if previous is not None:
        in_specs += [pl.BlockSpec(memory_space=pl.ANY)] * 2
        operands += list(previous)
        aliases = {3: 0, 4: 1}
    out_spec = pl.BlockSpec((rows, step), lambda i, s: (0, base + i))
    return pl.pallas_call(
        functools.partial(combine_kernel, peers, blocks, previous is not None),
        grid_spec=pltpu.PrefetchScalarGridSpec(
            num_scalar_prefetch=1,
            grid=(chunk_width // step,),
            in_specs=in_specs,
            out_specs=[out_spec, out_spec],
            scratch_shapes=[pltpu.VMEM((blocks, 2 * TILE, step), jnp.float32)],
        ),
        out_shape=[jax.ShapeDtypeStruct((rows, width), jnp.bfloat16)] * 2,
        input_output_aliases=aliases,
        cost_estimate=pl.CostEstimate(flops=0, bytes_accessed=12 * 1024 * 1024, transcendentals=0),
        compiler_params=pltpu.CompilerParams(vmem_limit_bytes=VMEM_LIMIT),
        name="combine",
    )(*operands)


def exchange(x):
    return lax.all_to_all(x, "ctx", split_axis=0, concat_axis=0, tiled=True)


def merge_lanes(a, b):
    low = jnp.concatenate([a[:, :HD], b[:, :HD]], axis=1)
    high = jnp.concatenate([a[:, HD:], b[:, HD:]], axis=1)
    return low, high


def pack_kernel(tokens, k_ref, v_ref, q_ref, g_ref, *refs):
    out_ref = refs[-1]
    kv = merge_lanes(k_ref[...], v_ref[...])
    qg = merge_lanes(q_ref[...], g_ref[...])
    for head in range(2):
        for core in range(2):
            part = slice(core * tokens, (core + 1) * tokens)
            out_ref[2 * head + core, :tokens, :] = kv[head][part]
            out_ref[2 * head + core, tokens : 2 * tokens, :] = qg[head][part]
            if len(refs) > 1:
                out_ref[2 * head + core, 2 * tokens :, :] = refs[0][core]


def pack_phase(key_rows, value_rows, queries, grad_out, phase, extra=None):
    rows, width = queries.shape
    slabs = width // PAIR // PHASES
    spec = pl.BlockSpec((rows, PAIR), lambda j: (0, phase * slabs + j))
    in_specs, operands = [spec] * 4, [key_rows, value_rows, queries, grad_out]
    length = rows
    if extra is not None:
        length += extra.shape[1]
        in_specs.append(pl.BlockSpec(extra.shape, lambda j: (0, 0, 0)))
        operands.append(extra)
    return pl.pallas_call(
        functools.partial(pack_kernel, rows // 2),
        grid=(slabs,),
        in_specs=in_specs,
        out_specs=pl.BlockSpec((4, length, PAIR), lambda j: (j, 0, 0)),
        out_shape=jax.ShapeDtypeStruct((4 * slabs, length, PAIR), jnp.bfloat16),
        cost_estimate=pl.CostEstimate(
            flops=0, bytes_accessed=8 * rows * width, transcendentals=0
        ),
        compiler_params=pltpu.CompilerParams(vmem_limit_bytes=VMEM_LIMIT),
        name="pack_phase",
    )(*operands)


def head_kernel(picks, table_ref, qg_ref, mine_ref, other_ref, out_ref, sum_ref, give_ref, *scratch):
    kv_scr, kt_scr, acc_ref, sems = scratch[:4]
    raws, pairs = scratch[4 : 4 + DEPTH], scratch[4 + DEPTH :]
    sources, tokens, _ = qg_ref.shape
    half = tokens // TILE
    lane = lax.broadcasted_iota(jnp.int32, (TILE, PAIR), 1)
    low = lane < HD
    parts = [slice(j * TILE, (j + 1) * TILE) for j in range(picks + 1)]
    final = sources * half - 1

    loads = [
        pltpu.make_async_copy(
            mine_ref.at[:, pl.ds(0, tokens)], kv_scr.at[pl.ds(0, sources)], sems.at[0]
        ),
        pltpu.make_async_copy(other_ref, kv_scr.at[pl.ds(sources, sources)], sems.at[1]),
    ]
    for load in loads:
        load.start()

    def clear(n, carry):
        rows = pl.ds(pl.multiple_of(n * tokens, tokens), tokens)
        acc_ref[rows, :] = jnp.zeros((tokens, PAIR), jnp.float32)
        return carry

    lax.fori_loop(0, 2 * sources, clear, 0)
    for load in loads:
        load.wait()

    def turn(n, carry):
        for j in range(half):
            kt_scr[n * half + j] = kv_scr[n, j * TILE : (j + 1) * TILE, :].T[:HD, :]
        return carry

    lax.fori_loop(0, 2 * sources, turn, 0)

    def tile_rows(n):
        return pl.ds(pl.multiple_of(n * TILE, TILE), TILE)

    def fold(x, op):
        return op(x.reshape(-1, 8, x.shape[-1]), axis=0)

    def load_block(index):
        block = jnp.minimum(index, final)
        named = [table_ref[block * picks + j] for j in range(picks)] + [block]
        rows = [tile_rows(n) for n in named]
        qg = qg_ref[block // half, tile_rows(block % half), :].astype(jnp.float32)
        zero = jnp.zeros_like(qg)
        both = jnp.concatenate(
            [jnp.where(low, qg * (HD**-0.5), zero), jnp.where(low, zero, qg)], axis=0
        )
        return named, rows, both

    def stage_raw(state, slot):
        named, _, both = state
        low_both = both.astype(jnp.bfloat16)
        top = None
        for j in range(picks + 1):
            n = named[j]
            raw = dot_nt(kv_scr[n // half, tile_rows(n % half), :], low_both)
            raws[slot][parts[j]] = raw
            part = fold(raw[:, :TILE], jnp.max)
            top = part if top is None else jnp.maximum(top, part)
            yield
        yield jnp.max(top, axis=0, keepdims=True)

    def stage_exp(top, slot):
        raw_scr, pair_scr = raws[slot], pairs[slot]
        total = jnp.zeros((8, TILE), jnp.float32)
        inner = jnp.zeros((8, TILE), jnp.float32)
        for j in range(picks + 1):
            p = jnp.exp2((raw_scr[parts[j], :TILE] - top) * LOG2E)
            raw_scr[parts[j], :TILE] = p
            pair_scr[parts[j], TILE:] = p.astype(jnp.bfloat16)
            total += fold(p, jnp.sum)
            inner += fold(p * raw_scr[parts[j], TILE:], jnp.sum)
            yield
        recip = 1.0 / jnp.sum(total, axis=0, keepdims=True)
        delta = jnp.sum(inner, axis=0, keepdims=True) * recip
        yield recip, delta

    def stage_grad(state, recip, delta, slot):
        named, rows, both = state
        raw_scr, pair_scr = raws[slot], pairs[slot]
        column = jnp.broadcast_to(recip, (TILE, TILE)).T
        scaled = jnp.concatenate([both[:TILE] * column, both[TILE:] * column], axis=0)
        scaled = scaled.astype(jnp.bfloat16)
        for j in range(picks + 1):
            ds = raw_scr[parts[j], :TILE] * (raw_scr[parts[j], TILE:] - delta)
            pair_scr[parts[j], :TILE] = ds.astype(jnp.bfloat16)
            acc_ref[rows[j], :] += dot_nn(pair_scr[parts[j]], scaled)
            yield
        turned = jnp.concatenate([kt_scr[n] for n in named], axis=1)
        dqt = dot_nn(turned, pair_scr[:, :TILE])
        yield dqt * (recip * (HD**-0.5))

    def together(*stages):
        results = [None] * len(stages)
        live = list(range(len(stages)))
        while live:
            for n in list(live):
                try:
                    value = next(stages[n])
                    if value is not None:
                        results[n] = value
                except StopIteration:
                    live.remove(n)
        return results

    (top0,) = together(stage_raw(load_block(0), 0))
    top1, stats0 = together(stage_raw(load_block(1), 1), stage_exp(top0, 0))

    def round_of_blocks(m, carry):
        top, recip, delta = carry
        held = None
        for n in range(DEPTH):
            index = m * DEPTH + n
            top, (next_recip, next_delta), dqt = together(
                stage_raw(load_block(index + 2), (n + 2) % DEPTH),
                stage_exp(top, (n + 1) % DEPTH),
                stage_grad(load_block(index), recip, delta, n),
            )
            recip, delta = next_recip, next_delta
            if n % 2 == 0:
                held = dqt
            else:
                both = jnp.concatenate([held, dqt], axis=0).T.astype(jnp.bfloat16)
                out_ref[index // half, tile_rows(index % half // 2), :] = both
        return top, recip, delta

    lax.fori_loop(0, sources * half // DEPTH, round_of_blocks, (top1, *stats0))

    store = pltpu.make_async_copy(acc_ref.at[pl.ds(0, sources * tokens)], sum_ref, sems.at[2])
    store.start()

    def finish(s, carry):
        rows = pl.ds(pl.multiple_of((sources + s) * tokens, tokens), tokens)
        give_ref[s] = acc_ref[rows, :].astype(jnp.bfloat16)
        return carry

    lax.fori_loop(0, sources, finish, 0)
    store.wait()


def attend_head(table, received, other):
    peers, tokens, _ = other.shape
    half = tokens // TILE
    total = 2 * peers * tokens
    picks = table.shape[0] // (peers * half)
    keys = TILE * (picks + 1)
    any_spec = pl.BlockSpec(memory_space=pl.ANY)
    scratch = [
        pltpu.VMEM((2 * peers, tokens, PAIR), jnp.bfloat16),
        pltpu.VMEM((2 * peers * half, HD, TILE), jnp.bfloat16),
        pltpu.VMEM((total, PAIR), jnp.float32),
        pltpu.SemaphoreType.DMA((3,)),
    ]
    scratch += [pltpu.VMEM((keys, 2 * TILE), jnp.float32)] * DEPTH
    scratch += [pltpu.VMEM((keys, 2 * TILE), jnp.bfloat16)] * DEPTH
    return pl.pallas_call(
        functools.partial(head_kernel, picks),
        grid_spec=pltpu.PrefetchScalarGridSpec(
            num_scalar_prefetch=1,
            grid=(1,),
            in_specs=[
                pl.BlockSpec((peers, tokens, PAIR), lambda i, t: (0, 1, 0)),
                any_spec,
                any_spec,
            ],
            out_specs=[
                pl.BlockSpec((peers, tokens // 2, PAIR), lambda i, t: (0, 2, 0)),
                any_spec,
                pl.BlockSpec((peers, tokens, PAIR), lambda i, t: (0, 0, 0)),
            ],
            scratch_shapes=scratch,
        ),
        out_shape=[
            jax.ShapeDtypeStruct((peers, 3 * tokens // 2, PAIR), jnp.bfloat16),
            jax.ShapeDtypeStruct((peers * tokens, PAIR), jnp.float32),
            jax.ShapeDtypeStruct((peers, tokens, PAIR), jnp.bfloat16),
        ],
        cost_estimate=pl.CostEstimate(
            flops=5 * 2 * TILE * PAIR * keys * peers * half,
            bytes_accessed=24 * 1024 * 1024,
            transcendentals=peers * half * keys * TILE,
        ),
        compiler_params=pltpu.CompilerParams(vmem_limit_bytes=VMEM_LIMIT),
        name="attend_head",
    )(table, received, received, other)


def merge_kernel(sum_ref, given_ref, before_ref, out_ref):
    out_ref[...] = (sum_ref[...] + given_ref[...].astype(jnp.float32)).astype(jnp.bfloat16)


def merge_sums(sums, given, payload):
    peers, tokens, _ = given.shape
    step = 4
    spec = pl.BlockSpec((step, tokens, PAIR), lambda i: (i, 0, 0))
    return pl.pallas_call(
        merge_kernel,
        grid=(peers // step,),
        in_specs=[spec, spec, pl.BlockSpec(memory_space=pl.ANY)],
        out_specs=spec,
        out_shape=jax.ShapeDtypeStruct(payload.shape, jnp.bfloat16),
        input_output_aliases={2: 0},
        cost_estimate=pl.CostEstimate(
            flops=0, bytes_accessed=8 * peers * tokens * PAIR, transcendentals=0
        ),
        compiler_params=pltpu.CompilerParams(vmem_limit_bytes=VMEM_LIMIT),
        name="merge_sums",
    )(sums.reshape(given.shape), given, payload)


def unpack_kernel(tokens, in_ref, *refs):
    gq_ref, gk_ref, gv_ref = refs[-3:]
    for core in range(2):
        part = slice(core * tokens, (core + 1) * tokens)
        gk_ref[part, :], gv_ref[part, :] = merge_lanes(
            in_ref[core, :tokens, :], in_ref[2 + core, :tokens, :]
        )
        for m in range(tokens // TILE // 2):
            rows = slice(tokens + m * TILE, tokens + (m + 1) * TILE)
            even, odd = merge_lanes(in_ref[core, rows, :], in_ref[2 + core, rows, :])
            base = core * tokens + 2 * m * TILE
            gq_ref[base : base + TILE, :] = even
            gq_ref[base + TILE : base + 2 * TILE, :] = odd


def unpack_phase(back, previous, phase, rows, width):
    slabs = width // PAIR // PHASES
    in_specs = [pl.BlockSpec((4, back.shape[1], PAIR), lambda j: (j, 0, 0))]
    operands = [back]
    aliases = {}
    if previous is not None:
        in_specs += [pl.BlockSpec(memory_space=pl.ANY)] * 3
        operands += list(previous)
        aliases = {1: 0, 2: 1, 3: 2}
    return pl.pallas_call(
        functools.partial(unpack_kernel, rows // 2),
        grid=(slabs,),
        in_specs=in_specs,
        out_specs=[pl.BlockSpec((rows, PAIR), lambda j: (0, phase * slabs + j))] * 3,
        out_shape=[jax.ShapeDtypeStruct((rows, width), jnp.bfloat16)] * 3,
        input_output_aliases=aliases,
        cost_estimate=pl.CostEstimate(
            flops=0, bytes_accessed=6 * rows * width, transcendentals=0
        ),
        compiler_params=pltpu.CompilerParams(vmem_limit_bytes=VMEM_LIMIT),
        name="unpack_phase",
    )(*operands)


def by_heads(queries, key_rows, value_rows, grad_out, tile_keys):
    rows, width = queries.shape
    blocks, picks = tile_keys.shape
    peers = lax.axis_size("ctx")
    half = blocks // 2
    tokens = half * TILE
    core = lax.axis_index("ctx") % 2

    def swap(x):
        return lax.ppermute(x, "ctx", [(i, i ^ 1) for i in range(peers)])

    extra = tile_keys.astype(jnp.bfloat16).reshape(2, half, picks)
    extra = jnp.pad(extra, ((0, 0), (0, 16 - half), (0, PAIR - picks)))
    received = [
        exchange(
            pack_phase(key_rows, value_rows, queries, grad_out, p, extra if p == 0 else None)
        )
        for p in range(PHASES)
    ]
    table = received[0][:, 2 * tokens : 2 * tokens + half, :picks].astype(jnp.int32)
    local = table % blocks
    side = (local // half + core) % 2
    table = (side * (peers * half) + table // blocks * half + local % half).reshape(-1)
    backs = []
    for p in range(PHASES):
        payload, sums, give = attend_head(table, received[p], swap(received[p][:, :tokens]))
        backs.append(exchange(merge_sums(sums, swap(give), payload)))
    result = None
    for p in range(PHASES):
        result = unpack_phase(backs[p], result, p, rows, width)
    return result


def by_blocks(queries, key_rows, value_rows, grad_out, tile_keys):
    rows, width = queries.shape
    blocks = rows // TILE
    peers = lax.axis_size("ctx")
    peer_range = jnp.arange(peers, dtype=jnp.int32)
    owners = tile_keys // blocks
    local_ids = tile_keys % blocks
    matches = owners[:, :, None] == peer_range[None, None, :]
    wanted = jnp.max(jnp.where(matches, local_ids[:, :, None], -1), axis=(0, 1))
    requested = exchange(wanted)
    slots = owners.reshape(-1)
    chunk_width = width // CHUNKS

    received = [
        exchange(gather_blocks(requested, key_rows, value_rows, c, chunk_width)) for c in range(CHUNKS)
    ]
    grad_queries = None
    owns, backs = [], []
    for c in range(CHUNKS):
        grad_queries, own, out = attend(
            slots, queries, grad_out, key_rows, value_rows, received[c], grad_queries, c
        )
        owns.append(own)
        backs.append(exchange(out))
    result = None
    for c in range(CHUNKS):
        result = combine(requested, owns[c], backs[c], result, c, width)
    return grad_queries, result[0], result[1]


def on_device(queries, key_rows, value_rows, grad_out, tile_keys):
    peers = lax.axis_size("ctx")
    blocks = tile_keys.shape[0]
    one_head_each = peers * HD == queries.shape[1]
    even = peers % 4 == 0 and blocks % 4 == 0 and blocks <= 32
    fits = one_head_each and even and peers * blocks <= 256
    plan = by_heads if fits else by_blocks
    return tuple(plan(queries, key_rows, value_rows, grad_out, tile_keys))


def solution(mesh):
    spec = P(("groups", "ctx"), None)
    return jax.shard_map(
        on_device, mesh=mesh, in_specs=(spec,) * 5, out_specs=(spec,) * 3, check_vma=False
    )
```

```python
import functools

import jax
import jax.numpy as jnp
from jax import lax
from jax.experimental import pallas as pl
from jax.experimental.pallas import tpu as pltpu
from jax.sharding import PartitionSpec as P

HD = 64
TILE = 128
PAIR = 2 * HD
LOG2E = 1.4426950408889634
CHUNKS = 2
DEPTH = 4
PHASES = 2
EXTRA = 16
SMALL_LIMIT = 16 * 1024 * 1024
VMEM_LIMIT = 60 * 1024 * 1024


def dot_nt(a, b):
    return lax.dot_general(a, b, (((1,), (1,)), ((), ())), preferred_element_type=jnp.float32)


def dot_nn(a, b):
    return lax.dot_general(a, b, (((1,), (0,)), ((), ())), preferred_element_type=jnp.float32)


def gather_kernel(peers, ids_ref, k_ref, v_ref, out_ref, sems):
    def copies(p):
        rows = pl.ds(pl.multiple_of(jnp.maximum(ids_ref[p], 0) * TILE, TILE), TILE)
        return (
            pltpu.make_async_copy(k_ref.at[rows], out_ref.at[p, pl.ds(0, TILE)], sems.at[0, p]),
            pltpu.make_async_copy(v_ref.at[rows], out_ref.at[p, pl.ds(TILE, TILE)], sems.at[1, p]),
        )

    for p in range(peers):
        for copy in copies(p):
            copy.start()
    for p in range(peers):
        for copy in copies(p):
            copy.wait()


def gather_blocks(ids, key_rows, value_rows, chunk, chunk_width):
    peers = ids.shape[0]
    rows_spec = pl.BlockSpec((key_rows.shape[0], chunk_width), lambda i, s: (0, chunk))
    return pl.pallas_call(
        functools.partial(gather_kernel, peers),
        grid_spec=pltpu.PrefetchScalarGridSpec(
            num_scalar_prefetch=1,
            grid=(1,),
            in_specs=[rows_spec, rows_spec],
            out_specs=pl.BlockSpec(memory_space=pl.ANY),
            scratch_shapes=[pltpu.SemaphoreType.DMA((2, peers))],
        ),
        out_shape=jax.ShapeDtypeStruct((peers, 2 * TILE, chunk_width), jnp.bfloat16),
        compiler_params=pltpu.CompilerParams(vmem_limit_bytes=VMEM_LIMIT),
        name="gather_blocks",
    )(ids, key_rows, value_rows)


def attend_kernel(peers, blocks, picks, aliased, slots_ref, q_ref, g_ref, k_ref, v_ref, recv_ref, *rest):
    if aliased:
        rest = rest[1:]
    dq_ref, own_ref, out_ref, s_scr, w_scr, p_scr, kt_scr, acc_scr = rest
    lane = lax.broadcasted_iota(jnp.int32, (TILE, PAIR), 1)
    first = lane < HD

    def prepare(p, carry):
        kt_scr[p] = recv_ref[p, :TILE, :].T
        acc_scr[p] = jnp.zeros((2 * TILE, PAIR), jnp.float32)
        return carry

    lax.fori_loop(0, peers, prepare, 0)

    def split(x):
        zero = jnp.zeros_like(x)
        return jnp.concatenate([jnp.where(first, x, zero), jnp.where(first, zero, x)], axis=0)

    def one_block(b, carry):
        rows = pl.ds(pl.multiple_of(b * TILE, TILE), TILE)
        q2f = split(q_ref[rows, :].astype(jnp.float32) * (HD**-0.5))
        g2f = split(g_ref[rows, :].astype(jnp.float32))
        q2 = q2f.astype(jnp.bfloat16)
        g2 = g2f.astype(jnp.bfloat16)
        slots = [slots_ref[b * picks + j] for j in range(picks)]

        def fold(x, op):
            x = x.reshape(TILE // 8, 8, 2 * TILE)
            return op(x, axis=0)

        top = None
        for j in range(picks + 1):
            if j < picks:
                kb, vb = recv_ref[slots[j], :TILE, :], recv_ref[slots[j], TILE:, :]
            else:
                kb, vb = k_ref[rows, :], v_ref[rows, :]
            s = dot_nt(kb, q2)
            s_scr[j] = s
            w_scr[j] = dot_nt(vb, g2)
            part = fold(s, jnp.max)
            top = part if top is None else jnp.maximum(top, part)
        top = jnp.max(top, axis=0, keepdims=True)
        total = jnp.zeros((8, 2 * TILE), jnp.float32)
        inner = jnp.zeros((8, 2 * TILE), jnp.float32)
        for j in range(picks + 1):
            p = jnp.exp2((s_scr[j] - top) * LOG2E)
            s_scr[j] = p
            p_scr[j] = p.astype(jnp.bfloat16)
            total += fold(p, jnp.sum)
            inner += fold(p * w_scr[j], jnp.sum)
        recip = 1.0 / jnp.sum(total, axis=0, keepdims=True)
        delta = jnp.sum(inner, axis=0, keepdims=True) * recip
        column = jnp.broadcast_to(recip, (PAIR, 2 * TILE)).T
        rq = (q2f * column).astype(jnp.bfloat16)
        rg = (g2f * column).astype(jnp.bfloat16)
        dqt = jnp.zeros((PAIR, 2 * TILE), jnp.float32)
        for j in range(picks + 1):
            ds = (s_scr[j] * (w_scr[j] - delta)).astype(jnp.bfloat16)
            dk = dot_nn(ds, rq)
            dv = dot_nn(p_scr[j], rg)
            if j < picks:
                acc_scr[slots[j], :TILE, :] += dk
                acc_scr[slots[j], TILE:, :] += dv
                kt = kt_scr[slots[j]]
            else:
                own_ref[0, rows, :] = dk
                own_ref[1, rows, :] = dv
                kt = k_ref[rows, :].T
            dqt += dot_nn(kt, ds)
        dqt = dqt * (recip * (HD**-0.5))
        dqt = jnp.concatenate([dqt[:HD, :TILE], dqt[HD:, TILE:]], axis=0)
        dq_ref[rows, :] = dqt.T.astype(jnp.bfloat16)
        return carry

    lax.fori_loop(0, blocks, one_block, 0)

    def finish(p, carry):
        out_ref[p] = acc_scr[p].astype(jnp.bfloat16)
        return carry

    lax.fori_loop(0, peers, finish, 0)


def attend(slots, queries, grad_out, key_rows, value_rows, received, previous, chunk):
    peers, _, chunk_width = received.shape
    rows, width = queries.shape
    blocks = rows // TILE
    picks = slots.shape[0] // blocks
    pairs = chunk_width // PAIR
    base = chunk * pairs
    rows_spec = pl.BlockSpec((rows, PAIR), lambda i, s: (0, base + i))
    pack_spec = pl.BlockSpec((peers, 2 * TILE, PAIR), lambda i, s: (0, 0, i))
    in_specs = [rows_spec] * 4 + [pack_spec]
    operands = [slots, queries, grad_out, key_rows, value_rows, received]
    aliases = {}
    if previous is not None:
        in_specs.append(pl.BlockSpec(memory_space=pl.ANY))
        operands.append(previous)
        aliases = {6: 0}
    keys = TILE * (picks + 1)
    flops = 5 * 2 * 2 * TILE * PAIR * keys * blocks * pairs
    return pl.pallas_call(
        functools.partial(attend_kernel, peers, blocks, picks, previous is not None),
        grid_spec=pltpu.PrefetchScalarGridSpec(
            num_scalar_prefetch=1,
            grid=(pairs,),
            in_specs=in_specs,
            out_specs=[
                rows_spec,
                pl.BlockSpec((2, rows, PAIR), lambda i, s: (0, 0, i)),
                pack_spec,
            ],
            scratch_shapes=[
                pltpu.VMEM((picks + 1, TILE, 2 * TILE), jnp.float32),
                pltpu.VMEM((picks + 1, TILE, 2 * TILE), jnp.float32),
                pltpu.VMEM((picks + 1, TILE, 2 * TILE), jnp.bfloat16),
                pltpu.VMEM((peers, PAIR, TILE), jnp.bfloat16),
                pltpu.VMEM((peers, 2 * TILE, PAIR), jnp.float32),
            ],
        ),
        out_shape=[
            jax.ShapeDtypeStruct((rows, width), jnp.bfloat16),
            jax.ShapeDtypeStruct((2, rows, chunk_width), jnp.float32),
            jax.ShapeDtypeStruct(received.shape, jnp.bfloat16),
        ],
        input_output_aliases=aliases,
        cost_estimate=pl.CostEstimate(
            flops=flops,
            bytes_accessed=24 * 1024 * 1024,
            transcendentals=blocks * pairs * keys * 2 * TILE,
        ),
        compiler_params=pltpu.CompilerParams(vmem_limit_bytes=VMEM_LIMIT),
        name="attend",
    )(*operands)


def combine_kernel(peers, blocks, aliased, ids_ref, own_ref, back_ref, *rest):
    if aliased:
        rest = rest[2:]
    gk_ref, gv_ref, acc = rest
    for b in range(blocks):
        acc[b, :TILE, :] = own_ref[0, b * TILE : (b + 1) * TILE, :]
        acc[b, TILE:, :] = own_ref[1, b * TILE : (b + 1) * TILE, :]

    def add(p, carry):
        target = ids_ref[p]

        @pl.when(target >= 0)
        def _():
            acc[jnp.maximum(target, 0)] += back_ref[p].astype(jnp.float32)

        return carry

    lax.fori_loop(0, peers, add, 0)
    for b in range(blocks):
        gk_ref[b * TILE : (b + 1) * TILE, :] = acc[b, :TILE, :].astype(jnp.bfloat16)
        gv_ref[b * TILE : (b + 1) * TILE, :] = acc[b, TILE:, :].astype(jnp.bfloat16)


def combine(requested, own, returned, previous, chunk, width):
    peers, _, chunk_width = returned.shape
    rows = own.shape[1]
    blocks = rows // TILE
    step = PAIR
    base = chunk * (chunk_width // step)
    in_specs = [
        pl.BlockSpec((2, rows, step), lambda i, s: (0, 0, i)),
        pl.BlockSpec((peers, 2 * TILE, step), lambda i, s: (0, 0, i)),
    ]
    operands = [requested, own, returned]
    aliases = {}
    if previous is not None:
        in_specs += [pl.BlockSpec(memory_space=pl.ANY)] * 2
        operands += list(previous)
        aliases = {3: 0, 4: 1}
    out_spec = pl.BlockSpec((rows, step), lambda i, s: (0, base + i))
    return pl.pallas_call(
        functools.partial(combine_kernel, peers, blocks, previous is not None),
        grid_spec=pltpu.PrefetchScalarGridSpec(
            num_scalar_prefetch=1,
            grid=(chunk_width // step,),
            in_specs=in_specs,
            out_specs=[out_spec, out_spec],
            scratch_shapes=[pltpu.VMEM((blocks, 2 * TILE, step), jnp.float32)],
        ),
        out_shape=[jax.ShapeDtypeStruct((rows, width), jnp.bfloat16)] * 2,
        input_output_aliases=aliases,
        cost_estimate=pl.CostEstimate(flops=0, bytes_accessed=12 * 1024 * 1024, transcendentals=0),
        compiler_params=pltpu.CompilerParams(vmem_limit_bytes=VMEM_LIMIT),
        name="combine",
    )(*operands)


def exchange(x):
    return lax.all_to_all(x, "ctx", split_axis=0, concat_axis=0, tiled=True)


def merge_lanes(a, b):
    low = jnp.concatenate([a[:, :HD], b[:, :HD]], axis=1)
    high = jnp.concatenate([a[:, HD:], b[:, HD:]], axis=1)
    return low, high


def pack_kernel(tokens, k_ref, v_ref, q_ref, g_ref, *refs):
    out_ref = refs[-1]
    kv = merge_lanes(k_ref[...], v_ref[...])
    qg = merge_lanes(q_ref[...], g_ref[...])
    for head in range(2):
        out_ref[head, 0, :tokens, :] = kv[head]
        out_ref[head, 0, tokens : 2 * tokens, :] = qg[head]
    if len(refs) > 1:
        table = refs[0][...].astype(jnp.float32)
        table = jnp.concatenate(
            [table, jnp.zeros((table.shape[0], PAIR - table.shape[1]), jnp.float32)], axis=1
        )
        table = jnp.concatenate(
            [table, jnp.zeros((EXTRA - table.shape[0], PAIR), jnp.float32)], axis=0
        ).astype(jnp.bfloat16)
        for head in range(2):
            out_ref[head, 0, 2 * tokens :, :] = table


def pack_phase(key_rows, value_rows, queries, grad_out, phase, extra=None):
    rows, width = queries.shape
    tokens = rows // 2
    slabs = width // PAIR // PHASES
    spec = pl.BlockSpec((tokens, PAIR), lambda j, c: (c, phase * slabs + j))
    in_specs, operands = [spec] * 4, [key_rows, value_rows, queries, grad_out]
    length = rows
    if extra is not None:
        length += EXTRA
        in_specs.append(pl.BlockSpec(extra.shape, lambda j, c: (0, 0)))
        operands.append(extra)
    packed = pl.pallas_call(
        functools.partial(pack_kernel, tokens),
        grid=(slabs, 2),
        in_specs=in_specs,
        out_specs=pl.BlockSpec((2, 1, length, PAIR), lambda j, c: (j, c, 0, 0)),
        out_shape=jax.ShapeDtypeStruct((2 * slabs, 2, length, PAIR), jnp.bfloat16),
        cost_estimate=pl.CostEstimate(
            flops=0, bytes_accessed=8 * rows * width, transcendentals=0
        ),
        compiler_params=pltpu.CompilerParams(vmem_limit_bytes=VMEM_LIMIT),
        name="pack_phase",
    )(*operands)
    return packed.reshape(4 * slabs, length, PAIR)


def head_kernel(picks, table_ref, qg_ref, mine_ref, other_ref, out_ref, sum_ref, give_ref, *scratch):
    kv_scr, kt_scr, acc_ref, sems = scratch[:4]
    raws, pairs = scratch[4 : 4 + DEPTH], scratch[4 + DEPTH :]
    sources, tokens, _ = qg_ref.shape
    half = tokens // TILE
    lane = lax.broadcasted_iota(jnp.int32, (TILE, PAIR), 1)
    low = lane < HD
    parts = [slice(j * TILE, (j + 1) * TILE) for j in range(picks + 1)]
    final = sources * half - 1

    loads = [
        pltpu.make_async_copy(
            mine_ref.at[:, pl.ds(0, tokens)], kv_scr.at[pl.ds(0, sources)], sems.at[0]
        ),
        pltpu.make_async_copy(other_ref, kv_scr.at[pl.ds(sources, sources)], sems.at[1]),
    ]
    for load in loads:
        load.start()

    def clear(n, carry):
        rows = pl.ds(pl.multiple_of(n * tokens, tokens), tokens)
        acc_ref[rows, :] = jnp.zeros((tokens, PAIR), jnp.float32)
        return carry

    lax.fori_loop(0, 2 * sources, clear, 0)
    for load in loads:
        load.wait()

    def turn(n, carry):
        for j in range(half):
            kt_scr[n * half + j] = kv_scr[n, j * TILE : (j + 1) * TILE, :].T[:HD, :]
        return carry

    lax.fori_loop(0, 2 * sources, turn, 0)

    def tile_rows(n):
        return pl.ds(pl.multiple_of(n * TILE, TILE), TILE)

    def fold(x, op):
        return op(x.reshape(-1, 8, x.shape[-1]), axis=0)

    def load_block(index):
        block = jnp.minimum(index, final)
        named = [table_ref[block * picks + j] for j in range(picks)] + [block]
        rows = [tile_rows(n) for n in named]
        qg = qg_ref[block // half, tile_rows(block % half), :].astype(jnp.float32)
        zero = jnp.zeros_like(qg)
        both = jnp.concatenate(
            [jnp.where(low, qg * (HD**-0.5), zero), jnp.where(low, zero, qg)], axis=0
        )
        return named, rows, both

    def stage_raw(state, slot):
        named, _, both = state
        low_both = both.astype(jnp.bfloat16)
        top = None
        for j in range(picks + 1):
            n = named[j]
            raw = dot_nt(kv_scr[n // half, tile_rows(n % half), :], low_both)
            raws[slot][parts[j]] = raw
            part = fold(raw[:, :TILE], jnp.max)
            top = part if top is None else jnp.maximum(top, part)
            yield
        yield jnp.max(top, axis=0, keepdims=True)

    def stage_exp(top, slot):
        raw_scr, pair_scr = raws[slot], pairs[slot]
        total = jnp.zeros((8, TILE), jnp.float32)
        inner = jnp.zeros((8, TILE), jnp.float32)
        for j in range(picks + 1):
            p = jnp.exp2((raw_scr[parts[j], :TILE] - top) * LOG2E)
            raw_scr[parts[j], :TILE] = p
            pair_scr[parts[j], TILE:] = p.astype(jnp.bfloat16)
            total += fold(p, jnp.sum)
            inner += fold(p * raw_scr[parts[j], TILE:], jnp.sum)
            yield
        recip = 1.0 / jnp.sum(total, axis=0, keepdims=True)
        delta = jnp.sum(inner, axis=0, keepdims=True) * recip
        yield recip, delta

    def stage_grad(state, recip, delta, slot):
        named, rows, both = state
        raw_scr, pair_scr = raws[slot], pairs[slot]
        column = jnp.broadcast_to(recip, (TILE, TILE)).T
        scaled = jnp.concatenate([both[:TILE] * column, both[TILE:] * column], axis=0)
        scaled = scaled.astype(jnp.bfloat16)
        for j in range(picks + 1):
            ds = raw_scr[parts[j], :TILE] * (raw_scr[parts[j], TILE:] - delta)
            pair_scr[parts[j], :TILE] = ds.astype(jnp.bfloat16)
            acc_ref[rows[j], :] += dot_nn(pair_scr[parts[j]], scaled)
            yield
        turned = jnp.concatenate([kt_scr[n] for n in named], axis=1)
        dqt = dot_nn(turned, pair_scr[:, :TILE])
        yield dqt * (recip * (HD**-0.5))

    def together(*stages):
        results = [None] * len(stages)
        live = list(range(len(stages)))
        while live:
            for n in list(live):
                try:
                    value = next(stages[n])
                    if value is not None:
                        results[n] = value
                except StopIteration:
                    live.remove(n)
        return results

    (top0,) = together(stage_raw(load_block(0), 0))
    top1, stats0 = together(stage_raw(load_block(1), 1), stage_exp(top0, 0))

    def round_of_blocks(m, carry):
        top, recip, delta = carry
        held = None
        for n in range(DEPTH):
            index = m * DEPTH + n
            top, (next_recip, next_delta), dqt = together(
                stage_raw(load_block(index + 2), (n + 2) % DEPTH),
                stage_exp(top, (n + 1) % DEPTH),
                stage_grad(load_block(index), recip, delta, n),
            )
            recip, delta = next_recip, next_delta
            if n % 2 == 0:
                held = dqt
            else:
                both = jnp.concatenate([held, dqt], axis=0).T.astype(jnp.bfloat16)
                out_ref[index // half, tile_rows(index % half // 2), :] = both
        return top, recip, delta

    lax.fori_loop(0, sources * half // DEPTH, round_of_blocks, (top1, *stats0))

    store = pltpu.make_async_copy(acc_ref.at[pl.ds(0, sources * tokens)], sum_ref, sems.at[2])
    store.start()

    def finish(s, carry):
        rows = pl.ds(pl.multiple_of((sources + s) * tokens, tokens), tokens)
        give_ref[s] = acc_ref[rows, :].astype(jnp.bfloat16)
        return carry

    lax.fori_loop(0, sources, finish, 0)
    store.wait()


def attend_head(table, received, other):
    peers, tokens, _ = other.shape
    half = tokens // TILE
    total = 2 * peers * tokens
    picks = table.shape[0] // (peers * half)
    keys = TILE * (picks + 1)
    any_spec = pl.BlockSpec(memory_space=pl.ANY)
    scratch = [
        pltpu.VMEM((2 * peers, tokens, PAIR), jnp.bfloat16),
        pltpu.VMEM((2 * peers * half, HD, TILE), jnp.bfloat16),
        pltpu.VMEM((total, PAIR), jnp.float32),
        pltpu.SemaphoreType.DMA((3,)),
    ]
    scratch += [pltpu.VMEM((keys, 2 * TILE), jnp.float32)] * DEPTH
    scratch += [pltpu.VMEM((keys, 2 * TILE), jnp.bfloat16)] * DEPTH
    return pl.pallas_call(
        functools.partial(head_kernel, picks),
        grid_spec=pltpu.PrefetchScalarGridSpec(
            num_scalar_prefetch=1,
            grid=(1,),
            in_specs=[
                pl.BlockSpec((peers, tokens, PAIR), lambda i, t: (0, 1, 0)),
                any_spec,
                any_spec,
            ],
            out_specs=[
                pl.BlockSpec((peers, tokens // 2, PAIR), lambda i, t: (0, 2, 0)),
                any_spec,
                pl.BlockSpec((peers, tokens, PAIR), lambda i, t: (0, 0, 0)),
            ],
            scratch_shapes=scratch,
        ),
        out_shape=[
            jax.ShapeDtypeStruct((peers, 3 * tokens // 2, PAIR), jnp.bfloat16),
            jax.ShapeDtypeStruct((peers * tokens, PAIR), jnp.float32),
            jax.ShapeDtypeStruct((peers, tokens, PAIR), jnp.bfloat16),
        ],
        cost_estimate=pl.CostEstimate(
            flops=5 * 2 * TILE * PAIR * keys * peers * half,
            bytes_accessed=24 * 1024 * 1024,
            transcendentals=peers * half * keys * TILE,
        ),
        compiler_params=pltpu.CompilerParams(vmem_limit_bytes=VMEM_LIMIT),
        name="attend_head",
    )(table, received, received, other)


def merge_kernel(sum_ref, given_ref, before_ref, out_ref):
    out_ref[...] = (sum_ref[...] + given_ref[...].astype(jnp.float32)).astype(jnp.bfloat16)


def merge_sums(sums, given, payload):
    peers, tokens, _ = given.shape
    step = 4
    spec = pl.BlockSpec((step, tokens, PAIR), lambda i: (i, 0, 0))
    return pl.pallas_call(
        merge_kernel,
        grid=(peers // step,),
        in_specs=[spec, spec, pl.BlockSpec(memory_space=pl.ANY)],
        out_specs=spec,
        out_shape=jax.ShapeDtypeStruct(payload.shape, jnp.bfloat16),
        input_output_aliases={2: 0},
        cost_estimate=pl.CostEstimate(
            flops=0, bytes_accessed=8 * peers * tokens * PAIR, transcendentals=0
        ),
        compiler_params=pltpu.CompilerParams(vmem_limit_bytes=VMEM_LIMIT),
        name="merge_sums",
    )(sums.reshape(given.shape), given, payload)


def unpack_kernel(tokens, in_ref, *refs):
    gq_ref, gk_ref, gv_ref = refs[-3:]
    gk_ref[...], gv_ref[...] = merge_lanes(in_ref[0, 0, :tokens, :], in_ref[1, 0, :tokens, :])
    for m in range(tokens // TILE // 2):
        rows = slice(tokens + m * TILE, tokens + (m + 1) * TILE)
        even, odd = merge_lanes(in_ref[0, 0, rows, :], in_ref[1, 0, rows, :])
        gq_ref[2 * m * TILE : (2 * m + 1) * TILE, :] = even
        gq_ref[(2 * m + 1) * TILE : (2 * m + 2) * TILE, :] = odd


def unpack_phase(back, previous, phase, rows, width):
    slabs = width // PAIR // PHASES
    tokens = rows // 2
    in_specs = [pl.BlockSpec((2, 1, back.shape[1], PAIR), lambda j, c: (j, c, 0, 0))]
    operands = [back.reshape(2 * slabs, 2, back.shape[1], PAIR)]
    aliases = {}
    if previous is not None:
        in_specs += [pl.BlockSpec(memory_space=pl.ANY)] * 3
        operands += list(previous)
        aliases = {1: 0, 2: 1, 3: 2}
    return pl.pallas_call(
        functools.partial(unpack_kernel, tokens),
        grid=(slabs, 2),
        in_specs=in_specs,
        out_specs=[pl.BlockSpec((tokens, PAIR), lambda j, c: (c, phase * slabs + j))] * 3,
        out_shape=[jax.ShapeDtypeStruct((rows, width), jnp.bfloat16)] * 3,
        input_output_aliases=aliases,
        cost_estimate=pl.CostEstimate(
            flops=0, bytes_accessed=6 * rows * width, transcendentals=0
        ),
        compiler_params=pltpu.CompilerParams(vmem_limit_bytes=SMALL_LIMIT),
        name="unpack_phase",
    )(*operands)


def by_heads(queries, key_rows, value_rows, grad_out, tile_keys):
    rows, width = queries.shape
    blocks, picks = tile_keys.shape
    peers = lax.axis_size("ctx")
    half = blocks // 2
    tokens = half * TILE
    core = lax.axis_index("ctx") % 2

    def swap(x):
        return lax.ppermute(x, "ctx", [(i, i ^ 1) for i in range(peers)])

    received = [
        exchange(
            pack_phase(
                key_rows, value_rows, queries, grad_out, p, tile_keys if p == 0 else None
            )
        )
        for p in range(PHASES)
    ]
    table = received[0][:, 2 * tokens : 2 * tokens + blocks, :picks].astype(jnp.int32)
    table = jnp.where(core == 0, table[:, :half], table[:, half:])
    local = table % blocks
    side = (local // half + core) % 2
    table = (side * (peers * half) + table // blocks * half + local % half).reshape(-1)
    backs = []
    for p in range(PHASES):
        payload, sums, give = attend_head(table, received[p], swap(received[p][:, :tokens]))
        backs.append(exchange(merge_sums(sums, swap(give), payload)))
    result = None
    for p in range(PHASES):
        result = unpack_phase(backs[p], result, p, rows, width)
    return result


def by_blocks(queries, key_rows, value_rows, grad_out, tile_keys):
    rows, width = queries.shape
    blocks = rows // TILE
    peers = lax.axis_size("ctx")
    peer_range = jnp.arange(peers, dtype=jnp.int32)
    owners = tile_keys // blocks
    local_ids = tile_keys % blocks
    matches = owners[:, :, None] == peer_range[None, None, :]
    wanted = jnp.max(jnp.where(matches, local_ids[:, :, None], -1), axis=(0, 1))
    requested = exchange(wanted)
    slots = owners.reshape(-1)
    chunk_width = width // CHUNKS

    received = [
        exchange(gather_blocks(requested, key_rows, value_rows, c, chunk_width)) for c in range(CHUNKS)
    ]
    grad_queries = None
    owns, backs = [], []
    for c in range(CHUNKS):
        grad_queries, own, out = attend(
            slots, queries, grad_out, key_rows, value_rows, received[c], grad_queries, c
        )
        owns.append(own)
        backs.append(exchange(out))
    result = None
    for c in range(CHUNKS):
        result = combine(requested, owns[c], backs[c], result, c, width)
    return grad_queries, result[0], result[1]


def on_device(queries, key_rows, value_rows, grad_out, tile_keys):
    peers = lax.axis_size("ctx")
    blocks = tile_keys.shape[0]
    one_head_each = peers * HD == queries.shape[1]
    even = peers % 4 == 0 and blocks % 4 == 0 and blocks <= EXTRA
    fits = one_head_each and even and peers * blocks <= 256
    plan = by_heads if fits else by_blocks
    return tuple(plan(queries, key_rows, value_rows, grad_out, tile_keys))


def solution(mesh):
    spec = P(("groups", "ctx"), None)
    return jax.shard_map(
        on_device, mesh=mesh, in_specs=(spec,) * 5, out_specs=(spec,) * 3, check_vma=False
    )
```

```python
import functools

import jax
import jax.numpy as jnp
from jax import lax
from jax.experimental import pallas as pl
from jax.experimental.pallas import tpu as pltpu
from jax.sharding import PartitionSpec as P

HD = 64
TILE = 128
PAIR = 2 * HD
LOG2E = 1.4426950408889634
CHUNKS = 2
DEPTH = 4
PHASES = 2
EXTRA = 16
PARTS = 4
SMALL_LIMIT = 16 * 1024 * 1024
VMEM_LIMIT = 60 * 1024 * 1024


def dot_nt(a, b):
    return lax.dot_general(a, b, (((1,), (1,)), ((), ())), preferred_element_type=jnp.float32)


def dot_nn(a, b):
    return lax.dot_general(a, b, (((1,), (0,)), ((), ())), preferred_element_type=jnp.float32)


def gather_kernel(peers, ids_ref, k_ref, v_ref, out_ref, sems):
    def copies(p):
        rows = pl.ds(pl.multiple_of(jnp.maximum(ids_ref[p], 0) * TILE, TILE), TILE)
        return (
            pltpu.make_async_copy(k_ref.at[rows], out_ref.at[p, pl.ds(0, TILE)], sems.at[0, p]),
            pltpu.make_async_copy(v_ref.at[rows], out_ref.at[p, pl.ds(TILE, TILE)], sems.at[1, p]),
        )

    for p in range(peers):
        for copy in copies(p):
            copy.start()
    for p in range(peers):
        for copy in copies(p):
            copy.wait()


def gather_blocks(ids, key_rows, value_rows, chunk, chunk_width):
    peers = ids.shape[0]
    rows_spec = pl.BlockSpec((key_rows.shape[0], chunk_width), lambda i, s: (0, chunk))
    return pl.pallas_call(
        functools.partial(gather_kernel, peers),
        grid_spec=pltpu.PrefetchScalarGridSpec(
            num_scalar_prefetch=1,
            grid=(1,),
            in_specs=[rows_spec, rows_spec],
            out_specs=pl.BlockSpec(memory_space=pl.ANY),
            scratch_shapes=[pltpu.SemaphoreType.DMA((2, peers))],
        ),
        out_shape=jax.ShapeDtypeStruct((peers, 2 * TILE, chunk_width), jnp.bfloat16),
        compiler_params=pltpu.CompilerParams(vmem_limit_bytes=VMEM_LIMIT),
        name="gather_blocks",
    )(ids, key_rows, value_rows)


def attend_kernel(peers, blocks, picks, aliased, slots_ref, q_ref, g_ref, k_ref, v_ref, recv_ref, *rest):
    if aliased:
        rest = rest[1:]
    dq_ref, own_ref, out_ref, s_scr, w_scr, p_scr, kt_scr, acc_scr = rest
    lane = lax.broadcasted_iota(jnp.int32, (TILE, PAIR), 1)
    first = lane < HD

    def prepare(p, carry):
        kt_scr[p] = recv_ref[p, :TILE, :].T
        acc_scr[p] = jnp.zeros((2 * TILE, PAIR), jnp.float32)
        return carry

    lax.fori_loop(0, peers, prepare, 0)

    def split(x):
        zero = jnp.zeros_like(x)
        return jnp.concatenate([jnp.where(first, x, zero), jnp.where(first, zero, x)], axis=0)

    def one_block(b, carry):
        rows = pl.ds(pl.multiple_of(b * TILE, TILE), TILE)
        q2f = split(q_ref[rows, :].astype(jnp.float32) * (HD**-0.5))
        g2f = split(g_ref[rows, :].astype(jnp.float32))
        q2 = q2f.astype(jnp.bfloat16)
        g2 = g2f.astype(jnp.bfloat16)
        slots = [slots_ref[b * picks + j] for j in range(picks)]

        def fold(x, op):
            x = x.reshape(TILE // 8, 8, 2 * TILE)
            return op(x, axis=0)

        top = None
        for j in range(picks + 1):
            if j < picks:
                kb, vb = recv_ref[slots[j], :TILE, :], recv_ref[slots[j], TILE:, :]
            else:
                kb, vb = k_ref[rows, :], v_ref[rows, :]
            s = dot_nt(kb, q2)
            s_scr[j] = s
            w_scr[j] = dot_nt(vb, g2)
            part = fold(s, jnp.max)
            top = part if top is None else jnp.maximum(top, part)
        top = jnp.max(top, axis=0, keepdims=True)
        total = jnp.zeros((8, 2 * TILE), jnp.float32)
        inner = jnp.zeros((8, 2 * TILE), jnp.float32)
        for j in range(picks + 1):
            p = jnp.exp2((s_scr[j] - top) * LOG2E)
            s_scr[j] = p
            p_scr[j] = p.astype(jnp.bfloat16)
            total += fold(p, jnp.sum)
            inner += fold(p * w_scr[j], jnp.sum)
        recip = 1.0 / jnp.sum(total, axis=0, keepdims=True)
        delta = jnp.sum(inner, axis=0, keepdims=True) * recip
        column = jnp.broadcast_to(recip, (PAIR, 2 * TILE)).T
        rq = (q2f * column).astype(jnp.bfloat16)
        rg = (g2f * column).astype(jnp.bfloat16)
        dqt = jnp.zeros((PAIR, 2 * TILE), jnp.float32)
        for j in range(picks + 1):
            ds = (s_scr[j] * (w_scr[j] - delta)).astype(jnp.bfloat16)
            dk = dot_nn(ds, rq)
            dv = dot_nn(p_scr[j], rg)
            if j < picks:
                acc_scr[slots[j], :TILE, :] += dk
                acc_scr[slots[j], TILE:, :] += dv
                kt = kt_scr[slots[j]]
            else:
                own_ref[0, rows, :] = dk
                own_ref[1, rows, :] = dv
                kt = k_ref[rows, :].T
            dqt += dot_nn(kt, ds)
        dqt = dqt * (recip * (HD**-0.5))
        dqt = jnp.concatenate([dqt[:HD, :TILE], dqt[HD:, TILE:]], axis=0)
        dq_ref[rows, :] = dqt.T.astype(jnp.bfloat16)
        return carry

    lax.fori_loop(0, blocks, one_block, 0)

    def finish(p, carry):
        out_ref[p] = acc_scr[p].astype(jnp.bfloat16)
        return carry

    lax.fori_loop(0, peers, finish, 0)


def attend(slots, queries, grad_out, key_rows, value_rows, received, previous, chunk):
    peers, _, chunk_width = received.shape
    rows, width = queries.shape
    blocks = rows // TILE
    picks = slots.shape[0] // blocks
    pairs = chunk_width // PAIR
    base = chunk * pairs
    rows_spec = pl.BlockSpec((rows, PAIR), lambda i, s: (0, base + i))
    pack_spec = pl.BlockSpec((peers, 2 * TILE, PAIR), lambda i, s: (0, 0, i))
    in_specs = [rows_spec] * 4 + [pack_spec]
    operands = [slots, queries, grad_out, key_rows, value_rows, received]
    aliases = {}
    if previous is not None:
        in_specs.append(pl.BlockSpec(memory_space=pl.ANY))
        operands.append(previous)
        aliases = {6: 0}
    keys = TILE * (picks + 1)
    flops = 5 * 2 * 2 * TILE * PAIR * keys * blocks * pairs
    return pl.pallas_call(
        functools.partial(attend_kernel, peers, blocks, picks, previous is not None),
        grid_spec=pltpu.PrefetchScalarGridSpec(
            num_scalar_prefetch=1,
            grid=(pairs,),
            in_specs=in_specs,
            out_specs=[
                rows_spec,
                pl.BlockSpec((2, rows, PAIR), lambda i, s: (0, 0, i)),
                pack_spec,
            ],
            scratch_shapes=[
                pltpu.VMEM((picks + 1, TILE, 2 * TILE), jnp.float32),
                pltpu.VMEM((picks + 1, TILE, 2 * TILE), jnp.float32),
                pltpu.VMEM((picks + 1, TILE, 2 * TILE), jnp.bfloat16),
                pltpu.VMEM((peers, PAIR, TILE), jnp.bfloat16),
                pltpu.VMEM((peers, 2 * TILE, PAIR), jnp.float32),
            ],
        ),
        out_shape=[
            jax.ShapeDtypeStruct((rows, width), jnp.bfloat16),
            jax.ShapeDtypeStruct((2, rows, chunk_width), jnp.float32),
            jax.ShapeDtypeStruct(received.shape, jnp.bfloat16),
        ],
        input_output_aliases=aliases,
        cost_estimate=pl.CostEstimate(
            flops=flops,
            bytes_accessed=24 * 1024 * 1024,
            transcendentals=blocks * pairs * keys * 2 * TILE,
        ),
        compiler_params=pltpu.CompilerParams(vmem_limit_bytes=VMEM_LIMIT),
        name="attend",
    )(*operands)


def combine_kernel(peers, blocks, aliased, ids_ref, own_ref, back_ref, *rest):
    if aliased:
        rest = rest[2:]
    gk_ref, gv_ref, acc = rest
    for b in range(blocks):
        acc[b, :TILE, :] = own_ref[0, b * TILE : (b + 1) * TILE, :]
        acc[b, TILE:, :] = own_ref[1, b * TILE : (b + 1) * TILE, :]

    def add(p, carry):
        target = ids_ref[p]

        @pl.when(target >= 0)
        def _():
            acc[jnp.maximum(target, 0)] += back_ref[p].astype(jnp.float32)

        return carry

    lax.fori_loop(0, peers, add, 0)
    for b in range(blocks):
        gk_ref[b * TILE : (b + 1) * TILE, :] = acc[b, :TILE, :].astype(jnp.bfloat16)
        gv_ref[b * TILE : (b + 1) * TILE, :] = acc[b, TILE:, :].astype(jnp.bfloat16)


def combine(requested, own, returned, previous, chunk, width):
    peers, _, chunk_width = returned.shape
    rows = own.shape[1]
    blocks = rows // TILE
    step = PAIR
    base = chunk * (chunk_width // step)
    in_specs = [
        pl.BlockSpec((2, rows, step), lambda i, s: (0, 0, i)),
        pl.BlockSpec((peers, 2 * TILE, step), lambda i, s: (0, 0, i)),
    ]
    operands = [requested, own, returned]
    aliases = {}
    if previous is not None:
        in_specs += [pl.BlockSpec(memory_space=pl.ANY)] * 2
        operands += list(previous)
        aliases = {3: 0, 4: 1}
    out_spec = pl.BlockSpec((rows, step), lambda i, s: (0, base + i))
    return pl.pallas_call(
        functools.partial(combine_kernel, peers, blocks, previous is not None),
        grid_spec=pltpu.PrefetchScalarGridSpec(
            num_scalar_prefetch=1,
            grid=(chunk_width // step,),
            in_specs=in_specs,
            out_specs=[out_spec, out_spec],
            scratch_shapes=[pltpu.VMEM((blocks, 2 * TILE, step), jnp.float32)],
        ),
        out_shape=[jax.ShapeDtypeStruct((rows, width), jnp.bfloat16)] * 2,
        input_output_aliases=aliases,
        cost_estimate=pl.CostEstimate(flops=0, bytes_accessed=12 * 1024 * 1024, transcendentals=0),
        compiler_params=pltpu.CompilerParams(vmem_limit_bytes=VMEM_LIMIT),
        name="combine",
    )(*operands)


def exchange(x):
    return lax.all_to_all(x, "ctx", split_axis=0, concat_axis=0, tiled=True)


def merge_lanes(a, b):
    low = jnp.concatenate([a[:, :HD], b[:, :HD]], axis=1)
    high = jnp.concatenate([a[:, HD:], b[:, HD:]], axis=1)
    return low, high


def pack_kernel(tokens, lanes, k_ref, v_ref, q_ref, g_ref, *refs):
    has_table = len(refs) > 5
    table_ref = refs[0]
    out_ref, in_scr, out_scr, in_sems, out_sems = refs[-5:]
    step = tokens // 2
    sources = (k_ref, v_ref, q_ref, g_ref)
    slabs = in_scr.shape[2] // PAIR
    loads = [
        [
            pltpu.make_async_copy(
                ref.at[pl.ds(t * step, step), pl.ds(lanes, slabs * PAIR)],
                in_scr.at[n, pl.ds(t * step, step)],
                in_sems.at[n, t],
            )
            for n, ref in enumerate(sources)
        ]
        for t in range(PARTS)
    ]
    for group in loads:
        for load in group:
            load.start()
    stores = []

    def send(core, start, count, sem):
        rows = pl.ds(start, count)
        copy = pltpu.make_async_copy(
            out_scr.at[:, core, rows], out_ref.at[:, core, rows], out_sems.at[sem]
        )
        copy.start()
        stores.append(copy)

    if has_table:
        table = table_ref[...].astype(jnp.float32)
        table = jnp.concatenate(
            [table, jnp.zeros((table.shape[0], PAIR - table.shape[1]), jnp.float32)], axis=1
        )
        table = jnp.concatenate(
            [table, jnp.zeros((EXTRA - table.shape[0], PAIR), jnp.float32)], axis=0
        ).astype(jnp.bfloat16)
        for chip in range(2 * slabs):
            for core in range(2):
                out_scr[chip, core, 2 * tokens :, :] = table
        for core in range(2):
            send(core, 2 * tokens, EXTRA, 2 * PARTS + core)
    for t in range(PARTS):
        for load in loads[t]:
            load.wait()
        core, start = divmod(t, 2)
        start *= step
        rows = slice(t * step, (t + 1) * step)
        for j in range(slabs):
            cols = slice(j * PAIR, (j + 1) * PAIR)
            for n, place in ((0, start), (2, tokens + start)):
                low, high = merge_lanes(in_scr[n, rows, cols], in_scr[n + 1, rows, cols])
                out_scr[2 * j, core, place : place + step, :] = low
                out_scr[2 * j + 1, core, place : place + step, :] = high
        send(core, start, step, 2 * t)
        send(core, tokens + start, step, 2 * t + 1)
    for copy in stores:
        copy.wait()


def pack_phase(key_rows, value_rows, queries, grad_out, phase, extra=None):
    rows, width = queries.shape
    part = width // PHASES
    chips = part // HD
    any_spec = pl.BlockSpec(memory_space=pl.ANY)
    in_specs, operands = [any_spec] * 4, [key_rows, value_rows, queries, grad_out]
    length = rows
    if extra is not None:
        length += EXTRA
        in_specs.append(pl.BlockSpec(memory_space=pltpu.VMEM))
        operands.append(extra)
    packed = pl.pallas_call(
        functools.partial(pack_kernel, rows // 2, phase * part),
        in_specs=in_specs,
        out_specs=any_spec,
        out_shape=jax.ShapeDtypeStruct((chips, 2, length, PAIR), jnp.bfloat16),
        scratch_shapes=[
            pltpu.VMEM((4, rows, part), jnp.bfloat16),
            pltpu.VMEM((chips, 2, length, PAIR), jnp.bfloat16),
            pltpu.SemaphoreType.DMA((4, PARTS)),
            pltpu.SemaphoreType.DMA((2 * PARTS + 2,)),
        ],
        cost_estimate=pl.CostEstimate(
            flops=0, bytes_accessed=8 * rows * width, transcendentals=0
        ),
        compiler_params=pltpu.CompilerParams(vmem_limit_bytes=VMEM_LIMIT),
        name="pack_phase",
    )(*operands)
    return packed.reshape(2 * chips, length, PAIR)


def head_kernel(picks, table_ref, qg_ref, mine_ref, other_ref, out_ref, sum_ref, give_ref, *scratch):
    kv_scr, kt_scr, acc_ref, sems = scratch[:4]
    raws, pairs = scratch[4 : 4 + DEPTH], scratch[4 + DEPTH :]
    sources, tokens, _ = qg_ref.shape
    half = tokens // TILE
    lane = lax.broadcasted_iota(jnp.int32, (TILE, PAIR), 1)
    low = lane < HD
    parts = [slice(j * TILE, (j + 1) * TILE) for j in range(picks + 1)]
    final = sources * half - 1

    loads = [
        pltpu.make_async_copy(
            mine_ref.at[:, pl.ds(0, tokens)], kv_scr.at[pl.ds(0, sources)], sems.at[0]
        ),
        pltpu.make_async_copy(other_ref, kv_scr.at[pl.ds(sources, sources)], sems.at[1]),
    ]
    for load in loads:
        load.start()

    def clear(n, carry):
        rows = pl.ds(pl.multiple_of(n * tokens, tokens), tokens)
        acc_ref[rows, :] = jnp.zeros((tokens, PAIR), jnp.float32)
        return carry

    lax.fori_loop(0, 2 * sources, clear, 0)
    for load in loads:
        load.wait()

    def turn(n, carry):
        for j in range(half):
            kt_scr[n * half + j] = kv_scr[n, j * TILE : (j + 1) * TILE, :].T[:HD, :]
        return carry

    lax.fori_loop(0, 2 * sources, turn, 0)

    def tile_rows(n):
        return pl.ds(pl.multiple_of(n * TILE, TILE), TILE)

    def fold(x, op):
        return op(x.reshape(-1, 8, x.shape[-1]), axis=0)

    def load_block(index):
        block = jnp.minimum(index, final)
        named = [table_ref[block * picks + j] for j in range(picks)] + [block]
        rows = [tile_rows(n) for n in named]
        qg = qg_ref[block // half, tile_rows(block % half), :].astype(jnp.float32)
        zero = jnp.zeros_like(qg)
        both = jnp.concatenate(
            [jnp.where(low, qg * (HD**-0.5), zero), jnp.where(low, zero, qg)], axis=0
        )
        return named, rows, both

    def stage_raw(state, slot):
        named, _, both = state
        low_both = both.astype(jnp.bfloat16)
        top = None
        for j in range(picks + 1):
            n = named[j]
            raw = dot_nt(kv_scr[n // half, tile_rows(n % half), :], low_both)
            raws[slot][parts[j]] = raw
            part = fold(raw[:, :TILE], jnp.max)
            top = part if top is None else jnp.maximum(top, part)
            yield
        yield jnp.max(top, axis=0, keepdims=True)

    def stage_exp(top, slot):
        raw_scr, pair_scr = raws[slot], pairs[slot]
        total = jnp.zeros((8, TILE), jnp.float32)
        inner = jnp.zeros((8, TILE), jnp.float32)
        for j in range(picks + 1):
            p = jnp.exp2((raw_scr[parts[j], :TILE] - top) * LOG2E)
            raw_scr[parts[j], :TILE] = p
            pair_scr[parts[j], TILE:] = p.astype(jnp.bfloat16)
            total += fold(p, jnp.sum)
            inner += fold(p * raw_scr[parts[j], TILE:], jnp.sum)
            yield
        recip = 1.0 / jnp.sum(total, axis=0, keepdims=True)
        delta = jnp.sum(inner, axis=0, keepdims=True) * recip
        yield recip, delta

    def stage_grad(state, recip, delta, slot):
        named, rows, both = state
        raw_scr, pair_scr = raws[slot], pairs[slot]
        column = jnp.broadcast_to(recip, (TILE, TILE)).T
        scaled = jnp.concatenate([both[:TILE] * column, both[TILE:] * column], axis=0)
        scaled = scaled.astype(jnp.bfloat16)
        for j in range(picks + 1):
            ds = raw_scr[parts[j], :TILE] * (raw_scr[parts[j], TILE:] - delta)
            pair_scr[parts[j], :TILE] = ds.astype(jnp.bfloat16)
            acc_ref[rows[j], :] += dot_nn(pair_scr[parts[j]], scaled)
            yield
        turned = jnp.concatenate([kt_scr[n] for n in named], axis=1)
        dqt = dot_nn(turned, pair_scr[:, :TILE])
        yield dqt * (recip * (HD**-0.5))

    def together(*stages):
        results = [None] * len(stages)
        live = list(range(len(stages)))
        while live:
            for n in list(live):
                try:
                    value = next(stages[n])
                    if value is not None:
                        results[n] = value
                except StopIteration:
                    live.remove(n)
        return results

    (top0,) = together(stage_raw(load_block(0), 0))
    top1, stats0 = together(stage_raw(load_block(1), 1), stage_exp(top0, 0))

    def round_of_blocks(m, carry):
        top, recip, delta = carry
        held = None
        for n in range(DEPTH):
            index = m * DEPTH + n
            top, (next_recip, next_delta), dqt = together(
                stage_raw(load_block(index + 2), (n + 2) % DEPTH),
                stage_exp(top, (n + 1) % DEPTH),
                stage_grad(load_block(index), recip, delta, n),
            )
            recip, delta = next_recip, next_delta
            if n % 2 == 0:
                held = dqt
            else:
                both = jnp.concatenate([held, dqt], axis=0).T.astype(jnp.bfloat16)
                out_ref[index // half, tile_rows(index % half // 2), :] = both
        return top, recip, delta

    lax.fori_loop(0, sources * half // DEPTH, round_of_blocks, (top1, *stats0))

    store = pltpu.make_async_copy(acc_ref.at[pl.ds(0, sources * tokens)], sum_ref, sems.at[2])
    store.start()

    def finish(s, carry):
        rows = pl.ds(pl.multiple_of((sources + s) * tokens, tokens), tokens)
        give_ref[s] = acc_ref[rows, :].astype(jnp.bfloat16)
        return carry

    lax.fori_loop(0, sources, finish, 0)
    store.wait()


def attend_head(table, received, other):
    peers, tokens, _ = other.shape
    half = tokens // TILE
    total = 2 * peers * tokens
    picks = table.shape[0] // (peers * half)
    keys = TILE * (picks + 1)
    any_spec = pl.BlockSpec(memory_space=pl.ANY)
    scratch = [
        pltpu.VMEM((2 * peers, tokens, PAIR), jnp.bfloat16),
        pltpu.VMEM((2 * peers * half, HD, TILE), jnp.bfloat16),
        pltpu.VMEM((total, PAIR), jnp.float32),
        pltpu.SemaphoreType.DMA((3,)),
    ]
    scratch += [pltpu.VMEM((keys, 2 * TILE), jnp.float32)] * DEPTH
    scratch += [pltpu.VMEM((keys, 2 * TILE), jnp.bfloat16)] * DEPTH
    return pl.pallas_call(
        functools.partial(head_kernel, picks),
        grid_spec=pltpu.PrefetchScalarGridSpec(
            num_scalar_prefetch=1,
            grid=(1,),
            in_specs=[
                pl.BlockSpec((peers, tokens, PAIR), lambda i, t: (0, 1, 0)),
                any_spec,
                any_spec,
            ],
            out_specs=[
                pl.BlockSpec((peers, tokens // 2, PAIR), lambda i, t: (0, 2, 0)),
                any_spec,
                pl.BlockSpec((peers, tokens, PAIR), lambda i, t: (0, 0, 0)),
            ],
            scratch_shapes=scratch,
        ),
        out_shape=[
            jax.ShapeDtypeStruct((peers, 3 * tokens // 2, PAIR), jnp.bfloat16),
            jax.ShapeDtypeStruct((peers * tokens, PAIR), jnp.float32),
            jax.ShapeDtypeStruct((peers, tokens, PAIR), jnp.bfloat16),
        ],
        cost_estimate=pl.CostEstimate(
            flops=5 * 2 * TILE * PAIR * keys * peers * half,
            bytes_accessed=24 * 1024 * 1024,
            transcendentals=peers * half * keys * TILE,
        ),
        compiler_params=pltpu.CompilerParams(vmem_limit_bytes=VMEM_LIMIT),
        name="attend_head",
    )(table, received, received, other)


def merge_kernel(sum_ref, given_ref, before_ref, out_ref):
    out_ref[...] = (sum_ref[...] + given_ref[...].astype(jnp.float32)).astype(jnp.bfloat16)


def merge_sums(sums, given, payload):
    peers, tokens, _ = given.shape
    step = 4
    spec = pl.BlockSpec((step, tokens, PAIR), lambda i: (i, 0, 0))
    return pl.pallas_call(
        merge_kernel,
        grid=(peers // step,),
        in_specs=[spec, spec, pl.BlockSpec(memory_space=pl.ANY)],
        out_specs=spec,
        out_shape=jax.ShapeDtypeStruct(payload.shape, jnp.bfloat16),
        input_output_aliases={2: 0},
        cost_estimate=pl.CostEstimate(
            flops=0, bytes_accessed=8 * peers * tokens * PAIR, transcendentals=0
        ),
        compiler_params=pltpu.CompilerParams(vmem_limit_bytes=VMEM_LIMIT),
        name="merge_sums",
    )(sums.reshape(given.shape), given, payload)


def unpack_kernel(tokens, lanes, in_ref, *refs):
    gq_ref, gk_ref, gv_ref, in_scr, gq_scr, gk_scr, gv_scr, in_sems, out_sems = refs[-9:]
    step = tokens // 2
    slabs = gq_scr.shape[1] // PAIR
    loads = []
    for t in range(PARTS):
        core, side = divmod(t, 2)
        places = (pl.ds(side * step, step), pl.ds(tokens + side * step // 2, step // 2))
        loads.append(
            [
                pltpu.make_async_copy(
                    in_ref.at[:, core, rows], in_scr.at[:, core, rows], in_sems.at[n, t]
                )
                for n, rows in enumerate(places)
            ]
        )
    for group in loads:
        for load in group:
            load.start()
    stores = []
    for t in range(PARTS):
        for load in loads[t]:
            load.wait()
        core, side = divmod(t, 2)
        rows = slice(t * step, (t + 1) * step)
        for j in range(slabs):
            cols = slice(j * PAIR, (j + 1) * PAIR)
            place = slice(side * step, (side + 1) * step)
            gk_scr[rows, cols], gv_scr[rows, cols] = merge_lanes(
                in_scr[2 * j, core, place, :], in_scr[2 * j + 1, core, place, :]
            )
            for m in range(step // TILE // 2):
                base = tokens + side * step // 2 + m * TILE
                even, odd = merge_lanes(
                    in_scr[2 * j, core, base : base + TILE, :],
                    in_scr[2 * j + 1, core, base : base + TILE, :],
                )
                base = t * step + 2 * m * TILE
                gq_scr[base : base + TILE, cols] = even
                gq_scr[base + TILE : base + 2 * TILE, cols] = odd
        for n, (scr, ref) in enumerate(((gq_scr, gq_ref), (gk_scr, gk_ref), (gv_scr, gv_ref))):
            copy = pltpu.make_async_copy(
                scr.at[pl.ds(t * step, step)],
                ref.at[pl.ds(t * step, step), pl.ds(lanes, slabs * PAIR)],
                out_sems.at[n, t],
            )
            copy.start()
            stores.append(copy)
    for copy in stores:
        copy.wait()


def unpack_phase(back, previous, phase, rows, width):
    part = width // PHASES
    any_spec = pl.BlockSpec(memory_space=pl.ANY)
    operands = [back.reshape(back.shape[0] // 2, 2, *back.shape[1:])]
    aliases = {}
    if previous is not None:
        operands += list(previous)
        aliases = {1: 0, 2: 1, 3: 2}
    return pl.pallas_call(
        functools.partial(unpack_kernel, rows // 2, phase * part),
        in_specs=[any_spec] * len(operands),
        out_specs=[any_spec] * 3,
        out_shape=[jax.ShapeDtypeStruct((rows, width), jnp.bfloat16)] * 3,
        scratch_shapes=[pltpu.VMEM(operands[0].shape, jnp.bfloat16)]
        + [pltpu.VMEM((rows, part), jnp.bfloat16)] * 3
        + [pltpu.SemaphoreType.DMA((2, PARTS)), pltpu.SemaphoreType.DMA((3, PARTS))],
        input_output_aliases=aliases,
        cost_estimate=pl.CostEstimate(
            flops=0, bytes_accessed=6 * rows * width, transcendentals=0
        ),
        compiler_params=pltpu.CompilerParams(vmem_limit_bytes=SMALL_LIMIT),
        name="unpack_phase",
    )(*operands)


def by_heads(queries, key_rows, value_rows, grad_out, tile_keys):
    rows, width = queries.shape
    blocks, picks = tile_keys.shape
    peers = lax.axis_size("ctx")
    half = blocks // 2
    tokens = half * TILE
    core = lax.axis_index("ctx") % 2

    def swap(x):
        return lax.ppermute(x, "ctx", [(i, i ^ 1) for i in range(peers)])

    received = [
        exchange(
            pack_phase(
                key_rows, value_rows, queries, grad_out, p, tile_keys if p == 0 else None
            )
        )
        for p in range(PHASES)
    ]
    table = received[0][:, 2 * tokens : 2 * tokens + blocks, :picks].astype(jnp.int32)
    table = jnp.where(core == 0, table[:, :half], table[:, half:])
    local = table % blocks
    side = (local // half + core) % 2
    table = (side * (peers * half) + table // blocks * half + local % half).reshape(-1)
    backs = []
    for p in range(PHASES):
        payload, sums, give = attend_head(table, received[p], swap(received[p][:, :tokens]))
        backs.append(exchange(merge_sums(sums, swap(give), payload)))
    result = None
    for p in range(PHASES):
        result = unpack_phase(backs[p], result, p, rows, width)
    return result


def by_blocks(queries, key_rows, value_rows, grad_out, tile_keys):
    rows, width = queries.shape
    blocks = rows // TILE
    peers = lax.axis_size("ctx")
    peer_range = jnp.arange(peers, dtype=jnp.int32)
    owners = tile_keys // blocks
    local_ids = tile_keys % blocks
    matches = owners[:, :, None] == peer_range[None, None, :]
    wanted = jnp.max(jnp.where(matches, local_ids[:, :, None], -1), axis=(0, 1))
    requested = exchange(wanted)
    slots = owners.reshape(-1)
    chunk_width = width // CHUNKS

    received = [
        exchange(gather_blocks(requested, key_rows, value_rows, c, chunk_width)) for c in range(CHUNKS)
    ]
    grad_queries = None
    owns, backs = [], []
    for c in range(CHUNKS):
        grad_queries, own, out = attend(
            slots, queries, grad_out, key_rows, value_rows, received[c], grad_queries, c
        )
        owns.append(own)
        backs.append(exchange(out))
    result = None
    for c in range(CHUNKS):
        result = combine(requested, owns[c], backs[c], result, c, width)
    return grad_queries, result[0], result[1]


def on_device(queries, key_rows, value_rows, grad_out, tile_keys):
    peers = lax.axis_size("ctx")
    blocks = tile_keys.shape[0]
    one_head_each = peers * HD == queries.shape[1]
    even = peers % 4 == 0 and blocks % 4 == 0 and blocks <= EXTRA
    fits = one_head_each and even and peers * blocks <= 256
    plan = by_heads if fits else by_blocks
    return tuple(plan(queries, key_rows, value_rows, grad_out, tile_keys))


def solution(mesh):
    spec = P(("groups", "ctx"), None)
    return jax.shard_map(
        on_device, mesh=mesh, in_specs=(spec,) * 5, out_specs=(spec,) * 3, check_vma=False
    )
```

```python
import functools

import jax
import jax.numpy as jnp
from jax import lax
from jax.experimental import pallas as pl
from jax.experimental.pallas import tpu as pltpu
from jax.sharding import PartitionSpec as P

HD = 64
TILE = 128
PAIR = 2 * HD
LOG2E = 1.4426950408889634
CHUNKS = 2
DEPTH = 4
PHASES = 2
PARTS = 4
SMALL_LIMIT = 8 * 1024 * 1024
VMEM_LIMIT = 60 * 1024 * 1024


def dot_nt(a, b):
    return lax.dot_general(a, b, (((1,), (1,)), ((), ())), preferred_element_type=jnp.float32)


def dot_nn(a, b):
    return lax.dot_general(a, b, (((1,), (0,)), ((), ())), preferred_element_type=jnp.float32)


def gather_kernel(peers, ids_ref, k_ref, v_ref, out_ref, sems):
    def copies(p):
        rows = pl.ds(pl.multiple_of(jnp.maximum(ids_ref[p], 0) * TILE, TILE), TILE)
        return (
            pltpu.make_async_copy(k_ref.at[rows], out_ref.at[p, pl.ds(0, TILE)], sems.at[0, p]),
            pltpu.make_async_copy(v_ref.at[rows], out_ref.at[p, pl.ds(TILE, TILE)], sems.at[1, p]),
        )

    for p in range(peers):
        for copy in copies(p):
            copy.start()
    for p in range(peers):
        for copy in copies(p):
            copy.wait()


def gather_blocks(ids, key_rows, value_rows, chunk, chunk_width):
    peers = ids.shape[0]
    rows_spec = pl.BlockSpec((key_rows.shape[0], chunk_width), lambda i, s: (0, chunk))
    return pl.pallas_call(
        functools.partial(gather_kernel, peers),
        grid_spec=pltpu.PrefetchScalarGridSpec(
            num_scalar_prefetch=1,
            grid=(1,),
            in_specs=[rows_spec, rows_spec],
            out_specs=pl.BlockSpec(memory_space=pl.ANY),
            scratch_shapes=[pltpu.SemaphoreType.DMA((2, peers))],
        ),
        out_shape=jax.ShapeDtypeStruct((peers, 2 * TILE, chunk_width), jnp.bfloat16),
        compiler_params=pltpu.CompilerParams(vmem_limit_bytes=VMEM_LIMIT),
        name="gather_blocks",
    )(ids, key_rows, value_rows)


def attend_kernel(peers, blocks, picks, aliased, slots_ref, q_ref, g_ref, k_ref, v_ref, recv_ref, *rest):
    if aliased:
        rest = rest[1:]
    dq_ref, own_ref, out_ref, s_scr, w_scr, p_scr, kt_scr, acc_scr = rest
    lane = lax.broadcasted_iota(jnp.int32, (TILE, PAIR), 1)
    first = lane < HD

    def prepare(p, carry):
        kt_scr[p] = recv_ref[p, :TILE, :].T
        acc_scr[p] = jnp.zeros((2 * TILE, PAIR), jnp.float32)
        return carry

    lax.fori_loop(0, peers, prepare, 0)

    def split(x):
        zero = jnp.zeros_like(x)
        return jnp.concatenate([jnp.where(first, x, zero), jnp.where(first, zero, x)], axis=0)

    def one_block(b, carry):
        rows = pl.ds(pl.multiple_of(b * TILE, TILE), TILE)
        q2f = split(q_ref[rows, :].astype(jnp.float32) * (HD**-0.5))
        g2f = split(g_ref[rows, :].astype(jnp.float32))
        q2 = q2f.astype(jnp.bfloat16)
        g2 = g2f.astype(jnp.bfloat16)
        slots = [slots_ref[b * picks + j] for j in range(picks)]

        def fold(x, op):
            x = x.reshape(TILE // 8, 8, 2 * TILE)
            return op(x, axis=0)

        top = None
        for j in range(picks + 1):
            if j < picks:
                kb, vb = recv_ref[slots[j], :TILE, :], recv_ref[slots[j], TILE:, :]
            else:
                kb, vb = k_ref[rows, :], v_ref[rows, :]
            s = dot_nt(kb, q2)
            s_scr[j] = s
            w_scr[j] = dot_nt(vb, g2)
            part = fold(s, jnp.max)
            top = part if top is None else jnp.maximum(top, part)
        top = jnp.max(top, axis=0, keepdims=True)
        total = jnp.zeros((8, 2 * TILE), jnp.float32)
        inner = jnp.zeros((8, 2 * TILE), jnp.float32)
        for j in range(picks + 1):
            p = jnp.exp2((s_scr[j] - top) * LOG2E)
            s_scr[j] = p
            p_scr[j] = p.astype(jnp.bfloat16)
            total += fold(p, jnp.sum)
            inner += fold(p * w_scr[j], jnp.sum)
        recip = 1.0 / jnp.sum(total, axis=0, keepdims=True)
        delta = jnp.sum(inner, axis=0, keepdims=True) * recip
        column = jnp.broadcast_to(recip, (PAIR, 2 * TILE)).T
        rq = (q2f * column).astype(jnp.bfloat16)
        rg = (g2f * column).astype(jnp.bfloat16)
        dqt = jnp.zeros((PAIR, 2 * TILE), jnp.float32)
        for j in range(picks + 1):
            ds = (s_scr[j] * (w_scr[j] - delta)).astype(jnp.bfloat16)
            dk = dot_nn(ds, rq)
            dv = dot_nn(p_scr[j], rg)
            if j < picks:
                acc_scr[slots[j], :TILE, :] += dk
                acc_scr[slots[j], TILE:, :] += dv
                kt = kt_scr[slots[j]]
            else:
                own_ref[0, rows, :] = dk
                own_ref[1, rows, :] = dv
                kt = k_ref[rows, :].T
            dqt += dot_nn(kt, ds)
        dqt = dqt * (recip * (HD**-0.5))
        dqt = jnp.concatenate([dqt[:HD, :TILE], dqt[HD:, TILE:]], axis=0)
        dq_ref[rows, :] = dqt.T.astype(jnp.bfloat16)
        return carry

    lax.fori_loop(0, blocks, one_block, 0)

    def finish(p, carry):
        out_ref[p] = acc_scr[p].astype(jnp.bfloat16)
        return carry

    lax.fori_loop(0, peers, finish, 0)


def attend(slots, queries, grad_out, key_rows, value_rows, received, previous, chunk):
    peers, _, chunk_width = received.shape
    rows, width = queries.shape
    blocks = rows // TILE
    picks = slots.shape[0] // blocks
    pairs = chunk_width // PAIR
    base = chunk * pairs
    rows_spec = pl.BlockSpec((rows, PAIR), lambda i, s: (0, base + i))
    pack_spec = pl.BlockSpec((peers, 2 * TILE, PAIR), lambda i, s: (0, 0, i))
    in_specs = [rows_spec] * 4 + [pack_spec]
    operands = [slots, queries, grad_out, key_rows, value_rows, received]
    aliases = {}
    if previous is not None:
        in_specs.append(pl.BlockSpec(memory_space=pl.ANY))
        operands.append(previous)
        aliases = {6: 0}
    keys = TILE * (picks + 1)
    flops = 5 * 2 * 2 * TILE * PAIR * keys * blocks * pairs
    return pl.pallas_call(
        functools.partial(attend_kernel, peers, blocks, picks, previous is not None),
        grid_spec=pltpu.PrefetchScalarGridSpec(
            num_scalar_prefetch=1,
            grid=(pairs,),
            in_specs=in_specs,
            out_specs=[
                rows_spec,
                pl.BlockSpec((2, rows, PAIR), lambda i, s: (0, 0, i)),
                pack_spec,
            ],
            scratch_shapes=[
                pltpu.VMEM((picks + 1, TILE, 2 * TILE), jnp.float32),
                pltpu.VMEM((picks + 1, TILE, 2 * TILE), jnp.float32),
                pltpu.VMEM((picks + 1, TILE, 2 * TILE), jnp.bfloat16),
                pltpu.VMEM((peers, PAIR, TILE), jnp.bfloat16),
                pltpu.VMEM((peers, 2 * TILE, PAIR), jnp.float32),
            ],
        ),
        out_shape=[
            jax.ShapeDtypeStruct((rows, width), jnp.bfloat16),
            jax.ShapeDtypeStruct((2, rows, chunk_width), jnp.float32),
            jax.ShapeDtypeStruct(received.shape, jnp.bfloat16),
        ],
        input_output_aliases=aliases,
        cost_estimate=pl.CostEstimate(
            flops=flops,
            bytes_accessed=24 * 1024 * 1024,
            transcendentals=blocks * pairs * keys * 2 * TILE,
        ),
        compiler_params=pltpu.CompilerParams(vmem_limit_bytes=VMEM_LIMIT),
        name="attend",
    )(*operands)


def combine_kernel(peers, blocks, aliased, ids_ref, own_ref, back_ref, *rest):
    if aliased:
        rest = rest[2:]
    gk_ref, gv_ref, acc = rest
    for b in range(blocks):
        acc[b, :TILE, :] = own_ref[0, b * TILE : (b + 1) * TILE, :]
        acc[b, TILE:, :] = own_ref[1, b * TILE : (b + 1) * TILE, :]

    def add(p, carry):
        target = ids_ref[p]

        @pl.when(target >= 0)
        def _():
            acc[jnp.maximum(target, 0)] += back_ref[p].astype(jnp.float32)

        return carry

    lax.fori_loop(0, peers, add, 0)
    for b in range(blocks):
        gk_ref[b * TILE : (b + 1) * TILE, :] = acc[b, :TILE, :].astype(jnp.bfloat16)
        gv_ref[b * TILE : (b + 1) * TILE, :] = acc[b, TILE:, :].astype(jnp.bfloat16)


def combine(requested, own, returned, previous, chunk, width):
    peers, _, chunk_width = returned.shape
    rows = own.shape[1]
    blocks = rows // TILE
    step = PAIR
    base = chunk * (chunk_width // step)
    in_specs = [
        pl.BlockSpec((2, rows, step), lambda i, s: (0, 0, i)),
        pl.BlockSpec((peers, 2 * TILE, step), lambda i, s: (0, 0, i)),
    ]
    operands = [requested, own, returned]
    aliases = {}
    if previous is not None:
        in_specs += [pl.BlockSpec(memory_space=pl.ANY)] * 2
        operands += list(previous)
        aliases = {3: 0, 4: 1}
    out_spec = pl.BlockSpec((rows, step), lambda i, s: (0, base + i))
    return pl.pallas_call(
        functools.partial(combine_kernel, peers, blocks, previous is not None),
        grid_spec=pltpu.PrefetchScalarGridSpec(
            num_scalar_prefetch=1,
            grid=(chunk_width // step,),
            in_specs=in_specs,
            out_specs=[out_spec, out_spec],
            scratch_shapes=[pltpu.VMEM((blocks, 2 * TILE, step), jnp.float32)],
        ),
        out_shape=[jax.ShapeDtypeStruct((rows, width), jnp.bfloat16)] * 2,
        input_output_aliases=aliases,
        cost_estimate=pl.CostEstimate(flops=0, bytes_accessed=12 * 1024 * 1024, transcendentals=0),
        compiler_params=pltpu.CompilerParams(vmem_limit_bytes=VMEM_LIMIT),
        name="combine",
    )(*operands)


def exchange(x):
    return lax.all_to_all(x, "ctx", split_axis=0, concat_axis=0, tiled=True)


def merge_lanes(a, b):
    low = jnp.concatenate([a[:, :HD], b[:, :HD]], axis=1)
    high = jnp.concatenate([a[:, HD:], b[:, HD:]], axis=1)
    return low, high


def pack_kernel(tokens, lanes, k_ref, v_ref, q_ref, g_ref, out_ref, *scratch):
    in_scr, out_scr, in_sems, out_sems = scratch
    step = tokens // 2
    sources = (k_ref, v_ref, q_ref, g_ref)
    slabs = in_scr.shape[2] // PAIR
    loads = [
        [
            pltpu.make_async_copy(
                ref.at[pl.ds(t * step, step), pl.ds(lanes, slabs * PAIR)],
                in_scr.at[n, pl.ds(t * step, step)],
                in_sems.at[n, t],
            )
            for n, ref in enumerate(sources)
        ]
        for t in range(PARTS)
    ]
    for group in loads:
        for load in group:
            load.start()
    stores = []

    def send(core, start, count, sem):
        rows = pl.ds(start, count)
        copy = pltpu.make_async_copy(
            out_scr.at[:, core, rows], out_ref.at[:, core, rows], out_sems.at[sem]
        )
        copy.start()
        stores.append(copy)

    for t in range(PARTS):
        for load in loads[t]:
            load.wait()
        core, start = divmod(t, 2)
        start *= step
        rows = slice(t * step, (t + 1) * step)
        for j in range(slabs):
            cols = slice(j * PAIR, (j + 1) * PAIR)
            for n, place in ((0, start), (2, tokens + start)):
                low, high = merge_lanes(in_scr[n, rows, cols], in_scr[n + 1, rows, cols])
                out_scr[2 * j, core, place : place + step, :] = low
                out_scr[2 * j + 1, core, place : place + step, :] = high
        send(core, start, step, 2 * t)
        send(core, tokens + start, step, 2 * t + 1)
    for copy in stores:
        copy.wait()


def pack_phase(key_rows, value_rows, queries, grad_out, phase):
    rows, width = queries.shape
    part = width // PHASES
    chips = part // HD
    any_spec = pl.BlockSpec(memory_space=pl.ANY)
    packed = pl.pallas_call(
        functools.partial(pack_kernel, rows // 2, phase * part),
        in_specs=[any_spec] * 4,
        out_specs=any_spec,
        out_shape=jax.ShapeDtypeStruct((chips, 2, rows, PAIR), jnp.bfloat16),
        scratch_shapes=[
            pltpu.VMEM((4, rows, part), jnp.bfloat16),
            pltpu.VMEM((chips, 2, rows, PAIR), jnp.bfloat16),
            pltpu.SemaphoreType.DMA((4, PARTS)),
            pltpu.SemaphoreType.DMA((2 * PARTS,)),
        ],
        cost_estimate=pl.CostEstimate(
            flops=0, bytes_accessed=8 * rows * width, transcendentals=0
        ),
        compiler_params=pltpu.CompilerParams(vmem_limit_bytes=VMEM_LIMIT),
        name="pack_phase",
    )(key_rows, value_rows, queries, grad_out)
    return packed.reshape(2 * chips, rows, PAIR)


def head_kernel(picks, table_ref, qg_ref, mine_ref, other_ref, out_ref, sum_ref, give_ref, *scratch):
    kv_scr, kt_scr, acc_ref, sems = scratch[:4]
    raws, pairs = scratch[4 : 4 + DEPTH], scratch[4 + DEPTH :]
    sources, tokens, _ = qg_ref.shape
    half = tokens // TILE
    lane = lax.broadcasted_iota(jnp.int32, (TILE, PAIR), 1)
    low = lane < HD
    parts = [slice(j * TILE, (j + 1) * TILE) for j in range(picks + 1)]
    final = sources * half - 1

    loads = [
        pltpu.make_async_copy(
            mine_ref.at[:, pl.ds(0, tokens)], kv_scr.at[pl.ds(0, sources)], sems.at[0]
        ),
        pltpu.make_async_copy(other_ref, kv_scr.at[pl.ds(sources, sources)], sems.at[1]),
    ]
    for load in loads:
        load.start()

    def clear(n, carry):
        rows = pl.ds(pl.multiple_of(n * tokens, tokens), tokens)
        acc_ref[rows, :] = jnp.zeros((tokens, PAIR), jnp.float32)
        return carry

    lax.fori_loop(0, 2 * sources, clear, 0)
    for load in loads:
        load.wait()

    def turn(n, carry):
        for j in range(half):
            kt_scr[n * half + j] = kv_scr[n, j * TILE : (j + 1) * TILE, :].T[:HD, :]
        return carry

    lax.fori_loop(0, 2 * sources, turn, 0)

    def tile_rows(n):
        return pl.ds(pl.multiple_of(n * TILE, TILE), TILE)

    def fold(x, op):
        return op(x.reshape(-1, 8, x.shape[-1]), axis=0)

    def load_block(index):
        block = jnp.minimum(index, final)
        named = [table_ref[block * picks + j] for j in range(picks)] + [block]
        rows = [tile_rows(n) for n in named]
        qg = qg_ref[block // half, tile_rows(block % half), :].astype(jnp.float32)
        zero = jnp.zeros_like(qg)
        both = jnp.concatenate(
            [jnp.where(low, qg * (HD**-0.5), zero), jnp.where(low, zero, qg)], axis=0
        )
        return named, rows, both

    def stage_raw(state, slot):
        named, _, both = state
        low_both = both.astype(jnp.bfloat16)
        top = None
        for j in range(picks + 1):
            n = named[j]
            raw = dot_nt(kv_scr[n // half, tile_rows(n % half), :], low_both)
            raws[slot][parts[j]] = raw
            part = fold(raw[:, :TILE], jnp.max)
            top = part if top is None else jnp.maximum(top, part)
            yield
        yield jnp.max(top, axis=0, keepdims=True)

    def stage_exp(top, slot):
        raw_scr, pair_scr = raws[slot], pairs[slot]
        total = jnp.zeros((8, TILE), jnp.float32)
        inner = jnp.zeros((8, TILE), jnp.float32)
        for j in range(picks + 1):
            p = jnp.exp2((raw_scr[parts[j], :TILE] - top) * LOG2E)
            raw_scr[parts[j], :TILE] = p
            pair_scr[parts[j], TILE:] = p.astype(jnp.bfloat16)
            total += fold(p, jnp.sum)
            inner += fold(p * raw_scr[parts[j], TILE:], jnp.sum)
            yield
        recip = 1.0 / jnp.sum(total, axis=0, keepdims=True)
        delta = jnp.sum(inner, axis=0, keepdims=True) * recip
        yield recip, delta

    def stage_grad(state, recip, delta, slot):
        named, rows, both = state
        raw_scr, pair_scr = raws[slot], pairs[slot]
        column = jnp.broadcast_to(recip, (TILE, TILE)).T
        scaled = jnp.concatenate([both[:TILE] * column, both[TILE:] * column], axis=0)
        scaled = scaled.astype(jnp.bfloat16)
        for j in range(picks + 1):
            ds = raw_scr[parts[j], :TILE] * (raw_scr[parts[j], TILE:] - delta)
            pair_scr[parts[j], :TILE] = ds.astype(jnp.bfloat16)
            acc_ref[rows[j], :] += dot_nn(pair_scr[parts[j]], scaled)
            yield
        turned = jnp.concatenate([kt_scr[n] for n in named], axis=1)
        dqt = dot_nn(turned, pair_scr[:, :TILE])
        yield dqt * (recip * (HD**-0.5))

    def together(*stages):
        results = [None] * len(stages)
        live = list(range(len(stages)))
        while live:
            for n in list(live):
                try:
                    value = next(stages[n])
                    if value is not None:
                        results[n] = value
                except StopIteration:
                    live.remove(n)
        return results

    (top0,) = together(stage_raw(load_block(0), 0))
    top1, stats0 = together(stage_raw(load_block(1), 1), stage_exp(top0, 0))

    def round_of_blocks(m, carry):
        top, recip, delta = carry
        held = None
        for n in range(DEPTH):
            index = m * DEPTH + n
            top, (next_recip, next_delta), dqt = together(
                stage_raw(load_block(index + 2), (n + 2) % DEPTH),
                stage_exp(top, (n + 1) % DEPTH),
                stage_grad(load_block(index), recip, delta, n),
            )
            recip, delta = next_recip, next_delta
            if n % 2 == 0:
                held = dqt
            else:
                both = jnp.concatenate([held, dqt], axis=0).T.astype(jnp.bfloat16)
                out_ref[index // half, tile_rows(index % half // 2), :] = both
        return top, recip, delta

    lax.fori_loop(0, sources * half // DEPTH, round_of_blocks, (top1, *stats0))

    store = pltpu.make_async_copy(acc_ref.at[pl.ds(0, sources * tokens)], sum_ref, sems.at[2])
    store.start()

    def finish(s, carry):
        rows = pl.ds(pl.multiple_of((sources + s) * tokens, tokens), tokens)
        give_ref[s] = acc_ref[rows, :].astype(jnp.bfloat16)
        return carry

    lax.fori_loop(0, sources, finish, 0)
    store.wait()


def attend_head(table, received, other):
    peers, tokens, _ = other.shape
    half = tokens // TILE
    total = 2 * peers * tokens
    picks = table.shape[0] // (peers * half)
    keys = TILE * (picks + 1)
    any_spec = pl.BlockSpec(memory_space=pl.ANY)
    scratch = [
        pltpu.VMEM((2 * peers, tokens, PAIR), jnp.bfloat16),
        pltpu.VMEM((2 * peers * half, HD, TILE), jnp.bfloat16),
        pltpu.VMEM((total, PAIR), jnp.float32),
        pltpu.SemaphoreType.DMA((3,)),
    ]
    scratch += [pltpu.VMEM((keys, 2 * TILE), jnp.float32)] * DEPTH
    scratch += [pltpu.VMEM((keys, 2 * TILE), jnp.bfloat16)] * DEPTH
    return pl.pallas_call(
        functools.partial(head_kernel, picks),
        grid_spec=pltpu.PrefetchScalarGridSpec(
            num_scalar_prefetch=1,
            grid=(1,),
            in_specs=[
                pl.BlockSpec((peers, tokens, PAIR), lambda i, t: (0, 1, 0)),
                any_spec,
                any_spec,
            ],
            out_specs=[
                pl.BlockSpec((peers, tokens // 2, PAIR), lambda i, t: (0, 2, 0)),
                any_spec,
                pl.BlockSpec((peers, tokens, PAIR), lambda i, t: (0, 0, 0)),
            ],
            scratch_shapes=scratch,
        ),
        out_shape=[
            jax.ShapeDtypeStruct((peers, 3 * tokens // 2, PAIR), jnp.bfloat16),
            jax.ShapeDtypeStruct((peers * tokens, PAIR), jnp.float32),
            jax.ShapeDtypeStruct((peers, tokens, PAIR), jnp.bfloat16),
        ],
        cost_estimate=pl.CostEstimate(
            flops=5 * 2 * TILE * PAIR * keys * peers * half,
            bytes_accessed=24 * 1024 * 1024,
            transcendentals=peers * half * keys * TILE,
        ),
        compiler_params=pltpu.CompilerParams(vmem_limit_bytes=VMEM_LIMIT),
        name="attend_head",
    )(table, received, received, other)


def merge_kernel(sum_ref, given_ref, before_ref, out_ref):
    out_ref[...] = (sum_ref[...] + given_ref[...].astype(jnp.float32)).astype(jnp.bfloat16)


def merge_sums(sums, given, payload):
    peers, tokens, _ = given.shape
    step = 4
    spec = pl.BlockSpec((step, tokens, PAIR), lambda i: (i, 0, 0))
    return pl.pallas_call(
        merge_kernel,
        grid=(peers // step,),
        in_specs=[spec, spec, pl.BlockSpec(memory_space=pl.ANY)],
        out_specs=spec,
        out_shape=jax.ShapeDtypeStruct(payload.shape, jnp.bfloat16),
        input_output_aliases={2: 0},
        cost_estimate=pl.CostEstimate(
            flops=0, bytes_accessed=8 * peers * tokens * PAIR, transcendentals=0
        ),
        compiler_params=pltpu.CompilerParams(vmem_limit_bytes=VMEM_LIMIT),
        name="merge_sums",
    )(sums.reshape(given.shape), given, payload)


def unpack_kernel(tokens, lanes, in_ref, *refs):
    gq_ref, gk_ref, gv_ref, in_scr, gq_scr, gk_scr, gv_scr, in_sems, out_sems = refs[-9:]
    step = tokens // 2
    slabs = gq_scr.shape[1] // PAIR
    loads = []
    for t in range(PARTS):
        core, side = divmod(t, 2)
        places = (pl.ds(side * step, step), pl.ds(tokens + side * step // 2, step // 2))
        loads.append(
            [
                pltpu.make_async_copy(
                    in_ref.at[:, core, rows], in_scr.at[:, core, rows], in_sems.at[n, t]
                )
                for n, rows in enumerate(places)
            ]
        )
    for group in loads:
        for load in group:
            load.start()
    stores = []
    for t in range(PARTS):
        for load in loads[t]:
            load.wait()
        core, side = divmod(t, 2)
        rows = slice(t * step, (t + 1) * step)
        for j in range(slabs):
            cols = slice(j * PAIR, (j + 1) * PAIR)
            place = slice(side * step, (side + 1) * step)
            gk_scr[rows, cols], gv_scr[rows, cols] = merge_lanes(
                in_scr[2 * j, core, place, :], in_scr[2 * j + 1, core, place, :]
            )
            for m in range(step // TILE // 2):
                base = tokens + side * step // 2 + m * TILE
                even, odd = merge_lanes(
                    in_scr[2 * j, core, base : base + TILE, :],
                    in_scr[2 * j + 1, core, base : base + TILE, :],
                )
                base = t * step + 2 * m * TILE
                gq_scr[base : base + TILE, cols] = even
                gq_scr[base + TILE : base + 2 * TILE, cols] = odd
        for n, (scr, ref) in enumerate(((gq_scr, gq_ref), (gk_scr, gk_ref), (gv_scr, gv_ref))):
            copy = pltpu.make_async_copy(
                scr.at[pl.ds(t * step, step)],
                ref.at[pl.ds(t * step, step), pl.ds(lanes, slabs * PAIR)],
                out_sems.at[n, t],
            )
            copy.start()
            stores.append(copy)
    for copy in stores:
        copy.wait()


def unpack_phase(back, previous, phase, rows, width):
    part = width // PHASES
    any_spec = pl.BlockSpec(memory_space=pl.ANY)
    operands = [back.reshape(back.shape[0] // 2, 2, *back.shape[1:])]
    aliases = {}
    if previous is not None:
        operands += list(previous)
        aliases = {1: 0, 2: 1, 3: 2}
    return pl.pallas_call(
        functools.partial(unpack_kernel, rows // 2, phase * part),
        in_specs=[any_spec] * len(operands),
        out_specs=[any_spec] * 3,
        out_shape=[jax.ShapeDtypeStruct((rows, width), jnp.bfloat16)] * 3,
        scratch_shapes=[pltpu.VMEM(operands[0].shape, jnp.bfloat16)]
        + [pltpu.VMEM((rows, part), jnp.bfloat16)] * 3
        + [pltpu.SemaphoreType.DMA((2, PARTS)), pltpu.SemaphoreType.DMA((3, PARTS))],
        input_output_aliases=aliases,
        cost_estimate=pl.CostEstimate(
            flops=0, bytes_accessed=6 * rows * width, transcendentals=0
        ),
        compiler_params=pltpu.CompilerParams(vmem_limit_bytes=SMALL_LIMIT),
        name="unpack_phase",
    )(*operands)


def by_heads(queries, key_rows, value_rows, grad_out, tile_keys):
    rows, width = queries.shape
    blocks, picks = tile_keys.shape
    peers = lax.axis_size("ctx")
    half = blocks // 2
    tokens = half * TILE
    core = lax.axis_index("ctx") % 2

    def swap(x):
        return lax.ppermute(x, "ctx", [(i, i ^ 1) for i in range(peers)])

    packed = [
        pack_phase(key_rows, value_rows, queries, grad_out, p) for p in range(PHASES)
    ]
    table, packed[1] = lax.optimization_barrier((tile_keys, packed[1]))
    index = lax.axis_index("ctx")
    bit = 1
    while bit < peers:
        there = lax.ppermute(table, "ctx", [(i, i ^ bit) for i in range(peers)])
        upper = index // bit % 2 == 1
        table = jnp.concatenate(
            [jnp.where(upper, there, table), jnp.where(upper, table, there)], axis=0
        )
        bit *= 2
    table = table.reshape(peers, blocks, picks)
    table = jnp.where(core == 0, table[:, :half], table[:, half:])
    local = table % blocks
    side = (local // half + core) % 2
    table = (side * (peers * half) + table // blocks * half + local % half).reshape(-1)
    table, packed[1] = lax.optimization_barrier((table, packed[1]))
    received = [exchange(x) for x in packed]
    backs = []
    for p in range(PHASES):
        payload, sums, give = attend_head(table, received[p], swap(received[p][:, :tokens]))
        backs.append(exchange(merge_sums(sums, swap(give), payload)))
    result = None
    for p in range(PHASES):
        result = unpack_phase(backs[p], result, p, rows, width)
    return result


def by_blocks(queries, key_rows, value_rows, grad_out, tile_keys):
    rows, width = queries.shape
    blocks = rows // TILE
    peers = lax.axis_size("ctx")
    peer_range = jnp.arange(peers, dtype=jnp.int32)
    owners = tile_keys // blocks
    local_ids = tile_keys % blocks
    matches = owners[:, :, None] == peer_range[None, None, :]
    wanted = jnp.max(jnp.where(matches, local_ids[:, :, None], -1), axis=(0, 1))
    requested = exchange(wanted)
    slots = owners.reshape(-1)
    chunk_width = width // CHUNKS

    received = [
        exchange(gather_blocks(requested, key_rows, value_rows, c, chunk_width)) for c in range(CHUNKS)
    ]
    grad_queries = None
    owns, backs = [], []
    for c in range(CHUNKS):
        grad_queries, own, out = attend(
            slots, queries, grad_out, key_rows, value_rows, received[c], grad_queries, c
        )
        owns.append(own)
        backs.append(exchange(out))
    result = None
    for c in range(CHUNKS):
        result = combine(requested, owns[c], backs[c], result, c, width)
    return grad_queries, result[0], result[1]


def on_device(queries, key_rows, value_rows, grad_out, tile_keys):
    peers = lax.axis_size("ctx")
    blocks = tile_keys.shape[0]
    one_head_each = peers * HD == queries.shape[1]
    even = peers & (peers - 1) == 0 and peers % 4 == 0 and blocks % 4 == 0
    fits = one_head_each and even
    plan = by_heads if fits else by_blocks
    return tuple(plan(queries, key_rows, value_rows, grad_out, tile_keys))


def solution(mesh):
    spec = P(("groups", "ctx"), None)
    return jax.shard_map(
        on_device, mesh=mesh, in_specs=(spec,) * 5, out_specs=(spec,) * 3, check_vma=False
    )
```

```python
import functools

import jax
import jax.numpy as jnp
from jax import lax
from jax.experimental import pallas as pl
from jax.experimental.pallas import tpu as pltpu
from jax.sharding import PartitionSpec as P

HD = 64
TILE = 128
PAIR = 2 * HD
LOG2E = 1.4426950408889634
CHUNKS = 2
DEPTH = 4
PHASES = 2
EXTRA = 16
PARTS = 4
SMALL_LIMIT = 16 * 1024 * 1024
VMEM_LIMIT = 60 * 1024 * 1024


def dot_nt(a, b):
    return lax.dot_general(a, b, (((1,), (1,)), ((), ())), preferred_element_type=jnp.float32)


def dot_nn(a, b):
    return lax.dot_general(a, b, (((1,), (0,)), ((), ())), preferred_element_type=jnp.float32)


def gather_kernel(peers, ids_ref, k_ref, v_ref, out_ref, sems):
    def copies(p):
        rows = pl.ds(pl.multiple_of(jnp.maximum(ids_ref[p], 0) * TILE, TILE), TILE)
        return (
            pltpu.make_async_copy(k_ref.at[rows], out_ref.at[p, pl.ds(0, TILE)], sems.at[0, p]),
            pltpu.make_async_copy(v_ref.at[rows], out_ref.at[p, pl.ds(TILE, TILE)], sems.at[1, p]),
        )

    for p in range(peers):
        for copy in copies(p):
            copy.start()
    for p in range(peers):
        for copy in copies(p):
            copy.wait()


def gather_blocks(ids, key_rows, value_rows, chunk, chunk_width):
    peers = ids.shape[0]
    rows_spec = pl.BlockSpec((key_rows.shape[0], chunk_width), lambda i, s: (0, chunk))
    return pl.pallas_call(
        functools.partial(gather_kernel, peers),
        grid_spec=pltpu.PrefetchScalarGridSpec(
            num_scalar_prefetch=1,
            grid=(1,),
            in_specs=[rows_spec, rows_spec],
            out_specs=pl.BlockSpec(memory_space=pl.ANY),
            scratch_shapes=[pltpu.SemaphoreType.DMA((2, peers))],
        ),
        out_shape=jax.ShapeDtypeStruct((peers, 2 * TILE, chunk_width), jnp.bfloat16),
        compiler_params=pltpu.CompilerParams(vmem_limit_bytes=VMEM_LIMIT),
        name="gather_blocks",
    )(ids, key_rows, value_rows)


def attend_kernel(peers, blocks, picks, aliased, slots_ref, q_ref, g_ref, k_ref, v_ref, recv_ref, *rest):
    if aliased:
        rest = rest[1:]
    dq_ref, own_ref, out_ref, s_scr, w_scr, p_scr, kt_scr, acc_scr = rest
    lane = lax.broadcasted_iota(jnp.int32, (TILE, PAIR), 1)
    first = lane < HD

    def prepare(p, carry):
        kt_scr[p] = recv_ref[p, :TILE, :].T
        acc_scr[p] = jnp.zeros((2 * TILE, PAIR), jnp.float32)
        return carry

    lax.fori_loop(0, peers, prepare, 0)

    def split(x):
        zero = jnp.zeros_like(x)
        return jnp.concatenate([jnp.where(first, x, zero), jnp.where(first, zero, x)], axis=0)

    def one_block(b, carry):
        rows = pl.ds(pl.multiple_of(b * TILE, TILE), TILE)
        q2f = split(q_ref[rows, :].astype(jnp.float32) * (HD**-0.5))
        g2f = split(g_ref[rows, :].astype(jnp.float32))
        q2 = q2f.astype(jnp.bfloat16)
        g2 = g2f.astype(jnp.bfloat16)
        slots = [slots_ref[b * picks + j] for j in range(picks)]

        def fold(x, op):
            x = x.reshape(TILE // 8, 8, 2 * TILE)
            return op(x, axis=0)

        top = None
        for j in range(picks + 1):
            if j < picks:
                kb, vb = recv_ref[slots[j], :TILE, :], recv_ref[slots[j], TILE:, :]
            else:
                kb, vb = k_ref[rows, :], v_ref[rows, :]
            s = dot_nt(kb, q2)
            s_scr[j] = s
            w_scr[j] = dot_nt(vb, g2)
            part = fold(s, jnp.max)
            top = part if top is None else jnp.maximum(top, part)
        top = jnp.max(top, axis=0, keepdims=True)
        total = jnp.zeros((8, 2 * TILE), jnp.float32)
        inner = jnp.zeros((8, 2 * TILE), jnp.float32)
        for j in range(picks + 1):
            p = jnp.exp2((s_scr[j] - top) * LOG2E)
            s_scr[j] = p
            p_scr[j] = p.astype(jnp.bfloat16)
            total += fold(p, jnp.sum)
            inner += fold(p * w_scr[j], jnp.sum)
        recip = 1.0 / jnp.sum(total, axis=0, keepdims=True)
        delta = jnp.sum(inner, axis=0, keepdims=True) * recip
        column = jnp.broadcast_to(recip, (PAIR, 2 * TILE)).T
        rq = (q2f * column).astype(jnp.bfloat16)
        rg = (g2f * column).astype(jnp.bfloat16)
        dqt = jnp.zeros((PAIR, 2 * TILE), jnp.float32)
        for j in range(picks + 1):
            ds = (s_scr[j] * (w_scr[j] - delta)).astype(jnp.bfloat16)
            dk = dot_nn(ds, rq)
            dv = dot_nn(p_scr[j], rg)
            if j < picks:
                acc_scr[slots[j], :TILE, :] += dk
                acc_scr[slots[j], TILE:, :] += dv
                kt = kt_scr[slots[j]]
            else:
                own_ref[0, rows, :] = dk
                own_ref[1, rows, :] = dv
                kt = k_ref[rows, :].T
            dqt += dot_nn(kt, ds)
        dqt = dqt * (recip * (HD**-0.5))
        dqt = jnp.concatenate([dqt[:HD, :TILE], dqt[HD:, TILE:]], axis=0)
        dq_ref[rows, :] = dqt.T.astype(jnp.bfloat16)
        return carry

    lax.fori_loop(0, blocks, one_block, 0)

    def finish(p, carry):
        out_ref[p] = acc_scr[p].astype(jnp.bfloat16)
        return carry

    lax.fori_loop(0, peers, finish, 0)


def attend(slots, queries, grad_out, key_rows, value_rows, received, previous, chunk):
    peers, _, chunk_width = received.shape
    rows, width = queries.shape
    blocks = rows // TILE
    picks = slots.shape[0] // blocks
    pairs = chunk_width // PAIR
    base = chunk * pairs
    rows_spec = pl.BlockSpec((rows, PAIR), lambda i, s: (0, base + i))
    pack_spec = pl.BlockSpec((peers, 2 * TILE, PAIR), lambda i, s: (0, 0, i))
    in_specs = [rows_spec] * 4 + [pack_spec]
    operands = [slots, queries, grad_out, key_rows, value_rows, received]
    aliases = {}
    if previous is not None:
        in_specs.append(pl.BlockSpec(memory_space=pl.ANY))
        operands.append(previous)
        aliases = {6: 0}
    keys = TILE * (picks + 1)
    flops = 5 * 2 * 2 * TILE * PAIR * keys * blocks * pairs
    return pl.pallas_call(
        functools.partial(attend_kernel, peers, blocks, picks, previous is not None),
        grid_spec=pltpu.PrefetchScalarGridSpec(
            num_scalar_prefetch=1,
            grid=(pairs,),
            in_specs=in_specs,
            out_specs=[
                rows_spec,
                pl.BlockSpec((2, rows, PAIR), lambda i, s: (0, 0, i)),
                pack_spec,
            ],
            scratch_shapes=[
                pltpu.VMEM((picks + 1, TILE, 2 * TILE), jnp.float32),
                pltpu.VMEM((picks + 1, TILE, 2 * TILE), jnp.float32),
                pltpu.VMEM((picks + 1, TILE, 2 * TILE), jnp.bfloat16),
                pltpu.VMEM((peers, PAIR, TILE), jnp.bfloat16),
                pltpu.VMEM((peers, 2 * TILE, PAIR), jnp.float32),
            ],
        ),
        out_shape=[
            jax.ShapeDtypeStruct((rows, width), jnp.bfloat16),
            jax.ShapeDtypeStruct((2, rows, chunk_width), jnp.float32),
            jax.ShapeDtypeStruct(received.shape, jnp.bfloat16),
        ],
        input_output_aliases=aliases,
        cost_estimate=pl.CostEstimate(
            flops=flops,
            bytes_accessed=24 * 1024 * 1024,
            transcendentals=blocks * pairs * keys * 2 * TILE,
        ),
        compiler_params=pltpu.CompilerParams(vmem_limit_bytes=VMEM_LIMIT),
        name="attend",
    )(*operands)


def combine_kernel(peers, blocks, aliased, ids_ref, own_ref, back_ref, *rest):
    if aliased:
        rest = rest[2:]
    gk_ref, gv_ref, acc = rest
    for b in range(blocks):
        acc[b, :TILE, :] = own_ref[0, b * TILE : (b + 1) * TILE, :]
        acc[b, TILE:, :] = own_ref[1, b * TILE : (b + 1) * TILE, :]

    def add(p, carry):
        target = ids_ref[p]

        @pl.when(target >= 0)
        def _():
            acc[jnp.maximum(target, 0)] += back_ref[p].astype(jnp.float32)

        return carry

    lax.fori_loop(0, peers, add, 0)
    for b in range(blocks):
        gk_ref[b * TILE : (b + 1) * TILE, :] = acc[b, :TILE, :].astype(jnp.bfloat16)
        gv_ref[b * TILE : (b + 1) * TILE, :] = acc[b, TILE:, :].astype(jnp.bfloat16)


def combine(requested, own, returned, previous, chunk, width):
    peers, _, chunk_width = returned.shape
    rows = own.shape[1]
    blocks = rows // TILE
    step = PAIR
    base = chunk * (chunk_width // step)
    in_specs = [
        pl.BlockSpec((2, rows, step), lambda i, s: (0, 0, i)),
        pl.BlockSpec((peers, 2 * TILE, step), lambda i, s: (0, 0, i)),
    ]
    operands = [requested, own, returned]
    aliases = {}
    if previous is not None:
        in_specs += [pl.BlockSpec(memory_space=pl.ANY)] * 2
        operands += list(previous)
        aliases = {3: 0, 4: 1}
    out_spec = pl.BlockSpec((rows, step), lambda i, s: (0, base + i))
    return pl.pallas_call(
        functools.partial(combine_kernel, peers, blocks, previous is not None),
        grid_spec=pltpu.PrefetchScalarGridSpec(
            num_scalar_prefetch=1,
            grid=(chunk_width // step,),
            in_specs=in_specs,
            out_specs=[out_spec, out_spec],
            scratch_shapes=[pltpu.VMEM((blocks, 2 * TILE, step), jnp.float32)],
        ),
        out_shape=[jax.ShapeDtypeStruct((rows, width), jnp.bfloat16)] * 2,
        input_output_aliases=aliases,
        cost_estimate=pl.CostEstimate(flops=0, bytes_accessed=12 * 1024 * 1024, transcendentals=0),
        compiler_params=pltpu.CompilerParams(vmem_limit_bytes=VMEM_LIMIT),
        name="combine",
    )(*operands)


def exchange(x):
    return lax.all_to_all(x, "ctx", split_axis=0, concat_axis=0, tiled=True)


def merge_lanes(a, b):
    low = jnp.concatenate([a[:, :HD], b[:, :HD]], axis=1)
    high = jnp.concatenate([a[:, HD:], b[:, HD:]], axis=1)
    return low, high


def pack_kernel(tokens, lanes, k_ref, v_ref, q_ref, g_ref, *refs):
    has_table = len(refs) > 5
    if has_table:
        table_ref, refs, (table_scr, table_sem) = refs[0], refs[1:-2], refs[-2:]
    out_ref, in_scr, out_scr, in_sems, out_sems = refs
    step = tokens // 2
    sources = (k_ref, v_ref, q_ref, g_ref)
    slabs = in_scr.shape[2] // PAIR
    loads = [
        [
            pltpu.make_async_copy(
                ref.at[pl.ds(t * step, step), pl.ds(lanes, slabs * PAIR)],
                in_scr.at[n, pl.ds(t * step, step)],
                in_sems.at[n, t],
            )
            for n, ref in enumerate(sources)
        ]
        for t in range(PARTS)
    ]
    if has_table:
        fetch = pltpu.make_async_copy(table_ref, table_scr, table_sem)
        fetch.start()
    for group in loads:
        for load in group:
            load.start()
    stores = []

    def send(core, start, count, sem):
        rows = pl.ds(start, count)
        copy = pltpu.make_async_copy(
            out_scr.at[:, core, rows], out_ref.at[:, core, rows], out_sems.at[sem]
        )
        copy.start()
        stores.append(copy)

    for t in range(PARTS):
        for load in loads[t]:
            load.wait()
        core, start = divmod(t, 2)
        start *= step
        rows = slice(t * step, (t + 1) * step)
        for j in range(slabs):
            cols = slice(j * PAIR, (j + 1) * PAIR)
            for n, place in ((0, start), (2, tokens + start)):
                low, high = merge_lanes(in_scr[n, rows, cols], in_scr[n + 1, rows, cols])
                out_scr[2 * j, core, place : place + step, :] = low
                out_scr[2 * j + 1, core, place : place + step, :] = high
        send(core, start, step, 2 * t)
        tail = EXTRA if has_table and start + step == tokens else 0
        send(core, tokens + start, step + tail, 2 * t + 1)
        if has_table and t == 0:
            fetch.wait()
            table = table_scr[...].astype(jnp.float32)
            table = jnp.concatenate(
                [table, jnp.zeros((table.shape[0], PAIR - table.shape[1]), jnp.float32)], axis=1
            )
            table = jnp.concatenate(
                [table, jnp.zeros((EXTRA - table.shape[0], PAIR), jnp.float32)], axis=0
            ).astype(jnp.bfloat16)
            for chip in range(2 * slabs):
                for core in range(2):
                    out_scr[chip, core, 2 * tokens :, :] = table
    for copy in stores:
        copy.wait()


def pack_phase(key_rows, value_rows, queries, grad_out, phase, extra=None):
    rows, width = queries.shape
    part = width // PHASES
    chips = part // HD
    any_spec = pl.BlockSpec(memory_space=pl.ANY)
    in_specs, operands = [any_spec] * 4, [key_rows, value_rows, queries, grad_out]
    length, more = rows, []
    if extra is not None:
        length += EXTRA
        in_specs.append(any_spec)
        operands.append(extra)
        more = [pltpu.VMEM(extra.shape, extra.dtype), pltpu.SemaphoreType.DMA]
    packed = pl.pallas_call(
        functools.partial(pack_kernel, rows // 2, phase * part),
        in_specs=in_specs,
        out_specs=any_spec,
        out_shape=jax.ShapeDtypeStruct((chips, 2, length, PAIR), jnp.bfloat16),
        scratch_shapes=[
            pltpu.VMEM((4, rows, part), jnp.bfloat16),
            pltpu.VMEM((chips, 2, length, PAIR), jnp.bfloat16),
            pltpu.SemaphoreType.DMA((4, PARTS)),
            pltpu.SemaphoreType.DMA((2 * PARTS,)),
            *more,
        ],
        cost_estimate=pl.CostEstimate(
            flops=0, bytes_accessed=8 * rows * width, transcendentals=0
        ),
        compiler_params=pltpu.CompilerParams(vmem_limit_bytes=VMEM_LIMIT),
        name="pack_phase",
    )(*operands)
    return packed.reshape(2 * chips, length, PAIR)


def head_kernel(picks, table_ref, qg_ref, mine_ref, other_ref, out_ref, sum_ref, give_ref, *scratch):
    kv_scr, kt_scr, acc_ref, sems = scratch[:4]
    raws, pairs = scratch[4 : 4 + DEPTH], scratch[4 + DEPTH :]
    sources, tokens, _ = qg_ref.shape
    half = tokens // TILE
    lane = lax.broadcasted_iota(jnp.int32, (TILE, PAIR), 1)
    low = lane < HD
    parts = [slice(j * TILE, (j + 1) * TILE) for j in range(picks + 1)]
    final = sources * half - 1

    loads = [
        pltpu.make_async_copy(
            mine_ref.at[:, pl.ds(0, tokens)], kv_scr.at[pl.ds(0, sources)], sems.at[0]
        ),
        pltpu.make_async_copy(other_ref, kv_scr.at[pl.ds(sources, sources)], sems.at[1]),
    ]
    for load in loads:
        load.start()

    def clear(n, carry):
        rows = pl.ds(pl.multiple_of(n * tokens, tokens), tokens)
        acc_ref[rows, :] = jnp.zeros((tokens, PAIR), jnp.float32)
        return carry

    lax.fori_loop(0, 2 * sources, clear, 0)
    for load in loads:
        load.wait()

    def turn(n, carry):
        for j in range(half):
            kt_scr[n * half + j] = kv_scr[n, j * TILE : (j + 1) * TILE, :].T[:HD, :]
        return carry

    lax.fori_loop(0, 2 * sources, turn, 0)

    def tile_rows(n):
        return pl.ds(pl.multiple_of(n * TILE, TILE), TILE)

    def fold(x, op):
        return op(x.reshape(-1, 8, x.shape[-1]), axis=0)

    def load_block(index):
        block = jnp.minimum(index, final)
        named = [table_ref[block * picks + j] for j in range(picks)] + [block]
        rows = [tile_rows(n) for n in named]
        qg = qg_ref[block // half, tile_rows(block % half), :].astype(jnp.float32)
        zero = jnp.zeros_like(qg)
        both = jnp.concatenate(
            [jnp.where(low, qg * (HD**-0.5), zero), jnp.where(low, zero, qg)], axis=0
        )
        return named, rows, both

    def stage_raw(state, slot):
        named, _, both = state
        low_both = both.astype(jnp.bfloat16)
        top = None
        for j in range(picks + 1):
            n = named[j]
            raw = dot_nt(kv_scr[n // half, tile_rows(n % half), :], low_both)
            raws[slot][parts[j]] = raw
            part = fold(raw[:, :TILE], jnp.max)
            top = part if top is None else jnp.maximum(top, part)
            yield
        yield jnp.max(top, axis=0, keepdims=True)

    def stage_exp(top, slot):
        raw_scr, pair_scr = raws[slot], pairs[slot]
        total = jnp.zeros((8, TILE), jnp.float32)
        inner = jnp.zeros((8, TILE), jnp.float32)
        for j in range(picks + 1):
            p = jnp.exp2((raw_scr[parts[j], :TILE] - top) * LOG2E)
            raw_scr[parts[j], :TILE] = p
            pair_scr[parts[j], TILE:] = p.astype(jnp.bfloat16)
            total += fold(p, jnp.sum)
            inner += fold(p * raw_scr[parts[j], TILE:], jnp.sum)
            yield
        recip = 1.0 / jnp.sum(total, axis=0, keepdims=True)
        delta = jnp.sum(inner, axis=0, keepdims=True) * recip
        yield recip, delta

    def stage_grad(state, recip, delta, slot):
        named, rows, both = state
        raw_scr, pair_scr = raws[slot], pairs[slot]
        column = jnp.broadcast_to(recip, (TILE, TILE)).T
        scaled = jnp.concatenate([both[:TILE] * column, both[TILE:] * column], axis=0)
        scaled = scaled.astype(jnp.bfloat16)
        for j in range(picks + 1):
            ds = raw_scr[parts[j], :TILE] * (raw_scr[parts[j], TILE:] - delta)
            pair_scr[parts[j], :TILE] = ds.astype(jnp.bfloat16)
            acc_ref[rows[j], :] += dot_nn(pair_scr[parts[j]], scaled)
            yield
        turned = jnp.concatenate([kt_scr[n] for n in named], axis=1)
        dqt = dot_nn(turned, pair_scr[:, :TILE])
        yield dqt * (recip * (HD**-0.5))

    def together(*stages):
        results = [None] * len(stages)
        live = list(range(len(stages)))
        while live:
            for n in list(live):
                try:
                    value = next(stages[n])
                    if value is not None:
                        results[n] = value
                except StopIteration:
                    live.remove(n)
        return results

    (top0,) = together(stage_raw(load_block(0), 0))
    top1, stats0 = together(stage_raw(load_block(1), 1), stage_exp(top0, 0))

    def round_of_blocks(m, carry):
        top, recip, delta = carry
        held = None
        for n in range(DEPTH):
            index = m * DEPTH + n
            top, (next_recip, next_delta), dqt = together(
                stage_raw(load_block(index + 2), (n + 2) % DEPTH),
                stage_exp(top, (n + 1) % DEPTH),
                stage_grad(load_block(index), recip, delta, n),
            )
            recip, delta = next_recip, next_delta
            if n % 2 == 0:
                held = dqt
            else:
                both = jnp.concatenate([held, dqt], axis=0).T.astype(jnp.bfloat16)
                out_ref[index // half, tile_rows(index % half // 2), :] = both
        return top, recip, delta

    lax.fori_loop(0, sources * half // DEPTH, round_of_blocks, (top1, *stats0))

    store = pltpu.make_async_copy(acc_ref.at[pl.ds(0, sources * tokens)], sum_ref, sems.at[2])
    store.start()

    def finish(s, carry):
        rows = pl.ds(pl.multiple_of((sources + s) * tokens, tokens), tokens)
        give_ref[s] = acc_ref[rows, :].astype(jnp.bfloat16)
        return carry

    lax.fori_loop(0, sources, finish, 0)
    store.wait()


def attend_head(table, received, other):
    peers, tokens, _ = other.shape
    half = tokens // TILE
    total = 2 * peers * tokens
    picks = table.shape[0] // (peers * half)
    keys = TILE * (picks + 1)
    any_spec = pl.BlockSpec(memory_space=pl.ANY)
    scratch = [
        pltpu.VMEM((2 * peers, tokens, PAIR), jnp.bfloat16),
        pltpu.VMEM((2 * peers * half, HD, TILE), jnp.bfloat16),
        pltpu.VMEM((total, PAIR), jnp.float32),
        pltpu.SemaphoreType.DMA((3,)),
    ]
    scratch += [pltpu.VMEM((keys, 2 * TILE), jnp.float32)] * DEPTH
    scratch += [pltpu.VMEM((keys, 2 * TILE), jnp.bfloat16)] * DEPTH
    return pl.pallas_call(
        functools.partial(head_kernel, picks),
        grid_spec=pltpu.PrefetchScalarGridSpec(
            num_scalar_prefetch=1,
            grid=(1,),
            in_specs=[
                pl.BlockSpec((peers, tokens, PAIR), lambda i, t: (0, 1, 0)),
                any_spec,
                any_spec,
            ],
            out_specs=[
                pl.BlockSpec((peers, tokens // 2, PAIR), lambda i, t: (0, 2, 0)),
                any_spec,
                pl.BlockSpec((peers, tokens, PAIR), lambda i, t: (0, 0, 0)),
            ],
            scratch_shapes=scratch,
        ),
        out_shape=[
            jax.ShapeDtypeStruct((peers, 3 * tokens // 2, PAIR), jnp.bfloat16),
            jax.ShapeDtypeStruct((peers * tokens, PAIR), jnp.float32),
            jax.ShapeDtypeStruct((peers, tokens, PAIR), jnp.bfloat16),
        ],
        cost_estimate=pl.CostEstimate(
            flops=5 * 2 * TILE * PAIR * keys * peers * half,
            bytes_accessed=24 * 1024 * 1024,
            transcendentals=peers * half * keys * TILE,
        ),
        compiler_params=pltpu.CompilerParams(vmem_limit_bytes=VMEM_LIMIT),
        name="attend_head",
    )(table, received, received, other)


def merge_kernel(sum_ref, given_ref, before_ref, out_ref):
    out_ref[...] = (sum_ref[...] + given_ref[...].astype(jnp.float32)).astype(jnp.bfloat16)


def merge_sums(sums, given, payload):
    peers, tokens, _ = given.shape
    step = 4
    spec = pl.BlockSpec((step, tokens, PAIR), lambda i: (i, 0, 0))
    return pl.pallas_call(
        merge_kernel,
        grid=(peers // step,),
        in_specs=[spec, spec, pl.BlockSpec(memory_space=pl.ANY)],
        out_specs=spec,
        out_shape=jax.ShapeDtypeStruct(payload.shape, jnp.bfloat16),
        input_output_aliases={2: 0},
        cost_estimate=pl.CostEstimate(
            flops=0, bytes_accessed=8 * peers * tokens * PAIR, transcendentals=0
        ),
        compiler_params=pltpu.CompilerParams(vmem_limit_bytes=VMEM_LIMIT),
        name="merge_sums",
    )(sums.reshape(given.shape), given, payload)


def unpack_kernel(tokens, lanes, in_ref, *refs):
    gq_ref, gk_ref, gv_ref, in_scr, gq_scr, gk_scr, gv_scr, in_sems, out_sems = refs[-9:]
    slabs = gq_scr.shape[1] // PAIR
    loads = [
        pltpu.make_async_copy(
            in_ref.at[pl.ds(2 * j, 2)], in_scr.at[pl.ds(2 * j, 2)], in_sems.at[j]
        )
        for j in range(slabs)
    ]
    for load in loads:
        load.start()
    stores = []
    for j in range(slabs):
        loads[j].wait()
        cols = slice(j * PAIR, (j + 1) * PAIR)
        for core in range(2):
            rows = slice(core * tokens, (core + 1) * tokens)
            gk_scr[rows, cols], gv_scr[rows, cols] = merge_lanes(
                in_scr[2 * j, core, :tokens, :], in_scr[2 * j + 1, core, :tokens, :]
            )
            for m in range(tokens // TILE // 2):
                base = tokens + m * TILE
                even, odd = merge_lanes(
                    in_scr[2 * j, core, base : base + TILE, :],
                    in_scr[2 * j + 1, core, base : base + TILE, :],
                )
                base = core * tokens + 2 * m * TILE
                gq_scr[base : base + TILE, cols] = even
                gq_scr[base + TILE : base + 2 * TILE, cols] = odd
        for n, (scr, ref) in enumerate(((gq_scr, gq_ref), (gk_scr, gk_ref), (gv_scr, gv_ref))):
            copy = pltpu.make_async_copy(
                scr.at[:, pl.ds(j * PAIR, PAIR)],
                ref.at[:, pl.ds(lanes + j * PAIR, PAIR)],
                out_sems.at[n, j],
            )
            copy.start()
            stores.append(copy)
    for copy in stores:
        copy.wait()


def unpack_phase(back, previous, phase, rows, width):
    part = width // PHASES
    any_spec = pl.BlockSpec(memory_space=pl.ANY)
    operands = [back.reshape(back.shape[0] // 2, 2, *back.shape[1:])]
    aliases = {}
    if previous is not None:
        operands += list(previous)
        aliases = {1: 0, 2: 1, 3: 2}
    return pl.pallas_call(
        functools.partial(unpack_kernel, rows // 2, phase * part),
        in_specs=[any_spec] * len(operands),
        out_specs=[any_spec] * 3,
        out_shape=[jax.ShapeDtypeStruct((rows, width), jnp.bfloat16)] * 3,
        scratch_shapes=[pltpu.VMEM(operands[0].shape, jnp.bfloat16)]
        + [pltpu.VMEM((rows, part), jnp.bfloat16)] * 3
        + [
            pltpu.SemaphoreType.DMA((part // PAIR,)),
            pltpu.SemaphoreType.DMA((3, part // PAIR)),
        ],
        input_output_aliases=aliases,
        cost_estimate=pl.CostEstimate(
            flops=0, bytes_accessed=6 * rows * width, transcendentals=0
        ),
        compiler_params=pltpu.CompilerParams(vmem_limit_bytes=SMALL_LIMIT),
        name="unpack_phase",
    )(*operands)


def by_heads(queries, key_rows, value_rows, grad_out, tile_keys):
    rows, width = queries.shape
    blocks, picks = tile_keys.shape
    peers = lax.axis_size("ctx")
    half = blocks // 2
    tokens = half * TILE
    core = lax.axis_index("ctx") % 2

    def swap(x):
        return lax.ppermute(x, "ctx", [(i, i ^ 1) for i in range(peers)])

    received = [
        exchange(
            pack_phase(
                key_rows, value_rows, queries, grad_out, p, tile_keys if p == 0 else None
            )
        )
        for p in range(PHASES)
    ]
    table = received[0][:, 2 * tokens : 2 * tokens + blocks, :picks].astype(jnp.int32)
    table = jnp.where(core == 0, table[:, :half], table[:, half:])
    local = table % blocks
    side = (local // half + core) % 2
    table = (side * (peers * half) + table // blocks * half + local % half).reshape(-1)
    backs = []
    for p in range(PHASES):
        payload, sums, give = attend_head(table, received[p], swap(received[p][:, :tokens]))
        backs.append(exchange(merge_sums(sums, swap(give), payload)))
    result = None
    for p in range(PHASES):
        result = unpack_phase(backs[p], result, p, rows, width)
    return result


def by_blocks(queries, key_rows, value_rows, grad_out, tile_keys):
    rows, width = queries.shape
    blocks = rows // TILE
    peers = lax.axis_size("ctx")
    peer_range = jnp.arange(peers, dtype=jnp.int32)
    owners = tile_keys // blocks
    local_ids = tile_keys % blocks
    matches = owners[:, :, None] == peer_range[None, None, :]
    wanted = jnp.max(jnp.where(matches, local_ids[:, :, None], -1), axis=(0, 1))
    requested = exchange(wanted)
    slots = owners.reshape(-1)
    chunk_width = width // CHUNKS

    received = [
        exchange(gather_blocks(requested, key_rows, value_rows, c, chunk_width)) for c in range(CHUNKS)
    ]
    grad_queries = None
    owns, backs = [], []
    for c in range(CHUNKS):
        grad_queries, own, out = attend(
            slots, queries, grad_out, key_rows, value_rows, received[c], grad_queries, c
        )
        owns.append(own)
        backs.append(exchange(out))
    result = None
    for c in range(CHUNKS):
        result = combine(requested, owns[c], backs[c], result, c, width)
    return grad_queries, result[0], result[1]


def on_device(queries, key_rows, value_rows, grad_out, tile_keys):
    peers = lax.axis_size("ctx")
    blocks = tile_keys.shape[0]
    one_head_each = peers * HD == queries.shape[1]
    even = peers % 4 == 0 and blocks % 4 == 0 and blocks <= EXTRA
    fits = one_head_each and even and peers * blocks <= 256
    plan = by_heads if fits else by_blocks
    return tuple(plan(queries, key_rows, value_rows, grad_out, tile_keys))


def solution(mesh):
    spec = P(("groups", "ctx"), None)
    return jax.shard_map(
        on_device, mesh=mesh, in_specs=(spec,) * 5, out_specs=(spec,) * 3, check_vma=False
    )
```
